256 devices in a mesh: dp: 16 (over z_lo, y), expert: 16 (over x, z_hi, core).
Axes of the slice: x: 4, y: 4, z: 8 (z_hi: 2, z_lo: 4; z = z_hi * 4 + z_lo), core: 2. Of those that a mesh axis runs over, the one named last changes fastest.
Arguments:
- tokens: bfloat16 [128, 256, 1280], P('dp'), may hold values from -288 to 288
- out_grad: bfloat16 [128, 256, 1280], P('dp'), may hold values from -6 to 6
- slot_params: bfloat16 [1280, 128], P(None, 'expert'), may hold values from -0.75 to 0.75
- w_in: bfloat16 [1280, 81920], P('dp', 'expert'), may hold values from -0.15625 to 0.15625
- w_out: bfloat16 [81920, 1280], P('expert', 'dp'), may hold values from -0.078125 to 0.078125
Outputs:
- token_grad: bfloat16 [128, 256, 1280], P('dp', 'expert')
- slot_grad: float32 [1280, 128], P(None, 'expert')
The draws below stay inside these ranges and needn't reach their ends.
All inputs are finite; a program needn't handle non-finite values.
Results may differ from the reference program's by a relative error of at most 0.02.
Values may be sent and summed in bfloat16 or wider, within the bound.
No kernel may reach another device: no remote copies, remote signals or barrier semaphores. Data moves between devices by JAX's collectives and lax.ppermute only.
A program may use at most 128 MiB of HBM per device.

```python
import math
import jax
import jax.numpy as jnp
from jax import lax

D = 1280
FF = 5120
S = 8
M = 256
IMAGES = 128
EXPERTS = 16
SLOTS = 128


def slot_table(key):
    return jax.random.truncated_normal(key, -4.0, 4.0, (D, SLOTS), jnp.float32) / math.sqrt(D)


def draw_slot_params(key, part):
    return slot_table(key).astype(jnp.bfloat16)


def draw_tokens(key, part):
    key = jax.random.fold_in(key, 3)
    base = jax.random.truncated_normal(key, -4.0, 4.0, (IMAGES, M, D), jnp.float32)
    return base.astype(jnp.bfloat16)


def block_levels(own_key, shape, cuts, smallest, high):
    def one(position, blocks):
        steps = jax.random.uniform(jax.random.fold_in(jax.random.fold_in(own_key, 6), position), (blocks,), jnp.float32, smallest / len(cuts), high / len(cuts))
        return jnp.repeat(jnp.exp(steps), shape[position] // blocks).reshape((-1,) + (1,) * (len(shape) - position - 1))

    factor_of = one(*cuts[0])
    for cut in cuts[1:]:
        factor_of = factor_of * one(*cut)
    return factor_of


def bell_draw(rng, shape, spread, most, cuts=(), kind=jnp.bfloat16):
    entries = jax.random.normal(rng, shape, jnp.float32) * spread
    if len(cuts) > 0:
        entries = block_levels(rng, shape, cuts, -0.22, 0.18) * entries
    return jnp.clip(entries, min=-most, max=most).astype(kind)


def setup_inputs(seed: int = 0) -> dict:
    key_list = jax.random.split(jax.random.key(seed), 6)
    tokens = draw_tokens(jax.random.fold_in(key_list[5], 71), 0)
    out_grad = bell_draw(key_list[1], (IMAGES, M, D), 1.0, 6.0, ((0, 16),))
    slot_params = draw_slot_params(jax.random.fold_in(key_list[5], 71), 0)
    w_in = bell_draw(key_list[3], (D, EXPERTS * FF), D ** -0.5, 0.15625, ((0, 16), (1, 16)))
    w_out = bell_draw(key_list[4], (EXPERTS * FF, D), FF ** -0.5, 0.078125, ((0, 16), (1, 16)))
    return dict(tokens=tokens, out_grad=out_grad, slot_params=slot_params, w_in=w_in, w_out=w_out)


def softmaxes(image_tokens, slot_params):
    logits = jnp.dot(image_tokens, slot_params, preferred_element_type=jnp.float32)
    return (jax.nn.softmax(logits, axis=0), jax.nn.softmax(logits, axis=1))

def slot_inputs(tokens, out_grad, slot_params):

    def image_step(totals, inputs):
        dispatch, combine = softmaxes(inputs[0], slot_params)
        slot_in = jnp.dot(dispatch.astype(jnp.bfloat16).T, inputs[0], preferred_element_type=jnp.float32).astype(jnp.bfloat16)
        slot_go = jnp.dot(combine.astype(jnp.bfloat16).T, inputs[1], preferred_element_type=jnp.float32).astype(jnp.bfloat16)
        return (totals, (slot_in, slot_go))
    return lax.scan(image_step, jnp.zeros((), jnp.float32), (tokens, out_grad))[1]

def expert_pass(operands):
    rows_in, rows_go, first_proj, second_proj = operands
    pre_act = jnp.dot(rows_in, first_proj, preferred_element_type=jnp.float32)
    hidden = jax.nn.gelu(pre_act).astype(jnp.bfloat16)
    slot_out = jnp.dot(hidden, second_proj, preferred_element_type=jnp.float32)
    hidden_grad = jnp.dot(rows_go, second_proj.T, preferred_element_type=jnp.float32)
    pre_grad = jax.vjp(jax.nn.gelu, pre_act)[1](hidden_grad)[0].astype(jnp.bfloat16)
    slot_in_grad = jnp.dot(pre_grad, first_proj.T, preferred_element_type=jnp.float32)
    return (slot_out, slot_in_grad)

def by_expert(slot_rows):
    return slot_rows.reshape(IMAGES, EXPERTS, S, D).transpose(1, 0, 2, 3).reshape(EXPERTS, IMAGES * S, D)

def by_image(expert_rows):
    return expert_rows.reshape(EXPERTS, IMAGES, S, D).transpose(1, 0, 2, 3).reshape(IMAGES, SLOTS, D)

def image_grads(image_tokens, image_grad, slot_out, slot_in_grad, slot_params):
    highest = lax.Precision.HIGHEST
    dispatch, combine = softmaxes(image_tokens, slot_params)
    dispatch_b = dispatch.astype(jnp.bfloat16)
    combine_grad = jnp.dot(image_grad.astype(jnp.float32), slot_out.T, precision=highest)
    dispatch_grad = jnp.dot(image_tokens.astype(jnp.float32), slot_in_grad.T, precision=highest)
    logit_grad = dispatch * (dispatch_grad - lax.optimization_barrier(jnp.sum(dispatch * dispatch_grad, axis=0, keepdims=True)))
    logit_grad = logit_grad + combine * (combine_grad - lax.optimization_barrier(jnp.sum(combine * combine_grad, axis=1, keepdims=True)))
    logit_grad_b = logit_grad.astype(jnp.bfloat16)
    through_slots = jnp.dot(dispatch_b.astype(jnp.float32), slot_in_grad, precision=highest)
    through_logits = jnp.dot(logit_grad_b, slot_params.T, preferred_element_type=jnp.float32)
    token_grad = (through_slots + through_logits).astype(jnp.bfloat16)
    slot_term = jnp.dot(image_tokens.T, logit_grad_b, preferred_element_type=jnp.float32)
    return (token_grad, slot_term)

def reference(tokens, out_grad, slot_params, w_in, w_out):
    slot_in, slot_go = slot_inputs(tokens, out_grad, slot_params)
    firsts = w_in.reshape(D, EXPERTS, FF).transpose(1, 0, 2)
    seconds = w_out.reshape(EXPERTS, FF, D)
    expert_out, expert_in_grad = lax.map(expert_pass, (by_expert(slot_in), by_expert(slot_go), firsts, seconds))
    slot_out = by_image(expert_out)
    slot_in_grad = by_image(expert_in_grad)

    def image_step(total, inputs):
        token_grad, slot_term = image_grads(inputs[0], inputs[1], inputs[2], inputs[3], slot_params)
        return (total + slot_term, token_grad)
    start = jnp.zeros((D, SLOTS), jnp.float32)
    slot_grad, token_grad = lax.scan(image_step, start, (tokens, out_grad, slot_out, slot_in_grad))
    return (token_grad, slot_grad)
```

```python
import math
import jax
import jax.numpy as jnp
from jax import lax
from jax.experimental import pallas as pl
from jax.experimental.pallas import tpu as pltpu
from jax.sharding import PartitionSpec as P

F32 = jnp.float32
BF16 = jnp.bfloat16
ROOT = math.sqrt(2.0 / math.pi)


def swap(value, axis, k):
    count = lax.axis_size(axis)
    return lax.ppermute(value, axis, [(i, i ^ k) for i in range(count)])


def nt(a, b):
    return lax.dot_general(a, b, (((1,), (1,)), ((), ())), preferred_element_type=F32)


def ffn_kernel(rows_in, rows_go, *refs):
    blocks = refs[:20]
    out_own, out_far, grad_own, grad_far = refs[20:24]
    w1, w2, hid, pgr, sems = refs[24:]
    me = lax.axis_index("dp")
    depth = w1.shape[0] // 16

    def place(index):
        return pl.ds(pl.multiple_of((me ^ index) * depth, 16), depth)

    copies = []
    for which, dst in ((0, w1), (1, w2)):
        for a in range(4):
            own, left, right, far1, far2 = blocks[5 * a : 5 * a + 5]
            for b, src in ((0, own.at[which]), (1, left.at[which]), (3, right.at[which]), (2, (far1, far2)[which])):
                copy = pltpu.make_async_copy(src, dst.at[place(4 * a + b)], sems.at[which * 16 + 4 * a + b])
                copy.start()
                copies.append(copy)
    for copy in copies:
        copy.wait()

    width = w1.shape[1]
    tile = 256

    @pl.loop(0, width // tile)
    def _(t):
        cols = pl.ds(pl.multiple_of(t * tile, tile), tile)
        pre = jnp.dot(rows_in[...], w1[:, cols], preferred_element_type=F32)
        hg = jnp.dot(rows_go[...], w2[:, cols], preferred_element_type=F32)
        sq = pre * pre
        th = jnp.tanh(ROOT * (pre + 0.044715 * (sq * pre)))
        cdf = 0.5 * (1.0 + th)
        hid[:, cols] = (pre * cdf).astype(BF16)
        slope = cdf + 0.5 * pre * (1.0 - th * th) * (ROOT * (1.0 + 3 * 0.044715 * sq))
        pgr[:, cols] = (hg * slope).astype(BF16)

    own_rows = out_own.shape[0]

    @pl.loop(0, w1.shape[0] // tile)
    def _(t):
        cols = pl.ds(pl.multiple_of(t * tile, tile), tile)
        grad = nt(pgr[...], w1[cols, :])
        grad_own[:, cols] = grad[:own_rows]
        grad_far[:, cols] = grad[own_rows:].astype(BF16)
        out = nt(hid[...], w2[cols, :])
        out_own[:, cols] = out[:own_rows]
        out_far[:, cols] = out[own_rows:].astype(BF16)


def ffn(rows_in, rows_go, blocks, own_rows):
    rows, width = rows_in.shape
    quarter = blocks[0].shape[2]
    any_spec = pl.BlockSpec(memory_space=pl.ANY)
    vmem = pl.BlockSpec(memory_space=pltpu.VMEM)
    return pl.pallas_call(
        ffn_kernel,
        out_shape=[
            jax.ShapeDtypeStruct((own_rows, width), F32),
            jax.ShapeDtypeStruct((rows - own_rows, width), BF16),
        ]
        * 2,
        in_specs=[vmem, vmem] + [any_spec] * 20,
        out_specs=[vmem] * 4,
        scratch_shapes=[
            pltpu.VMEM((width, quarter), BF16),
            pltpu.VMEM((width, quarter), BF16),
            pltpu.VMEM((rows, quarter), BF16),
            pltpu.VMEM((rows, quarter), BF16),
            pltpu.SemaphoreType.DMA((32,)),
        ],
        compiler_params=pltpu.CompilerParams(vmem_limit_bytes=32 * 2**20),
        cost_estimate=pl.CostEstimate(
            flops=8 * rows * width * quarter, bytes_accessed=4 * width * quarter, transcendentals=rows * quarter
        ),
        name="ffn",
    )(rows_in, rows_go, *blocks)


def spread_weights(w_in, w_out):
    me = lax.axis_index("dp")
    z = me // 4
    quarter = w_in.shape[1] // 4

    def unit(zz):
        start = zz * quarter
        return jnp.stack(
            [
                lax.dynamic_slice_in_dim(w_in, start, quarter, 1),
                lax.dynamic_slice_in_dim(w_out, start, quarter, 1),
            ]
        )

    blocks = []
    for a in range(4):
        own = unit(z ^ a)
        if a:
            own = swap(own, "dp", 4 * a)
        left = swap(own, "dp", 1)
        right = swap(own, "dp", 3)
        far1 = swap(right[0], "dp", 1)
        far2 = swap(left[1], "dp", 3)
        blocks += [own, left, right, far1, far2]
    return blocks


def gather_z(rows):
    one = swap(rows, "dp", 4)
    two = swap(rows, "dp", 8)
    three = swap(two, "dp", 4)
    return jnp.concatenate([rows, one, two, three], axis=0)


def reduce_z(own, far):
    count = own.shape[0]
    total = own
    for a in (1, 2, 3):
        total = total + swap(far[(a - 1) * count : a * count], "dp", 4 * a).astype(F32)
    return total


def gather_expert_small(v):
    v = jnp.concatenate([v, swap(v, "expert", 1)], axis=0)
    v = jnp.concatenate([v, swap(v, "expert", 2)], axis=0)
    return jnp.concatenate([v, swap(v, "expert", 4), swap(v, "expert", 8), swap(v, "expert", 12)], axis=0)


def sum_expert(v):
    v = v + swap(v, "expert", 1)
    v = v + swap(v, "expert", 2)
    return (v + swap(v, "expert", 4)) + (swap(v, "expert", 8) + swap(v, "expert", 12))


def gather_expert(rows):
    far = swap(rows, "expert", 2)
    pair = jnp.stack([rows, far])
    one = swap(pair, "expert", 4)
    three = swap(pair, "expert", 12)
    two_a = swap(three[0], "expert", 4)
    two_b = swap(one[1], "expert", 12)
    pieces = [rows, far, one[0], one[1], two_a, two_b, three[0], three[1]]
    mine = jnp.stack(pieces)
    other = swap(mine, "expert", 1)
    return jnp.stack([mine, other], axis=1).reshape((16,) + rows.shape)


def per_device(tokens, out_grad, slot_params, w_in, w_out):
    highest = lax.Precision.HIGHEST
    images, count, width = tokens.shape
    own = slot_params.shape[1]
    column = lax.axis_index("expert")
    params = slot_params.T
    blocks = spread_weights(w_in, w_out.T)
    table = gather_expert_small(params)

    own_logits = jnp.einsum("sd,bmd->bsm", params, tokens, preferred_element_type=F32)
    dispatch = jax.nn.softmax(own_logits, axis=2)
    dispatch_b = dispatch.astype(BF16)
    slot_in = jnp.einsum("bsm,bmd->bsd", dispatch_b, tokens, preferred_element_type=F32).astype(BF16)
    rows_in = gather_z(slot_in.reshape(images * own, width))

    logits = jnp.einsum("nd,bmd->bnm", table, tokens, preferred_element_type=F32)
    top = jnp.max(logits, axis=1, keepdims=True)
    total = jnp.sum(jnp.exp(logits - top), axis=1, keepdims=True)
    combine = jnp.exp(own_logits - top) / total
    combine_b = combine.astype(BF16)
    slot_go = jnp.einsum("bsm,bmd->bsd", combine_b, out_grad, preferred_element_type=F32).astype(BF16)
    rows_go = gather_z(slot_go.reshape(images * own, width))

    own_rows = count // 16
    full_dispatch = jax.nn.softmax(logits, axis=2).astype(BF16)
    row_dispatch = lax.dynamic_slice_in_dim(full_dispatch, column * own_rows, own_rows, 2)

    out_own, out_far, grad_own, grad_far = ffn(rows_in, rows_go, blocks, images * own)
    slot_in_grad = reduce_z(grad_own, grad_far)
    slot_out = reduce_z(out_own, out_far)
    grads = gather_expert(slot_in_grad.astype(BF16))

    slot_out = slot_out.reshape(images, own, width)
    slot_in_grad = slot_in_grad.reshape(images, own, width)
    combine_grad = jnp.einsum("bsd,bmd->bsm", slot_out, out_grad.astype(F32), precision=highest)
    combine_mix = sum_expert(jnp.sum(combine * combine_grad, axis=1))
    dispatch_grad = jnp.einsum("bsd,bmd->bsm", slot_in_grad, tokens.astype(F32), precision=highest)
    logit_grad = dispatch * (dispatch_grad - jnp.sum(dispatch * dispatch_grad, axis=2, keepdims=True))
    logit_grad = logit_grad + combine * (combine_grad - combine_mix[:, None, :])
    logit_grad_b = logit_grad.astype(BF16)
    slot_term = jnp.einsum("bsm,bmd->sd", logit_grad_b, tokens, preferred_element_type=F32)

    send = logit_grad_b.reshape(images, own, 16, own_rows).transpose(2, 0, 1, 3)
    got = lax.all_to_all(send.reshape(16, images, own * own_rows), "expert", 0, 0, tiled=False)
    got = got.reshape(16, images, own, own_rows)
    row_grads = jnp.take(got, column ^ jnp.arange(16), axis=0)

    term = slot_term.astype(BF16)
    for step in ((4, 8, 12), (1, 2, 3)):
        acc = term.astype(F32)
        for k in step:
            acc = acc + swap(term, "dp", k).astype(F32)
        term = acc.astype(BF16)
    slot_grad = acc.T

    grads = grads.reshape(16, images, own, width)
    token_grad = jnp.einsum("bnm,nbd->bmd", row_dispatch, grads.transpose(0, 2, 1, 3).reshape(16 * own, images, width),
                            preferred_element_type=F32)
    through = jnp.einsum("rbsm,rsd->bmd", row_grads, table.reshape(16, own, width), preferred_element_type=F32)
    return ((token_grad + through).astype(BF16), slot_grad)


def solution(mesh):
    return jax.shard_map(
        per_device,
        mesh=mesh,
        in_specs=(
            P("dp", None, None),
            P("dp", None, None),
            P(None, "expert"),
            P("dp", "expert"),
            P("expert", "dp"),
        ),
        out_specs=(P("dp", "expert", None), P(None, "expert")),
        check_vma=False,
    )
```

```python
import math
import jax
import jax.numpy as jnp
from jax import lax
from jax.experimental import pallas as pl
from jax.experimental.pallas import tpu as pltpu
from jax.sharding import PartitionSpec as P

F32 = jnp.float32
BF16 = jnp.bfloat16
ROOT = math.sqrt(2.0 / math.pi)


def swap(value, axis, k):
    count = lax.axis_size(axis)
    return lax.ppermute(value, axis, [(i, i ^ k) for i in range(count)])


def nt(a, b):
    return lax.dot_general(a, b, (((1,), (1,)), ((), ())), preferred_element_type=F32)


def ffn_kernel(rows_in, rows_go, *refs):
    blocks = refs[:20]
    out_own, out_far, grad_own, grad_far = refs[20:24]
    w1, w2, hid, pgr, slope, sems = refs[24:]
    me = lax.axis_index("dp")
    depth = w1.shape[0] // 16

    def place(index):
        return pl.ds(pl.multiple_of((me ^ index) * depth, 16), depth)

    copies = ([], [])
    for which, dst in ((0, w1), (1, w2)):
        for a in range(4):
            own, left, right, far1, far2 = blocks[5 * a : 5 * a + 5]
            for b, src in ((0, own.at[which]), (1, left.at[which]), (3, right.at[which]), (2, (far1, far2)[which])):
                copy = pltpu.make_async_copy(src, dst.at[place(4 * a + b)], sems.at[which * 16 + 4 * a + b])
                copy.start()
                copies[which].append(copy)
    for copy in copies[0]:
        copy.wait()

    width = w1.shape[1]
    tile = 256

    @pl.loop(0, width // tile)
    def _(t):
        cols = pl.ds(pl.multiple_of(t * tile, tile), tile)
        pre = jnp.dot(rows_in[...], w1[:, cols], preferred_element_type=F32)
        sq = pre * pre
        th = jnp.tanh(ROOT * (pre + 0.044715 * (sq * pre)))
        cdf = 0.5 * (1.0 + th)
        hid[:, cols] = (pre * cdf).astype(BF16)
        slope[:, cols] = cdf + 0.5 * pre * (1.0 - th * th) * (ROOT * (1.0 + 3 * 0.044715 * sq))

    for copy in copies[1]:
        copy.wait()

    @pl.loop(0, width // tile)
    def _(t):
        cols = pl.ds(pl.multiple_of(t * tile, tile), tile)
        hg = jnp.dot(rows_go[...], w2[:, cols], preferred_element_type=F32)
        pgr[:, cols] = (hg * slope[:, cols]).astype(BF16)

    own_rows = out_own.shape[0]

    @pl.loop(0, w1.shape[0] // tile)
    def _(t):
        cols = pl.ds(pl.multiple_of(t * tile, tile), tile)
        grad = nt(pgr[...], w1[cols, :])
        grad_own[:, cols] = grad[:own_rows]
        grad_far[:, cols] = grad[own_rows:].astype(BF16)
        out = nt(hid[...], w2[cols, :])
        out_own[:, cols] = out[:own_rows]
        out_far[:, cols] = out[own_rows:].astype(BF16)


def ffn(rows_in, rows_go, blocks, own_rows):
    rows, width = rows_in.shape
    quarter = blocks[0].shape[2]
    any_spec = pl.BlockSpec(memory_space=pl.ANY)
    vmem = pl.BlockSpec(memory_space=pltpu.VMEM)
    return pl.pallas_call(
        ffn_kernel,
        out_shape=[
            jax.ShapeDtypeStruct((own_rows, width), F32),
            jax.ShapeDtypeStruct((rows - own_rows, width), BF16),
        ]
        * 2,
        in_specs=[vmem, vmem] + [any_spec] * 20,
        out_specs=[vmem] * 4,
        scratch_shapes=[
            pltpu.VMEM((width, quarter), BF16),
            pltpu.VMEM((width, quarter), BF16),
            pltpu.VMEM((rows, quarter), BF16),
            pltpu.VMEM((rows, quarter), BF16),
            pltpu.VMEM((rows, quarter), F32),
            pltpu.SemaphoreType.DMA((32,)),
        ],
        compiler_params=pltpu.CompilerParams(vmem_limit_bytes=32 * 2**20),
        cost_estimate=pl.CostEstimate(
            flops=8 * rows * width * quarter, bytes_accessed=4 * width * quarter, transcendentals=rows * quarter
        ),
        name="ffn",
    )(rows_in, rows_go, *blocks)


def pick_rows(rows, count):
    start = lax.axis_index("expert") * rows
    col = lax.broadcasted_iota(jnp.int32, (rows, count), 1)
    row = lax.broadcasted_iota(jnp.int32, (rows, count), 0)
    return (col == row + start).astype(BF16)


def slots_kernel(table, tokens, out_grad, rows, dispatch_own, combine_own, spread):
    step = pl.program_id(0)
    own = 8
    slots = table.shape[0]
    count = tokens.shape[1]
    pick = pick_rows(16, count)
    ins, gos, disp, comb, spr = [], [], [], [], []
    for i in range(2):
        logits = nt(table[...], tokens[i])
        up = jnp.exp(logits - jnp.max(logits, axis=1, keepdims=True))
        dispatch = up / jnp.sum(up, axis=1, keepdims=True)
        down = jnp.exp(logits - jnp.max(logits, axis=0, keepdims=True))
        combine = down[:own] / jnp.sum(down, axis=0, keepdims=True)
        dispatch_b = dispatch.astype(BF16)
        ins.append(jnp.dot(dispatch_b[:16], tokens[i], preferred_element_type=F32)[:own])
        both = jnp.concatenate([combine, combine], axis=0).astype(BF16)
        gos.append(jnp.dot(both, out_grad[i], preferred_element_type=F32)[:own])
        disp.append(dispatch[:own])
        comb.append(combine)
        mine = nt(pick, dispatch_b).astype(BF16)
        image = 2 * step + i
        q = lax.broadcasted_iota(jnp.int32, (slots, 8 * slots), 0)
        col = lax.broadcasted_iota(jnp.int32, (slots, 8 * slots), 1)
        wide = (col == (q // 8) * 64 + q % 8 + image * 8).astype(BF16)
        spr.append(jnp.dot(mine, wide, preferred_element_type=F32))
    rows[0] = jnp.concatenate(ins, axis=0).astype(BF16)
    rows[1] = jnp.concatenate(gos, axis=0).astype(BF16)
    dispatch_own[...] = jnp.concatenate(disp, axis=0)
    combine_own[...] = jnp.concatenate(comb, axis=0)
    spread[...] = jnp.concatenate(spr, axis=0).astype(BF16)


def slots_call(table, tokens, out_grad):
    images, count, width = tokens.shape
    slots = table.shape[0]
    return pl.pallas_call(
        slots_kernel,
        grid=(images // 2,),
        out_shape=[
            jax.ShapeDtypeStruct((2, images * 8, width), BF16),
            jax.ShapeDtypeStruct((images * 8, count), F32),
            jax.ShapeDtypeStruct((images * 8, count), F32),
            jax.ShapeDtypeStruct((images * 16, slots * 8), BF16),
        ],
        in_specs=[
            pl.BlockSpec((slots, width), lambda i: (0, 0)),
            pl.BlockSpec((2, count, width), lambda i: (i, 0, 0)),
            pl.BlockSpec((2, count, width), lambda i: (i, 0, 0)),
        ],
        out_specs=[
            pl.BlockSpec((2, 16, width), lambda i: (0, i, 0)),
            pl.BlockSpec((16, count), lambda i: (i, 0)),
            pl.BlockSpec((16, count), lambda i: (i, 0)),
            pl.BlockSpec((32, slots * 8), lambda i: (i, 0)),
        ],
        compiler_params=pltpu.CompilerParams(vmem_limit_bytes=24 * 2**20),
        name="slots",
    )(table, tokens, out_grad)


def against_kernel(over_tokens, rows, big, weight, *outs):
    value = rows[...]
    high = value.astype(BF16)
    low = (value - high.astype(F32)).astype(BF16)
    both = jnp.concatenate([high, low], axis=0)
    prods = []
    for i in range(2):
        prod = nt(both, big[i])
        prods.append(prod[8 * i : 8 * i + 8] + prod[16 + 8 * i : 24 + 8 * i])
    prod = jnp.concatenate(prods, axis=0)
    w = weight[...]
    part = w * prod
    if over_tokens:
        outs[0][...] = w * (prod - jnp.sum(part, axis=1, keepdims=True))
    else:
        outs[0][...] = part
        step = pl.program_id(0)
        for i in range(2):
            outs[1][pl.ds(2 * step + i, 1), :] = jnp.sum(part[8 * i : 8 * i + 8], axis=0, keepdims=True)


def against(rows, big, weight, over_tokens):
    images, count, width = big.shape
    total = images * 8
    out_shape = [jax.ShapeDtypeStruct((total, count), F32)]
    out_specs = [pl.BlockSpec((16, count), lambda i: (i, 0))]
    if not over_tokens:
        out_shape.append(jax.ShapeDtypeStruct((images, count), F32))
        out_specs.append(pl.BlockSpec((images, count), lambda i: (0, 0)))
    return pl.pallas_call(
        lambda *refs: against_kernel(over_tokens, *refs),
        grid=(images // 2,),
        out_shape=out_shape,
        in_specs=[
            pl.BlockSpec((16, width), lambda i: (i, 0)),
            pl.BlockSpec((2, count, width), lambda i: (i, 0, 0)),
            pl.BlockSpec((16, count), lambda i: (i, 0)),
        ],
        out_specs=out_specs,
        compiler_params=pltpu.CompilerParams(vmem_limit_bytes=16 * 2**20),
        name="dispatch_grad" if over_tokens else "combine_grad",
    )(rows, big, weight)


def lines_kernel(grads, out):
    total, count = grads.shape
    x = nt(pick_rows(16, count), grads[...])
    x = jnp.concatenate([x] * 8, axis=0)
    row = lax.broadcasted_iota(jnp.int32, x.shape, 0)
    col = lax.broadcasted_iota(jnp.int32, x.shape, 1)
    x = jnp.where((col // 8) % 8 == row // 16, x, 0.0).astype(BF16)
    c = lax.broadcasted_iota(jnp.int32, (total, total // 8), 0)
    q = lax.broadcasted_iota(jnp.int32, (total, total // 8), 1)
    fold = ((c // 64 == q // 8) & (c % 8 == q % 8)).astype(BF16)
    out[...] = jnp.dot(x, fold, preferred_element_type=F32).astype(BF16)


def lines(grads):
    total = grads.shape[0]
    vmem = pl.BlockSpec(memory_space=pltpu.VMEM)
    return pl.pallas_call(
        lines_kernel,
        out_shape=jax.ShapeDtypeStruct((total // 8, total // 8), BF16),
        in_specs=[vmem],
        out_specs=vmem,
        compiler_params=pltpu.CompilerParams(vmem_limit_bytes=16 * 2**20),
        name="lines",
    )(grads)


def tokens_kernel(spread, rows, table, pair, one, three, two_a, two_b, pair_s, one_s, three_s, two_as, two_bs, out, held, sems):
    pieces = [
        (pair, pair_s),
        (one, one_s),
        ((two_a, two_b), (two_as, two_bs)),
        (three, three_s),
    ]
    copies = []
    size = two_a.shape[0]
    for x, sides in enumerate(pieces):
        for c, side in enumerate(sides):
            for h in range(2):
                src = side[h] if isinstance(side, tuple) else side.at[h]
                r = 4 * x + 2 * h + c
                copy = pltpu.make_async_copy(src, held.at[pl.ds(r * size, size)], sems.at[r])
                copy.start()
                copies.append(copy)
    base = jnp.dot(rows[...], table[...], preferred_element_type=F32)
    for copy in copies:
        copy.wait()
    total = base + jnp.dot(spread[...], held[...], preferred_element_type=F32)
    out[...] = total.astype(BF16)


def tokens_call(spread, rows, table, pieces):
    width = table.shape[1]
    vmem = pl.BlockSpec(memory_space=pltpu.VMEM)
    any_spec = pl.BlockSpec(memory_space=pl.ANY)
    return pl.pallas_call(
        tokens_kernel,
        out_shape=jax.ShapeDtypeStruct((spread.shape[0], width), BF16),
        in_specs=[vmem] * 3 + [any_spec] * 10,
        out_specs=vmem,
        scratch_shapes=[pltpu.VMEM((spread.shape[1], width), BF16), pltpu.SemaphoreType.DMA((16,))],
        compiler_params=pltpu.CompilerParams(vmem_limit_bytes=24 * 2**20),
        name="token_grad",
    )(spread, rows, table, *pieces)


def after(value, *earlier):
    return lax.optimization_barrier((value,) + earlier)[0]


def units_of(w_in, w_out):
    z = lax.axis_index("dp") // 4
    quarter = w_in.shape[1] // 4

    def unit(zz):
        start = zz * quarter
        return jnp.stack(
            [
                lax.dynamic_slice_in_dim(w_in, start, quarter, 1),
                lax.dynamic_slice_in_dim(w_out, start, quarter, 1),
            ]
        )

    return [unit(z ^ a) for a in range(4)]


def ring_y(unit):
    return swap(unit, "dp", 1), swap(unit, "dp", 3)


def far_y(left, right):
    return swap(right[0], "dp", 1), swap(left[1], "dp", 3)


def reduce_z(own, far):
    count = own.shape[0]
    total = own
    for a in (1, 2, 3):
        total = total + swap(far[(a - 1) * count : a * count], "dp", 4 * a).astype(F32)
    return total


def gather_x(v):
    return jnp.concatenate([v, swap(v, "expert", 4), swap(v, "expert", 8), swap(v, "expert", 12)], axis=0)


def sum_expert(v):
    v = (v + swap(v, "expert", 1)) + (swap(v, "expert", 2) + swap(v, "expert", 3))
    return (v + swap(v, "expert", 4)) + (swap(v, "expert", 8) + swap(v, "expert", 12))


def gather_expert(rows, far):
    pair = jnp.stack([rows, far])
    one = swap(pair, "expert", 4)
    three = swap(pair, "expert", 12)
    two_a = swap(three[0], "expert", 4)
    two_b = swap(one[1], "expert", 12)
    near = [pair, one, three, two_a, two_b]
    return near + [swap(v, "expert", 1) for v in near]


def per_device(tokens, out_grad, slot_params, w_in, w_out):
    images, count, width = tokens.shape
    own = slot_params.shape[1]
    params = slot_params.T

    units = units_of(w_in, w_out.T)
    l0, r0 = ring_y(units[0])
    u1 = swap(units[1], "dp", 4)
    u2 = swap(units[2], "dp", 8)
    table = jnp.concatenate([params, swap(params, "expert", 1)], axis=0)
    l0, r0, u1, u2, table = lax.optimization_barrier((l0, r0, u1, u2, table))
    u3 = swap(after(units[3], u1), "dp", 12)
    l1, r1 = ring_y(u1)
    p0, q0 = far_y(l0, r0)
    table = jnp.concatenate([table, swap(table, "expert", 2)], axis=0)
    table = gather_x(table)
    l1, r1, table = lax.optimization_barrier((l1, r1, table))
    l2, r2 = ring_y(after(u2, l1, r1))
    l1, r1, u3, p0, q0 = lax.optimization_barrier((l1, r1, u3, p0, q0))
    p1, q1 = far_y(l1, r1)

    rows, dispatch, combine, spread = slots_call(table, tokens, out_grad)
    rows = after(rows.reshape(2 * images * own, width), u3)
    z1, z2 = swap(rows, "dp", 4), swap(rows, "dp", 8)
    z3 = swap(z2, "dp", 4)
    l3, r3 = ring_y(after(u3, l2, r2, p1, q1))
    p2, q2 = far_y(l2, r2)
    l3, r3, p2, q2 = lax.optimization_barrier((l3, r3, p2, q2))
    p3, q3 = far_y(l3, r3)
    blocks = [units[0], l0, r0, p0, q0, u1, l1, r1, p1, q1, u2, l2, r2, p2, q2, u3, l3, r3, p3, q3]
    half = images * own
    rows_in = jnp.concatenate([v[:half] for v in (rows, z1, z2, z3)], axis=0)
    rows_go = jnp.concatenate([v[half:] for v in (rows, z1, z2, z3)], axis=0)

    out_own, out_far, grad_own, grad_far = ffn(rows_in, rows_go, blocks, half)
    slot_in_grad = reduce_z(grad_own, grad_far)
    slot_out = reduce_z(out_own, out_far)
    near = slot_in_grad.astype(BF16)
    far = swap(near, "expert", 2)
    pieces = gather_expert(near, far)

    part, mix = against(after(slot_out, far), out_grad, combine, False)
    mix = sum_expert(mix)
    (through,) = against(slot_in_grad, tokens, dispatch, True)
    part = after(part, pieces[1], pieces[2])
    logit_grad = through + (part - combine * jnp.repeat(mix, own, axis=0))
    logit_grad_b = logit_grad.astype(BF16)
    slot_term = jnp.einsum(
        "bsm,bmd->sd", logit_grad_b.reshape(images, own, count), tokens, preferred_element_type=F32
    )

    all_grads = jnp.concatenate([logit_grad_b, swap(logit_grad_b, "expert", 1)], axis=0)
    all_grads = jnp.concatenate([all_grads, swap(all_grads, "expert", 2)], axis=0)
    all_grads = gather_x(all_grads)

    term = slot_term.astype(BF16)
    for step in ((4, 8, 12), (1, 2, 3)):
        acc = term.astype(F32)
        for k in step:
            acc = acc + swap(term, "dp", k).astype(F32)
        term = acc.astype(BF16)
    slot_grad = acc.T

    token_grad = tokens_call(spread, lines(all_grads), table, pieces)
    return (token_grad.reshape(images, -1, width), slot_grad)


def solution(mesh):
    return jax.shard_map(
        per_device,
        mesh=mesh,
        in_specs=(
            P("dp", None, None),
            P("dp", None, None),
            P(None, "expert"),
            P("dp", "expert"),
            P("expert", "dp"),
        ),
        out_specs=(P("dp", "expert", None), P(None, "expert")),
        check_vma=False,
    )
```

```python
import math
import jax
import jax.numpy as jnp
from jax import lax
from jax.experimental import pallas as pl
from jax.experimental.pallas import tpu as pltpu
from jax.sharding import PartitionSpec as P

F32 = jnp.float32
BF16 = jnp.bfloat16
ROOT = math.sqrt(2.0 / math.pi)


def swap(value, axis, k):
    count = lax.axis_size(axis)
    return lax.ppermute(value, axis, [(i, i ^ k) for i in range(count)])


def nt(a, b):
    return lax.dot_general(a, b, (((1,), (1,)), ((), ())), preferred_element_type=F32)


def ffn_kernel(rows_in, rows_go, *refs):
    own, l0, r0, f0, both, lb, rb, pb, qb, last, l3, r3, f3 = refs[:13]
    out_own, out_far, grad_own, grad_far = refs[13:17]
    w1, w2 = refs[17:]
    me = lax.axis_index("dp")
    depth = w1.shape[0] // 16

    def place(which, dst):
        for a, sources in (
            (0, (own.at[which], l0.at[which], f0.at[which], r0.at[which])),
            (3, (last.at[which], l3.at[which], f3.at[which], r3.at[which])),
            (1, (both.at[which, 0], lb.at[which, 0], (pb, qb)[which].at[0], rb.at[which, 0])),
            (2, (both.at[which, 1], lb.at[which, 1], (pb, qb)[which].at[1], rb.at[which, 1])),
        ):
            for b, src in enumerate(sources):
                start = pl.multiple_of((me ^ (4 * a + b)) * depth, 16)
                dst[pl.ds(start, depth), :] = src[...]

    place(0, w1)
    place(1, w2)
    pre = jnp.dot(rows_in[...], w1[...], preferred_element_type=F32)
    sq = pre * pre
    th = jnp.tanh(ROOT * (pre + 0.044715 * (sq * pre)))
    cdf = 0.5 * (1.0 + th)
    hidden = (pre * cdf).astype(BF16)
    slope = cdf + 0.5 * pre * (1.0 - th * th) * (ROOT * (1.0 + 3 * 0.044715 * sq))
    hidden_grad = jnp.dot(rows_go[...], w2[...], preferred_element_type=F32)
    pre_grad = (hidden_grad * slope).astype(BF16)
    own_rows = out_own.shape[0]
    grad = nt(pre_grad, w1[...])
    grad_own[...] = grad[:own_rows]
    grad_far[...] = grad[own_rows:].astype(BF16)
    out = nt(hidden, w2[...])
    out_own[...] = out[:own_rows]
    out_far[...] = out[own_rows:].astype(BF16)


def ffn(rows_in, rows_go, blocks, own_rows):
    rows, width = rows_in.shape
    quarter = blocks[0].shape[2]
    vmem = pl.BlockSpec(memory_space=pltpu.VMEM)
    return pl.pallas_call(
        ffn_kernel,
        out_shape=[
            jax.ShapeDtypeStruct((own_rows, width), F32),
            jax.ShapeDtypeStruct((rows - own_rows, width), BF16),
        ]
        * 2,
        in_specs=[vmem] * (2 + len(blocks)),
        out_specs=[vmem] * 4,
        scratch_shapes=[pltpu.VMEM((width, quarter), BF16), pltpu.VMEM((width, quarter), BF16)],
        compiler_params=pltpu.CompilerParams(vmem_limit_bytes=40 * 2**20),
        name="ffn",
    )(rows_in, rows_go, *blocks)


def pick_rows(count):
    col = lax.broadcasted_iota(jnp.int32, (32, count), 1)
    row = lax.broadcasted_iota(jnp.int32, (32, count), 0)
    owner = lax.axis_index("expert") ^ (row // 16)
    return (col == owner * 16 + row % 16).astype(BF16)


def slots_kernel(table, tokens, out_grad, rows, dispatch_own, combine_own, spread):
    step = pl.program_id(0)
    own = 8
    near = table.shape[0] // 2
    count = tokens.shape[1]
    pick = pick_rows(count)
    ins, gos, disp, comb, mine, theirs = [], [], [], [], [], []
    for i in range(2):
        logits = nt(table[...], tokens[i])
        up = jnp.exp(logits[:near] - jnp.max(logits[:near], axis=1, keepdims=True))
        dispatch = up / jnp.sum(up, axis=1, keepdims=True)
        down = jnp.exp(logits - jnp.max(logits, axis=0, keepdims=True))
        combine = down[:own] / jnp.sum(down, axis=0, keepdims=True)
        dispatch_b = dispatch.astype(BF16)
        ins.append(jnp.dot(dispatch_b[:16], tokens[i], preferred_element_type=F32)[:own])
        both = jnp.concatenate([combine, combine], axis=0).astype(BF16)
        gos.append(jnp.dot(both, out_grad[i], preferred_element_type=F32)[:own])
        disp.append(dispatch[:own])
        comb.append(combine)
        lines = nt(pick, dispatch_b).astype(BF16)
        image = 2 * step + i
        q = lax.broadcasted_iota(jnp.int32, (near, 8 * near), 0)
        col = lax.broadcasted_iota(jnp.int32, (near, 8 * near), 1)
        wide = (col == (q // 8) * 64 + q % 8 + image * 8).astype(BF16)
        lines = jnp.dot(lines, wide, preferred_element_type=F32)
        mine.append(lines[:16])
        theirs.append(lines[16:])
    rows[0] = jnp.concatenate(ins, axis=0).astype(BF16)
    rows[1] = jnp.concatenate(gos, axis=0).astype(BF16)
    dispatch_own[...] = jnp.concatenate(disp, axis=0)
    combine_own[...] = jnp.concatenate(comb, axis=0)
    spread[0] = jnp.concatenate(mine, axis=0).astype(BF16)
    spread[1] = jnp.concatenate(theirs, axis=0).astype(BF16)


def slots_call(table, tokens, out_grad):
    images, count, width = tokens.shape
    slots = table.shape[0]
    return pl.pallas_call(
        slots_kernel,
        grid=(images // 2,),
        out_shape=[
            jax.ShapeDtypeStruct((2, images * 8, width), BF16),
            jax.ShapeDtypeStruct((images * 8, count), F32),
            jax.ShapeDtypeStruct((images * 8, count), F32),
            jax.ShapeDtypeStruct((2, images * 16, slots * 4), BF16),
        ],
        in_specs=[
            pl.BlockSpec((slots, width), lambda i: (0, 0)),
            pl.BlockSpec((2, count, width), lambda i: (i, 0, 0)),
            pl.BlockSpec((2, count, width), lambda i: (i, 0, 0)),
        ],
        out_specs=[
            pl.BlockSpec((2, 16, width), lambda i: (0, i, 0)),
            pl.BlockSpec((16, count), lambda i: (i, 0)),
            pl.BlockSpec((16, count), lambda i: (i, 0)),
            pl.BlockSpec((2, 32, slots * 4), lambda i: (0, i, 0)),
        ],
        compiler_params=pltpu.CompilerParams(vmem_limit_bytes=24 * 2**20),
        name="slots",
    )(table, tokens, out_grad)


def against_kernel(over_tokens, rows, big, weight, *outs):
    value = rows[...]
    high = value.astype(BF16)
    low = (value - high.astype(F32)).astype(BF16)
    both = jnp.concatenate([high, low], axis=0)
    prods = []
    for i in range(2):
        prod = nt(both, big[i])
        prods.append(prod[8 * i : 8 * i + 8] + prod[16 + 8 * i : 24 + 8 * i])
    prod = jnp.concatenate(prods, axis=0)
    w = weight[...]
    part = w * prod
    if over_tokens:
        outs[0][...] = w * (prod - jnp.sum(part, axis=1, keepdims=True))
    else:
        outs[0][...] = part
        step = pl.program_id(0)
        for i in range(2):
            outs[1][pl.ds(2 * step + i, 1), :] = jnp.sum(part[8 * i : 8 * i + 8], axis=0, keepdims=True)


def against(rows, big, weight, over_tokens):
    images, count, width = big.shape
    total = images * 8
    out_shape = [jax.ShapeDtypeStruct((total, count), F32)]
    out_specs = [pl.BlockSpec((16, count), lambda i: (i, 0))]
    if not over_tokens:
        out_shape.append(jax.ShapeDtypeStruct((images, count), F32))
        out_specs.append(pl.BlockSpec((images, count), lambda i: (0, 0)))
    return pl.pallas_call(
        lambda *refs: against_kernel(over_tokens, *refs),
        grid=(images // 2,),
        out_shape=out_shape,
        in_specs=[
            pl.BlockSpec((16, width), lambda i: (i, 0)),
            pl.BlockSpec((2, count, width), lambda i: (i, 0, 0)),
            pl.BlockSpec((16, count), lambda i: (i, 0)),
        ],
        out_specs=out_specs,
        compiler_params=pltpu.CompilerParams(vmem_limit_bytes=16 * 2**20),
        name="dispatch_grad" if over_tokens else "combine_grad",
    )(rows, big, weight)


def spread_kernel(spread, pair, one, two, three, out):
    side = spread[...].reshape(2 * spread.shape[1], spread.shape[2])
    depth = side.shape[1] // 4
    total = jnp.zeros(out.shape, F32)
    for x, piece in enumerate((pair, one, two, three)):
        block = piece[...].reshape(depth, piece.shape[2])
        total = total + jnp.dot(side[:, x * depth : (x + 1) * depth], block, preferred_element_type=F32)
    out[...] = total


def spread_call(spread, pieces):
    width = pieces[0].shape[2]
    vmem = pl.BlockSpec(memory_space=pltpu.VMEM)
    return pl.pallas_call(
        spread_kernel,
        out_shape=jax.ShapeDtypeStruct((2 * spread.shape[1], width), F32),
        in_specs=[vmem] * 5,
        out_specs=vmem,
        compiler_params=pltpu.CompilerParams(vmem_limit_bytes=24 * 2**20),
        name="through_slots",
    )(spread, *pieces)


def lines_kernel(pair, one, two, three, table, through, mine, theirs):
    count = pair.shape[1]
    grads = jnp.concatenate([pair[...], one[...], two[...], three[...]], axis=0)
    total = grads.shape[0]
    near = total // 8
    c = lax.broadcasted_iota(jnp.int32, (total, near), 0)
    q = lax.broadcasted_iota(jnp.int32, (total, near), 1)
    fold = ((c // 64 == q // 8) & (c % 8 == q % 8)).astype(BF16)
    x = nt(pick_rows(count), grads)
    half = through.shape[0] // 2
    parts = []
    for side in range(2):
        y = jnp.concatenate([x[16 * side : 16 * side + 16]] * 8, axis=0)
        row = lax.broadcasted_iota(jnp.int32, y.shape, 0)
        col = lax.broadcasted_iota(jnp.int32, y.shape, 1)
        y = jnp.where((col // 8) % 8 == row // 16, y, 0.0).astype(BF16)
        parts.append(jnp.dot(y, fold, preferred_element_type=F32).astype(BF16))
    lines = jnp.concatenate(parts, axis=0)
    sums = through[...] + jnp.dot(lines, table[:near], preferred_element_type=F32)
    mine[...] = sums[:half]
    theirs[...] = sums[half:]


def lines_call(pieces, table, through):
    vmem = pl.BlockSpec(memory_space=pltpu.VMEM)
    half = through.shape[0] // 2
    return pl.pallas_call(
        lines_kernel,
        out_shape=[jax.ShapeDtypeStruct((half, through.shape[1]), F32)] * 2,
        in_specs=[vmem] * 6,
        out_specs=[vmem] * 2,
        compiler_params=pltpu.CompilerParams(vmem_limit_bytes=24 * 2**20),
        name="through_logits",
    )(*pieces, table, through)


def after(value, *earlier):
    return lax.optimization_barrier((value,) + earlier)[0]


def units_of(w_in, w_out):
    z = lax.axis_index("dp") // 4
    quarter = w_in.shape[1] // 4

    def unit(zz):
        start = zz * quarter
        return jnp.stack(
            [
                lax.dynamic_slice_in_dim(w_in, start, quarter, 1),
                lax.dynamic_slice_in_dim(w_out, start, quarter, 1),
            ]
        )

    return [unit(z ^ a) for a in range(4)]


def all_y(unit):
    return swap(unit, "dp", 1), swap(unit, "dp", 3), swap(unit, "dp", 2)


def reduce_z(own, far):
    count = own.shape[0]
    total = own
    for a in (1, 2, 3):
        total = total + swap(far[(a - 1) * count : a * count], "dp", 4 * a).astype(F32)
    return total


def all_x(v):
    return [v, swap(v, "expert", 4), swap(v, "expert", 8), swap(v, "expert", 12)]


def sum_expert(v):
    v = (v + swap(v, "expert", 1)) + (swap(v, "expert", 2) + swap(v, "expert", 3))
    return (v + swap(v, "expert", 4)) + (swap(v, "expert", 8) + swap(v, "expert", 12))


def per_device(tokens, out_grad, slot_params, w_in, w_out):
    images, count, width = tokens.shape
    own = slot_params.shape[1]
    half = images * own
    params = slot_params.T

    units = units_of(w_in, w_out.T)
    l0, r0 = swap(units[0], "dp", 1), swap(units[0], "dp", 3)
    u1 = swap(units[1], "dp", 4)
    u2 = swap(units[2], "dp", 8)
    table = jnp.concatenate([params, swap(params, "expert", 2)], axis=0)
    table = jnp.concatenate(all_x(table), axis=0)
    l0, r0, table = lax.optimization_barrier((l0, r0, table))
    p0, q0 = swap(r0[0], "dp", 1), swap(l0[1], "dp", 3)
    table = jnp.concatenate([table, swap(table, "expert", 1)], axis=0)

    u1, u2, p0, q0, table = lax.optimization_barrier((u1, u2, p0, q0, table))
    both = jnp.stack([u1, u2], axis=1)
    lb, rb = swap(both, "dp", 1), swap(both, "dp", 3)
    u3 = swap(after(units[3], u1), "dp", 12)

    rows, dispatch, combine, spread = slots_call(table, tokens, out_grad)
    rows = rows.reshape(2 * half, width)

    lb, rb, rows = lax.optimization_barrier((lb, rb, rows))
    pb, qb = swap(rb[0], "dp", 1), swap(lb[1], "dp", 3)
    z1, z2, z3 = swap(rows, "dp", 4), swap(rows, "dp", 8), swap(rows, "dp", 12)
    u3 = after(u3, lb, rb)
    l3, r3, f3 = all_y(u3)
    rows_in = jnp.concatenate([v[:half] for v in (rows, z1, z2, z3)], axis=0)
    rows_go = jnp.concatenate([v[half:] for v in (rows, z1, z2, z3)], axis=0)

    f0 = jnp.stack([p0, q0])
    blocks = [units[0], l0, r0, f0, both, lb, rb, pb, qb, u3, l3, r3, f3]
    out_own, out_far, grad_own, grad_far = ffn(rows_in, rows_go, blocks, half)
    slot_in_grad = reduce_z(grad_own, grad_far)
    slot_out = reduce_z(out_own, out_far)

    near = slot_in_grad.astype(BF16)
    far = swap(near, "expert", 2)
    pieces = all_x(jnp.stack([near, far]))
    through = spread_call(spread, pieces)

    part, mix = against(after(slot_out, far), out_grad, combine, False)
    mix = sum_expert(mix)
    (back,) = against(slot_in_grad, tokens, dispatch, True)
    part = after(part, *pieces)
    logit_grad = back + (part - combine * jnp.repeat(mix, own, axis=0))
    logit_grad_b = logit_grad.astype(BF16)
    slot_term = jnp.einsum(
        "bsm,bmd->sd", logit_grad_b.reshape(images, own, count), tokens, preferred_element_type=F32
    )
    line = jnp.concatenate([logit_grad_b, swap(logit_grad_b, "expert", 2)], axis=0)
    mine, theirs = lines_call(all_x(line), table, through)

    term = slot_term.astype(BF16)
    for step in ((4, 8, 12), (1, 2, 3)):
        acc = term.astype(F32)
        for k in step:
            acc = acc + swap(term, "dp", k).astype(F32)
        term = acc.astype(BF16)
    slot_grad = acc.T

    token_grad = (mine + swap(theirs, "expert", 1)).astype(BF16)
    return (token_grad.reshape(images, -1, width), slot_grad)


def solution(mesh):
    return jax.shard_map(
        per_device,
        mesh=mesh,
        in_specs=(
            P("dp", None, None),
            P("dp", None, None),
            P(None, "expert"),
            P("dp", "expert"),
            P("expert", "dp"),
        ),
        out_specs=(P("dp", "expert", None), P(None, "expert")),
        check_vma=False,
    )
```

```python
import math
import jax
import jax.numpy as jnp
from jax import lax
from jax.experimental import pallas as pl
from jax.experimental.pallas import tpu as pltpu
from jax.sharding import PartitionSpec as P

F32 = jnp.float32
BF16 = jnp.bfloat16
ROOT = math.sqrt(2.0 / math.pi)


def swap(value, axis, k):
    count = lax.axis_size(axis)
    return lax.ppermute(value, axis, [(i, i ^ k) for i in range(count)])


def nt(a, b):
    return lax.dot_general(a, b, (((1,), (1,)), ((), ())), preferred_element_type=F32)


def ffn_kernel(rows_in, rows_go, *refs):
    own, l0, r0, p0, q0, both, lb, rb, pb, qb, last, l3, r3, p3, q3 = refs[:15]
    f0, f3 = (p0, q0), (p3, q3)
    outs, grads, (w1, w2) = refs[15:19], refs[19:23], refs[23:]
    me = lax.axis_index("dp")
    depth = w1.shape[0] // 16

    def place(which, dst):
        for a, sources in (
            (0, (own.at[which], l0.at[which], f0[which], r0.at[which])),
            (3, (last.at[which], l3.at[which], f3[which], r3.at[which])),
            (1, (both.at[which, 0], lb.at[which, 0], (pb, qb)[which].at[0], rb.at[which, 0])),
            (2, (both.at[which, 1], lb.at[which, 1], (pb, qb)[which].at[1], rb.at[which, 1])),
        ):
            for b, src in enumerate(sources):
                start = pl.multiple_of((me ^ (4 * a + b)) * depth, 16)
                dst[pl.ds(start, depth), :] = src[...]

    place(0, w1)
    place(1, w2)
    pre = jnp.dot(rows_in[...], w1[...], preferred_element_type=F32)
    sq = pre * pre
    th = jnp.tanh(ROOT * (pre + 0.044715 * (sq * pre)))
    cdf = 0.5 * (1.0 + th)
    hidden = (pre * cdf).astype(BF16)
    slope = cdf + 0.5 * pre * (1.0 - th * th) * (ROOT * (1.0 + 3 * 0.044715 * sq))
    hidden_grad = jnp.dot(rows_go[...], w2[...], preferred_element_type=F32)
    pre_grad = (hidden_grad * slope).astype(BF16)
    own_rows = outs[0].shape[0]
    for whole, blocks in ((nt(hidden, w2[...]), outs), (nt(pre_grad, w1[...]), grads)):
        for a, block in enumerate(blocks):
            block[...] = whole[a * own_rows : (a + 1) * own_rows].astype(block.dtype)


def ffn(rows_in, rows_go, blocks, own_rows):
    rows, width = rows_in.shape
    quarter = blocks[0].shape[2]
    vmem = pl.BlockSpec(memory_space=pltpu.VMEM)
    return pl.pallas_call(
        ffn_kernel,
        out_shape=[jax.ShapeDtypeStruct((own_rows, width), t) for t in (F32, BF16, BF16, BF16)] * 2,
        in_specs=[vmem] * (2 + len(blocks)),
        out_specs=[vmem] * 8,
        scratch_shapes=[pltpu.VMEM((width, quarter), BF16), pltpu.VMEM((width, quarter), BF16)],
        compiler_params=pltpu.CompilerParams(vmem_limit_bytes=40 * 2**20),
        name="ffn",
    )(rows_in, rows_go, *blocks)


def pick_rows(count):
    col = lax.broadcasted_iota(jnp.int32, (32, count), 1)
    row = lax.broadcasted_iota(jnp.int32, (32, count), 0)
    owner = lax.axis_index("expert") ^ (row // 16)
    return (col == owner * 16 + row % 16).astype(BF16)


def slots_kernel(table, tokens, out_grad, rows, dispatch_own, combine_own, spread):
    step = pl.program_id(0)
    own = 8
    near = table.shape[0] // 2
    count = tokens.shape[1]
    pick = pick_rows(count)
    ins, gos, disp, comb, mine, theirs = [], [], [], [], [], []
    for i in range(2):
        logits = nt(table[...], tokens[i])
        up = jnp.exp(logits[:near] - jnp.max(logits[:near], axis=1, keepdims=True))
        dispatch = up / jnp.sum(up, axis=1, keepdims=True)
        down = jnp.exp(logits - jnp.max(logits, axis=0, keepdims=True))
        combine = down[:own] / jnp.sum(down, axis=0, keepdims=True)
        dispatch_b = dispatch.astype(BF16)
        ins.append(jnp.dot(dispatch_b[:16], tokens[i], preferred_element_type=F32)[:own])
        both = jnp.concatenate([combine, combine], axis=0).astype(BF16)
        gos.append(jnp.dot(both, out_grad[i], preferred_element_type=F32)[:own])
        disp.append(dispatch[:own])
        comb.append(combine)
        lines = nt(pick, dispatch_b).astype(BF16)
        image = 2 * step + i
        q = lax.broadcasted_iota(jnp.int32, (near, 8 * near), 0)
        col = lax.broadcasted_iota(jnp.int32, (near, 8 * near), 1)
        wide = (col == (q // 8) * 64 + q % 8 + image * 8).astype(BF16)
        lines = jnp.dot(lines, wide, preferred_element_type=F32)
        mine.append(lines[:16])
        theirs.append(lines[16:])
    rows[0] = jnp.concatenate(ins, axis=0).astype(BF16)
    rows[1] = jnp.concatenate(gos, axis=0).astype(BF16)
    dispatch_own[...] = jnp.concatenate(disp, axis=0)
    combine_own[...] = jnp.concatenate(comb, axis=0)
    spread[0] = jnp.concatenate(mine, axis=0).astype(BF16)
    spread[1] = jnp.concatenate(theirs, axis=0).astype(BF16)


def slots_call(table, tokens, out_grad):
    images, count, width = tokens.shape
    slots = table.shape[0]
    return pl.pallas_call(
        slots_kernel,
        grid=(images // 2,),
        out_shape=[
            jax.ShapeDtypeStruct((2, images * 8, width), BF16),
            jax.ShapeDtypeStruct((images * 8, count), F32),
            jax.ShapeDtypeStruct((images * 8, count), F32),
            jax.ShapeDtypeStruct((2, images * 16, slots * 4), BF16),
        ],
        in_specs=[
            pl.BlockSpec((slots, width), lambda i: (0, 0)),
            pl.BlockSpec((2, count, width), lambda i: (i, 0, 0)),
            pl.BlockSpec((2, count, width), lambda i: (i, 0, 0)),
        ],
        out_specs=[
            pl.BlockSpec((2, 16, width), lambda i: (0, i, 0)),
            pl.BlockSpec((16, count), lambda i: (i, 0)),
            pl.BlockSpec((16, count), lambda i: (i, 0)),
            pl.BlockSpec((2, 32, slots * 4), lambda i: (0, i, 0)),
        ],
        compiler_params=pltpu.CompilerParams(vmem_limit_bytes=24 * 2**20),
        name="slots",
    )(table, tokens, out_grad)


def against_kernel(over_tokens, rows, big, weight, *outs):
    value = rows[...]
    high = value.astype(BF16)
    low = (value - high.astype(F32)).astype(BF16)
    both = jnp.concatenate([high, low], axis=0)
    prods = []
    for i in range(2):
        prod = nt(both, big[i])
        prods.append(prod[8 * i : 8 * i + 8] + prod[16 + 8 * i : 24 + 8 * i])
    prod = jnp.concatenate(prods, axis=0)
    w = weight[...]
    part = w * prod
    if over_tokens:
        outs[0][...] = w * (prod - jnp.sum(part, axis=1, keepdims=True))
    else:
        outs[0][...] = part
        step = pl.program_id(0)
        for i in range(2):
            outs[1][pl.ds(2 * step + i, 1), :] = jnp.sum(part[8 * i : 8 * i + 8], axis=0, keepdims=True)


def against(rows, big, weight, over_tokens):
    images, count, width = big.shape
    total = images * 8
    out_shape = [jax.ShapeDtypeStruct((total, count), F32)]
    out_specs = [pl.BlockSpec((16, count), lambda i: (i, 0))]
    if not over_tokens:
        out_shape.append(jax.ShapeDtypeStruct((images, count), F32))
        out_specs.append(pl.BlockSpec((images, count), lambda i: (0, 0)))
    return pl.pallas_call(
        lambda *refs: against_kernel(over_tokens, *refs),
        grid=(images // 2,),
        out_shape=out_shape,
        in_specs=[
            pl.BlockSpec((16, width), lambda i: (i, 0)),
            pl.BlockSpec((2, count, width), lambda i: (i, 0, 0)),
            pl.BlockSpec((16, count), lambda i: (i, 0)),
        ],
        out_specs=out_specs,
        compiler_params=pltpu.CompilerParams(vmem_limit_bytes=16 * 2**20),
        name="dispatch_grad" if over_tokens else "combine_grad",
    )(rows, big, weight)


def lines_kernel(grads, table, out):
    total, count = grads.shape
    near = total // 8
    c = lax.broadcasted_iota(jnp.int32, (total, near), 0)
    q = lax.broadcasted_iota(jnp.int32, (total, near), 1)
    fold = ((c // 64 == q // 8) & (c % 8 == q % 8)).astype(BF16)
    x = nt(pick_rows(count), grads[...])
    parts = []
    for side in range(2):
        y = jnp.concatenate([x[16 * side : 16 * side + 16]] * 8, axis=0)
        row = lax.broadcasted_iota(jnp.int32, y.shape, 0)
        col = lax.broadcasted_iota(jnp.int32, y.shape, 1)
        y = jnp.where((col // 8) % 8 == row // 16, y, 0.0).astype(BF16)
        parts.append(jnp.dot(y, fold, preferred_element_type=F32).astype(BF16))
    lines = jnp.concatenate(parts, axis=0)
    out[...] = jnp.dot(lines, table[:near], preferred_element_type=F32)


def lines_call(line, table):
    vmem = pl.BlockSpec(memory_space=pltpu.VMEM)
    return pl.pallas_call(
        lines_kernel,
        out_shape=jax.ShapeDtypeStruct((256, table.shape[1]), F32),
        in_specs=[vmem] * 2,
        out_specs=vmem,
        compiler_params=pltpu.CompilerParams(vmem_limit_bytes=24 * 2**20),
        name="through_logits",
    )(line, table)


def spread_kernel(spread, pair, one, two, three, base, mine, theirs):
    half = mine.shape[0]
    side = spread[...].reshape(2 * half, spread.shape[2])
    depth = side.shape[1] // 4
    total = base[...]
    for x, piece in enumerate((pair, one, two, three)):
        block = piece[...].reshape(depth, piece.shape[2])
        total = total + jnp.dot(side[:, x * depth : (x + 1) * depth], block, preferred_element_type=F32)
    mine[...] = total[:half]
    theirs[...] = total[half:]


def spread_call(spread, pieces, base):
    vmem = pl.BlockSpec(memory_space=pltpu.VMEM)
    half, width = base.shape[0] // 2, base.shape[1]
    return pl.pallas_call(
        spread_kernel,
        out_shape=[jax.ShapeDtypeStruct((half, width), F32)] * 2,
        in_specs=[vmem] * 6,
        out_specs=[vmem] * 2,
        compiler_params=pltpu.CompilerParams(vmem_limit_bytes=24 * 2**20),
        name="through_slots",
    )(spread, *pieces, base)


def after(value, *earlier):
    return lax.optimization_barrier((value,) + earlier)[0]


def units_of(w_in, w_out):
    z = lax.axis_index("dp") // 4
    quarter = w_in.shape[1] // 4

    def unit(zz):
        start = zz * quarter
        return jnp.stack(
            [
                lax.dynamic_slice_in_dim(w_in, start, quarter, 1),
                lax.dynamic_slice_in_dim(w_out, start, quarter, 1),
            ]
        )

    return [unit(z ^ a) for a in range(4)]


def together(*values):
    return lax.optimization_barrier(values)


def reduce_z(own, *far):
    one, two, three = together(*[swap(v, "dp", 4 * a) for a, v in enumerate(far, 1)])
    return (own + one.astype(F32)) + (two.astype(F32) + three.astype(F32))


def all_x(v):
    return [v, *together(swap(v, "expert", 4), swap(v, "expert", 8), swap(v, "expert", 12))]


def doubled(v, axis, *steps):
    for k in steps:
        v = jnp.concatenate([v, swap(v, axis, k)], axis=0)
    return v


def summed(v, axis, *steps):
    for k in steps:
        v = v + swap(v, axis, k)
    return v


def per_device(tokens, out_grad, slot_params, w_in, w_out):
    images, count, width = tokens.shape
    own = slot_params.shape[1]
    half = images * own

    units = units_of(w_in, w_out.T)
    l0, r0 = swap(units[0], "dp", 1), swap(units[0], "dp", 3)
    u1 = swap(units[1], "dp", 4)
    u2 = swap(units[2], "dp", 8)
    table = doubled(slot_params.T, "expert", 2, 4)
    l0, r0, table = together(l0, r0, table)
    p0, q0 = swap(r0[0], "dp", 1), swap(l0[1], "dp", 3)
    table = doubled(table, "expert", 8, 1)

    u1, u2, p0, q0, table = together(u1, u2, p0, q0, table)
    both = jnp.stack([u1, u2], axis=1)
    lb, rb = swap(both, "dp", 1), swap(both, "dp", 3)
    u3 = swap(after(units[3], u1), "dp", 12)
    rows, dispatch, combine, spread = slots_call(table, tokens, out_grad)
    rows = rows.reshape(2 * half, width)

    lb, rb, u3, rows = together(lb, rb, u3, rows)
    z1, z2 = swap(rows, "dp", 4), swap(rows, "dp", 8)
    l3, r3 = swap(u3, "dp", 1), swap(u3, "dp", 3)
    pb, qb = swap(rb[0], "dp", 1), swap(lb[1], "dp", 3)
    l3, r3, z2 = together(l3, r3, z2)
    p3, q3 = swap(r3[0], "dp", 1), swap(l3[1], "dp", 3)
    z3 = swap(z2, "dp", 4)
    pb, qb, p3, q3, z3 = together(pb, qb, p3, q3, z3)
    rows_in = jnp.concatenate([v[:half] for v in (rows, z1, z2, z3)], axis=0)
    rows_go = jnp.concatenate([v[half:] for v in (rows, z1, z2, z3)], axis=0)

    blocks = [units[0], l0, r0, p0, q0, both, lb, rb, pb, qb, u3, l3, r3, p3, q3]
    halves = ffn(rows_in, rows_go, blocks, half)
    slot_out = reduce_z(*halves[:4])
    slot_in_grad = reduce_z(*halves[4:])
    near = slot_in_grad.astype(BF16)
    far = swap(near, "expert", 2)

    part, mix = against(slot_out, out_grad, combine, False)
    mix = summed(mix, "expert", 1, 2, 4, 8)
    (back,) = against(slot_in_grad, tokens, dispatch, True)
    logit_grad = back + (part - combine * jnp.repeat(mix, own, axis=0))
    logit_grad_b = logit_grad.astype(BF16)
    slot_term = jnp.einsum(
        "bsm,bmd->sd", logit_grad_b.reshape(images, own, count), tokens, preferred_element_type=F32
    )
    line = doubled(logit_grad_b, "expert", 2)
    line = doubled(after(line, far), "expert", 4, 8)
    base = lines_call(line, table)

    pieces = all_x(jnp.stack([near, far]))
    slot_sum = summed(slot_term, "dp", 4, 8, 1)
    slot_grad = summed(after(slot_sum, *pieces), "dp", 2).T

    mine, theirs = spread_call(spread, pieces, after(base, slot_sum))
    token_grad = (mine + swap(theirs, "expert", 1)).astype(BF16)
    return (token_grad.reshape(images, -1, width), slot_grad)


def solution(mesh):
    return jax.shard_map(
        per_device,
        mesh=mesh,
        in_specs=(
            P("dp", None, None),
            P("dp", None, None),
            P(None, "expert"),
            P("dp", "expert"),
            P("expert", "dp"),
        ),
        out_specs=(P("dp", "expert", None), P(None, "expert")),
        check_vma=False,
    )
```

```python
import math
import jax
import jax.numpy as jnp
from jax import lax
from jax.experimental import pallas as pl
from jax.experimental.pallas import tpu as pltpu
from jax.sharding import PartitionSpec as P

F32 = jnp.float32
BF16 = jnp.bfloat16
ROOT = math.sqrt(2.0 / math.pi)


def swap(value, axis, k):
    count = lax.axis_size(axis)
    return lax.ppermute(value, axis, [(i, i ^ k) for i in range(count)])


def nt(a, b):
    return lax.dot_general(a, b, (((1,), (1,)), ((), ())), preferred_element_type=F32)


def ffn_kernel(rows_in, rows_go, *refs):
    own, l0, r0, p0, q0, both, lb, rb, pb, qb, last, l3, r3, p3, q3 = refs[:15]
    f0, f3 = (p0, q0), (p3, q3)
    outs, grads, (w1, w2) = refs[15:19], refs[19:23], refs[23:]
    me = lax.axis_index("dp")
    depth = w1.shape[0] // 16

    def place(which, dst):
        for a, sources in (
            (0, (own.at[which], l0.at[which], f0[which], r0.at[which])),
            (3, (last.at[which], l3.at[which], f3[which], r3.at[which])),
            (1, (both.at[which, 0], lb.at[which, 0], (pb, qb)[which].at[0], rb.at[which, 0])),
            (2, (both.at[which, 1], lb.at[which, 1], (pb, qb)[which].at[1], rb.at[which, 1])),
        ):
            for b, src in enumerate(sources):
                start = pl.multiple_of((me ^ (4 * a + b)) * depth, 16)
                dst[pl.ds(start, depth), :] = src[...]

    place(0, w1)
    place(1, w2)
    pre = jnp.dot(rows_in[...], w1[...], preferred_element_type=F32)
    sq = pre * pre
    th = jnp.tanh(ROOT * (pre + 0.044715 * (sq * pre)))
    cdf = 0.5 * (1.0 + th)
    hidden = (pre * cdf).astype(BF16)
    slope = cdf + 0.5 * pre * (1.0 - th * th) * (ROOT * (1.0 + 3 * 0.044715 * sq))
    hidden_grad = jnp.dot(rows_go[...], w2[...], preferred_element_type=F32)
    pre_grad = (hidden_grad * slope).astype(BF16)
    own_rows = outs[0].shape[0]
    for whole, blocks in ((nt(hidden, w2[...]), outs), (nt(pre_grad, w1[...]), grads)):
        for a, block in enumerate(blocks):
            block[...] = whole[a * own_rows : (a + 1) * own_rows].astype(block.dtype)


def ffn(rows_in, rows_go, blocks, own_rows):
    rows, width = rows_in.shape
    quarter = blocks[0].shape[2]
    vmem = pl.BlockSpec(memory_space=pltpu.VMEM)
    return pl.pallas_call(
        ffn_kernel,
        out_shape=[jax.ShapeDtypeStruct((own_rows, width), t) for t in (F32, BF16, BF16, BF16)] * 2,
        in_specs=[vmem] * (2 + len(blocks)),
        out_specs=[vmem] * 8,
        scratch_shapes=[pltpu.VMEM((width, quarter), BF16), pltpu.VMEM((width, quarter), BF16)],
        compiler_params=pltpu.CompilerParams(vmem_limit_bytes=40 * 2**20),
        name="ffn",
    )(rows_in, rows_go, *blocks)


def pick_rows(count):
    col = lax.broadcasted_iota(jnp.int32, (32, count), 1)
    row = lax.broadcasted_iota(jnp.int32, (32, count), 0)
    owner = lax.axis_index("expert") ^ (row // 16)
    return (col == owner * 16 + row % 16).astype(BF16)


def slots_kernel(table, tokens, out_grad, rows, dispatch_own, combine_own, spread):
    step = pl.program_id(0)
    own = 8
    near = table.shape[0] // 2
    count = tokens.shape[1]
    pick = pick_rows(count)
    ins, gos, disp, comb, mine, theirs = [], [], [], [], [], []
    for i in range(2):
        logits = nt(table[...], tokens[i])
        up = jnp.exp(logits[:near] - jnp.max(logits[:near], axis=1, keepdims=True))
        dispatch = up / jnp.sum(up, axis=1, keepdims=True)
        down = jnp.exp(logits - jnp.max(logits, axis=0, keepdims=True))
        combine = down[:own] / jnp.sum(down, axis=0, keepdims=True)
        dispatch_b = dispatch.astype(BF16)
        ins.append(jnp.dot(dispatch_b[:16], tokens[i], preferred_element_type=F32)[:own])
        both = jnp.concatenate([combine, combine], axis=0).astype(BF16)
        gos.append(jnp.dot(both, out_grad[i], preferred_element_type=F32)[:own])
        disp.append(dispatch[:own])
        comb.append(combine)
        lines = nt(pick, dispatch_b).astype(BF16)
        image = 2 * step + i
        q = lax.broadcasted_iota(jnp.int32, (near, 8 * near), 0)
        col = lax.broadcasted_iota(jnp.int32, (near, 8 * near), 1)
        wide = (col == (q // 8) * 64 + q % 8 + image * 8).astype(BF16)
        lines = jnp.dot(lines, wide, preferred_element_type=F32)
        mine.append(lines[:16])
        theirs.append(lines[16:])
    rows[0] = jnp.concatenate(ins, axis=0).astype(BF16)
    rows[1] = jnp.concatenate(gos, axis=0).astype(BF16)
    dispatch_own[...] = jnp.concatenate(disp, axis=0)
    combine_own[...] = jnp.concatenate(comb, axis=0)
    spread[0] = jnp.concatenate(mine, axis=0).astype(BF16)
    spread[1] = jnp.concatenate(theirs, axis=0).astype(BF16)


def slots_call(table, tokens, out_grad):
    images, count, width = tokens.shape
    slots = table.shape[0]
    return pl.pallas_call(
        slots_kernel,
        grid=(images // 2,),
        out_shape=[
            jax.ShapeDtypeStruct((2, images * 8, width), BF16),
            jax.ShapeDtypeStruct((images * 8, count), F32),
            jax.ShapeDtypeStruct((images * 8, count), F32),
            jax.ShapeDtypeStruct((2, images * 16, slots * 4), BF16),
        ],
        in_specs=[
            pl.BlockSpec((slots, width), lambda i: (0, 0)),
            pl.BlockSpec((2, count, width), lambda i: (i, 0, 0)),
            pl.BlockSpec((2, count, width), lambda i: (i, 0, 0)),
        ],
        out_specs=[
            pl.BlockSpec((2, 16, width), lambda i: (0, i, 0)),
            pl.BlockSpec((16, count), lambda i: (i, 0)),
            pl.BlockSpec((16, count), lambda i: (i, 0)),
            pl.BlockSpec((2, 32, slots * 4), lambda i: (0, i, 0)),
        ],
        compiler_params=pltpu.CompilerParams(vmem_limit_bytes=24 * 2**20),
        name="slots",
    )(table, tokens, out_grad)


def against_kernel(over_tokens, rows, big, weight, *outs):
    value = rows[...]
    high = value.astype(BF16)
    low = (value - high.astype(F32)).astype(BF16)
    both = jnp.concatenate([high, low], axis=0)
    prods = []
    for i in range(2):
        prod = nt(both, big[i])
        prods.append(prod[8 * i : 8 * i + 8] + prod[16 + 8 * i : 24 + 8 * i])
    prod = jnp.concatenate(prods, axis=0)
    w = weight[...]
    part = w * prod
    if over_tokens:
        outs[0][...] = w * (prod - jnp.sum(part, axis=1, keepdims=True))
    else:
        outs[0][...] = part
        step = pl.program_id(0)
        for i in range(2):
            outs[1][pl.ds(2 * step + i, 1), :] = jnp.sum(part[8 * i : 8 * i + 8], axis=0, keepdims=True)


def against(rows, big, weight, over_tokens):
    images, count, width = big.shape
    total = images * 8
    out_shape = [jax.ShapeDtypeStruct((total, count), F32)]
    out_specs = [pl.BlockSpec((16, count), lambda i: (i, 0))]
    if not over_tokens:
        out_shape.append(jax.ShapeDtypeStruct((images, count), F32))
        out_specs.append(pl.BlockSpec((images, count), lambda i: (0, 0)))
    return pl.pallas_call(
        lambda *refs: against_kernel(over_tokens, *refs),
        grid=(images // 2,),
        out_shape=out_shape,
        in_specs=[
            pl.BlockSpec((16, width), lambda i: (i, 0)),
            pl.BlockSpec((2, count, width), lambda i: (i, 0, 0)),
            pl.BlockSpec((16, count), lambda i: (i, 0)),
        ],
        out_specs=out_specs,
        compiler_params=pltpu.CompilerParams(vmem_limit_bytes=16 * 2**20),
        name="dispatch_grad" if over_tokens else "combine_grad",
    )(rows, big, weight)


def lines_kernel(grads, table, out):
    total, count = grads.shape
    near = total // 8
    c = lax.broadcasted_iota(jnp.int32, (total, near), 0)
    q = lax.broadcasted_iota(jnp.int32, (total, near), 1)
    fold = ((c // 64 == q // 8) & (c % 8 == q % 8)).astype(BF16)
    x = nt(pick_rows(count), grads[...])
    parts = []
    for side in range(2):
        y = jnp.concatenate([x[16 * side : 16 * side + 16]] * 8, axis=0)
        row = lax.broadcasted_iota(jnp.int32, y.shape, 0)
        col = lax.broadcasted_iota(jnp.int32, y.shape, 1)
        y = jnp.where((col // 8) % 8 == row // 16, y, 0.0).astype(BF16)
        parts.append(jnp.dot(y, fold, preferred_element_type=F32).astype(BF16))
    lines = jnp.concatenate(parts, axis=0)
    out[...] = jnp.dot(lines, table[:near], preferred_element_type=F32)


def lines_call(line, table):
    vmem = pl.BlockSpec(memory_space=pltpu.VMEM)
    return pl.pallas_call(
        lines_kernel,
        out_shape=jax.ShapeDtypeStruct((256, table.shape[1]), F32),
        in_specs=[vmem] * 2,
        out_specs=vmem,
        compiler_params=pltpu.CompilerParams(vmem_limit_bytes=24 * 2**20),
        name="through_logits",
    )(line, table)


def spread_kernel(spread, pair, one, two, three, base, mine, theirs):
    half = mine.shape[0]
    side = spread[...].reshape(2 * half, spread.shape[2])
    depth = side.shape[1] // 4
    total = base[...]
    for x, piece in enumerate((pair, one, two, three)):
        block = piece[...].reshape(depth, piece.shape[2])
        total = total + jnp.dot(side[:, x * depth : (x + 1) * depth], block, preferred_element_type=F32)
    mine[...] = total[:half]
    theirs[...] = total[half:]


def spread_call(spread, pieces, base):
    vmem = pl.BlockSpec(memory_space=pltpu.VMEM)
    half, width = base.shape[0] // 2, base.shape[1]
    return pl.pallas_call(
        spread_kernel,
        out_shape=[jax.ShapeDtypeStruct((half, width), F32)] * 2,
        in_specs=[vmem] * 6,
        out_specs=[vmem] * 2,
        compiler_params=pltpu.CompilerParams(vmem_limit_bytes=24 * 2**20),
        name="through_slots",
    )(spread, *pieces, base)


def after(value, *earlier):
    return lax.optimization_barrier((value,) + earlier)[0]


def units_of(w_in, w_out):
    z = lax.axis_index("dp") // 4
    quarter = w_in.shape[1] // 4

    def unit(zz):
        start = zz * quarter
        return jnp.stack(
            [
                lax.dynamic_slice_in_dim(w_in, start, quarter, 1),
                lax.dynamic_slice_in_dim(w_out, start, quarter, 1),
            ]
        )

    return [unit(z ^ a) for a in range(4)]


def together(*values):
    return lax.optimization_barrier(values)


def reduce_z(own, *far):
    one, two, three = together(*[swap(v, "dp", 4 * a) for a, v in enumerate(far, 1)])
    return (own + one.astype(F32)) + (two.astype(F32) + three.astype(F32))


def all_x(v):
    return [v, *together(swap(v, "expert", 4), swap(v, "expert", 8), swap(v, "expert", 12))]


def doubled(v, axis, *steps):
    for k in steps:
        v = jnp.concatenate([v, swap(v, axis, k)], axis=0)
    return v


def summed(v, axis, *steps):
    for k in steps:
        v = v + swap(v, axis, k)
    return v


def per_device(tokens, out_grad, slot_params, w_in, w_out):
    images, count, width = tokens.shape
    own = slot_params.shape[1]
    half = images * own

    units = units_of(w_in, w_out.T)
    l0, r0 = swap(units[0], "dp", 1), swap(units[0], "dp", 3)
    u1 = swap(units[1], "dp", 4)
    u2 = swap(units[2], "dp", 8)
    table = doubled(slot_params.T, "expert", 2, 4)
    l0, r0, table = together(l0, r0, table)
    p0, q0 = swap(r0[0], "dp", 1), swap(l0[1], "dp", 3)
    table = doubled(table, "expert", 8)

    u1, u2, p0, q0, table = together(u1, u2, p0, q0, table)
    both = jnp.stack([u1, u2], axis=1)
    lb, rb = swap(both, "dp", 1), swap(both, "dp", 3)
    u3 = swap(after(units[3], u1), "dp", 12)
    table = doubled(table, "expert", 1)
    rows, dispatch, combine, spread = slots_call(table, tokens, out_grad)
    rows = rows.reshape(2 * half, width)

    lb, rb, u3, rows = together(lb, rb, u3, rows)
    z2 = swap(rows, "dp", 8)
    l3, r3 = swap(u3, "dp", 1), swap(u3, "dp", 3)
    pb, qb = swap(rb[0], "dp", 1), swap(lb[1], "dp", 3)
    l3, r3 = together(l3, r3)
    p3, q3 = swap(r3[0], "dp", 1), swap(l3[1], "dp", 3)
    z1 = swap(after(rows, l3), "dp", 4)
    z3 = swap(z2, "dp", 4)
    pb, qb, p3, q3, z1, z3 = together(pb, qb, p3, q3, z1, z3)
    rows_in = jnp.concatenate([v[:half] for v in (rows, z1, z2, z3)], axis=0)
    rows_go = jnp.concatenate([v[half:] for v in (rows, z1, z2, z3)], axis=0)

    blocks = [units[0], l0, r0, p0, q0, both, lb, rb, pb, qb, u3, l3, r3, p3, q3]
    halves = ffn(rows_in, rows_go, blocks, half)
    slot_out = reduce_z(*halves[:4])
    slot_in_grad = reduce_z(*halves[4:])
    near = slot_in_grad.astype(BF16)
    far = swap(near, "expert", 2)

    part, mix = against(slot_out, out_grad, combine, False)
    mix = summed(mix, "expert", 1, 2, 4)
    mix = summed(after(mix, near), "expert", 8)
    (back,) = against(slot_in_grad, tokens, dispatch, True)
    logit_grad = back + (part - combine * jnp.repeat(mix, own, axis=0))
    logit_grad_b = logit_grad.astype(BF16)
    term = jnp.einsum(
        "bsm,bmd->sd", logit_grad_b.reshape(images, own, count), tokens, preferred_element_type=F32
    )

    line = doubled(logit_grad_b, "expert", 2)
    term = summed(term, "dp", 4)
    line, term, far = together(line, term, far)
    pieces = all_x(jnp.stack([near, far]))
    line = doubled(line, "expert", 4)
    term = summed(term, "dp", 8)
    line, term = together(line, term)
    line = doubled(line, "expert", 8)
    term = summed(term, "dp", 1)
    base = lines_call(line, table)
    slot_grad = summed(after(term, *pieces), "dp", 2).T

    mine, theirs = spread_call(spread, pieces, after(base, term))
    token_grad = (mine + swap(theirs, "expert", 1)).astype(BF16)
    return (token_grad.reshape(images, -1, width), slot_grad)


def solution(mesh):
    return jax.shard_map(
        per_device,
        mesh=mesh,
        in_specs=(
            P("dp", None, None),
            P("dp", None, None),
            P(None, "expert"),
            P("dp", "expert"),
            P("expert", "dp"),
        ),
        out_specs=(P("dp", "expert", None), P(None, "expert")),
        check_vma=False,
    )
```

```python
import math
import jax
import jax.numpy as jnp
from jax import lax
from jax.experimental import pallas as pl
from jax.experimental.pallas import tpu as pltpu
from jax.sharding import PartitionSpec as P

F32 = jnp.float32
BF16 = jnp.bfloat16
ROOT = math.sqrt(2.0 / math.pi)


def swap(value, axis, k):
    count = lax.axis_size(axis)
    return lax.ppermute(value, axis, [(i, i ^ k) for i in range(count)])


def nt(a, b):
    return lax.dot_general(a, b, (((1,), (1,)), ((), ())), preferred_element_type=F32)


def ffn_kernel(rows_in, rows_go, *refs):
    own, l0, r0, p0, q0, both, lb, rb, pb, qb, last, l3, r3, p3, q3 = refs[:15]
    f0, f3 = (p0, q0), (p3, q3)
    outs, grads, (w1, w2) = refs[15:19], refs[19:22], refs[22:]
    me = lax.axis_index("dp")
    depth = w1.shape[0] // 16

    def place(which, dst):
        for a, sources in (
            (0, (own.at[which], l0.at[which], f0[which], r0.at[which])),
            (3, (last.at[which], l3.at[which], f3[which], r3.at[which])),
            (1, (both.at[which, 0], lb.at[which, 0], (pb, qb)[which].at[0], rb.at[which, 0])),
            (2, (both.at[which, 1], lb.at[which, 1], (pb, qb)[which].at[1], rb.at[which, 1])),
        ):
            for b, src in enumerate(sources):
                start = pl.multiple_of((me ^ (4 * a + b)) * depth, 16)
                dst[pl.ds(start, depth), :] = src[...]

    place(0, w1)
    place(1, w2)
    pre = jnp.dot(rows_in[...], w1[...], preferred_element_type=F32)
    sq = pre * pre
    th = jnp.tanh(ROOT * (pre + 0.044715 * (sq * pre)))
    cdf = 0.5 * (1.0 + th)
    hidden = (pre * cdf).astype(BF16)
    slope = cdf + 0.5 * pre * (1.0 - th * th) * (ROOT * (1.0 + 3 * 0.044715 * sq))
    hidden_grad = jnp.dot(rows_go[...], w2[...], preferred_element_type=F32)
    pre_grad = (hidden_grad * slope).astype(BF16)
    rows = outs[0].shape[0]
    out = nt(hidden, w2[...])
    for a, block in enumerate(outs):
        block[...] = out[a * rows : (a + 1) * rows].astype(block.dtype)
    grad = nt(pre_grad, w1[...])
    grads[0][...] = grad[:rows]
    grads[1][...] = grad[2 * rows : 3 * rows]
    grads[2][0] = grad[rows : 2 * rows].astype(BF16)
    grads[2][1] = grad[3 * rows :].astype(BF16)


def ffn(rows_in, rows_go, blocks, own_rows):
    rows, width = rows_in.shape
    quarter = blocks[0].shape[2]
    vmem = pl.BlockSpec(memory_space=pltpu.VMEM)
    return pl.pallas_call(
        ffn_kernel,
        out_shape=[jax.ShapeDtypeStruct((own_rows, width), t) for t in (F32, BF16, BF16, BF16, F32, F32)]
        + [jax.ShapeDtypeStruct((2, own_rows, width), BF16)],
        in_specs=[vmem] * (2 + len(blocks)),
        out_specs=[vmem] * 7,
        scratch_shapes=[pltpu.VMEM((width, quarter), BF16), pltpu.VMEM((width, quarter), BF16)],
        compiler_params=pltpu.CompilerParams(vmem_limit_bytes=40 * 2**20),
        name="ffn",
    )(rows_in, rows_go, *blocks)


def pick_rows(count):
    col = lax.broadcasted_iota(jnp.int32, (32, count), 1)
    row = lax.broadcasted_iota(jnp.int32, (32, count), 0)
    owner = lax.axis_index("expert") ^ (row // 16)
    return (col == owner * 16 + row % 16).astype(BF16)


def slots_kernel(table, tokens, out_grad, rows, dispatch_own, combine_own, spread):
    step = pl.program_id(0)
    own = 8
    near = table.shape[0] // 2
    count = tokens.shape[1]
    pick = pick_rows(count)
    ins, gos, disp, comb, mine, theirs = [], [], [], [], [], []
    for i in range(2):
        logits = nt(table[...], tokens[i])
        up = jnp.exp(logits[:near] - jnp.max(logits[:near], axis=1, keepdims=True))
        dispatch = up / jnp.sum(up, axis=1, keepdims=True)
        down = jnp.exp(logits - jnp.max(logits, axis=0, keepdims=True))
        combine = down[:own] / jnp.sum(down, axis=0, keepdims=True)
        dispatch_b = dispatch.astype(BF16)
        ins.append(jnp.dot(dispatch_b[:16], tokens[i], preferred_element_type=F32)[:own])
        both = jnp.concatenate([combine, combine], axis=0).astype(BF16)
        gos.append(jnp.dot(both, out_grad[i], preferred_element_type=F32)[:own])
        disp.append(dispatch[:own])
        comb.append(combine)
        lines = nt(pick, dispatch_b).astype(BF16)
        image = 2 * step + i
        q = lax.broadcasted_iota(jnp.int32, (near, 8 * near), 0)
        col = lax.broadcasted_iota(jnp.int32, (near, 8 * near), 1)
        wide = (col == (q // 8) * 64 + q % 8 + image * 8).astype(BF16)
        lines = jnp.dot(lines, wide, preferred_element_type=F32)
        mine.append(lines[:16])
        theirs.append(lines[16:])
    rows[0] = jnp.concatenate(ins, axis=0).astype(BF16)
    rows[1] = jnp.concatenate(gos, axis=0).astype(BF16)
    dispatch_own[...] = jnp.concatenate(disp, axis=0)
    combine_own[...] = jnp.concatenate(comb, axis=0)
    spread[0] = jnp.concatenate(mine, axis=0).astype(BF16)
    spread[1] = jnp.concatenate(theirs, axis=0).astype(BF16)


def slots_call(table, tokens, out_grad):
    images, count, width = tokens.shape
    slots = table.shape[0]
    return pl.pallas_call(
        slots_kernel,
        grid=(images // 2,),
        out_shape=[
            jax.ShapeDtypeStruct((2, images * 8, width), BF16),
            jax.ShapeDtypeStruct((images * 8, count), F32),
            jax.ShapeDtypeStruct((images * 8, count), F32),
            jax.ShapeDtypeStruct((2, images * 16, slots * 4), BF16),
        ],
        in_specs=[
            pl.BlockSpec((slots, width), lambda i: (0, 0)),
            pl.BlockSpec((2, count, width), lambda i: (i, 0, 0)),
            pl.BlockSpec((2, count, width), lambda i: (i, 0, 0)),
        ],
        out_specs=[
            pl.BlockSpec((2, 16, width), lambda i: (0, i, 0)),
            pl.BlockSpec((16, count), lambda i: (i, 0)),
            pl.BlockSpec((16, count), lambda i: (i, 0)),
            pl.BlockSpec((2, 32, slots * 4), lambda i: (0, i, 0)),
        ],
        compiler_params=pltpu.CompilerParams(vmem_limit_bytes=24 * 2**20),
        cost_estimate=pl.CostEstimate(
            flops=2 * tokens.size * (slots + 32), bytes_accessed=4 * tokens.size, transcendentals=2 * images * slots * count
        ),
        name="slots",
    )(table, tokens, out_grad)


def against_kernel(over_tokens, rows, big, weight, *outs):
    value = rows[...]
    high = value.astype(BF16)
    low = (value - high.astype(F32)).astype(BF16)
    both = jnp.concatenate([high, low], axis=0)
    prods = []
    for i in range(2):
        prod = nt(both, big[i])
        prods.append(prod[8 * i : 8 * i + 8] + prod[16 + 8 * i : 24 + 8 * i])
    prod = jnp.concatenate(prods, axis=0)
    w = weight[...]
    part = w * prod
    if over_tokens:
        outs[0][...] = w * (prod - jnp.sum(part, axis=1, keepdims=True))
    else:
        outs[0][...] = part
        step = pl.program_id(0)
        for i in range(2):
            outs[1][pl.ds(2 * step + i, 1), :] = jnp.sum(part[8 * i : 8 * i + 8], axis=0, keepdims=True)


def against(rows, big, weight, over_tokens):
    images, count, width = big.shape
    total = images * 8
    out_shape = [jax.ShapeDtypeStruct((total, count), F32)]
    out_specs = [pl.BlockSpec((16, count), lambda i: (i, 0))]
    if not over_tokens:
        out_shape.append(jax.ShapeDtypeStruct((images, count), F32))
        out_specs.append(pl.BlockSpec((images, count), lambda i: (0, 0)))
    return pl.pallas_call(
        lambda *refs: against_kernel(over_tokens, *refs),
        grid=(images // 2,),
        out_shape=out_shape,
        in_specs=[
            pl.BlockSpec((16, width), lambda i: (i, 0)),
            pl.BlockSpec((2, count, width), lambda i: (i, 0, 0)),
            pl.BlockSpec((16, count), lambda i: (i, 0)),
        ],
        out_specs=out_specs,
        compiler_params=pltpu.CompilerParams(vmem_limit_bytes=16 * 2**20),
        cost_estimate=pl.CostEstimate(flops=64 * big.size, bytes_accessed=2 * big.size, transcendentals=0),
        name="dispatch_grad" if over_tokens else "combine_grad",
    )(rows, big, weight)


def lines_kernel(grads, table, out):
    total, count = grads.shape
    near = total // 8
    c = lax.broadcasted_iota(jnp.int32, (total, near), 0)
    q = lax.broadcasted_iota(jnp.int32, (total, near), 1)
    fold = ((c // 64 == q // 8) & (c % 8 == q % 8)).astype(BF16)
    x = nt(pick_rows(count), grads[...])
    parts = []
    for side in range(2):
        y = jnp.concatenate([x[16 * side : 16 * side + 16]] * 8, axis=0)
        row = lax.broadcasted_iota(jnp.int32, y.shape, 0)
        col = lax.broadcasted_iota(jnp.int32, y.shape, 1)
        y = jnp.where((col // 8) % 8 == row // 16, y, 0.0).astype(BF16)
        parts.append(jnp.dot(y, fold, preferred_element_type=F32).astype(BF16))
    lines = jnp.concatenate(parts, axis=0)
    out[...] = jnp.dot(lines, table[:near], preferred_element_type=F32)


def lines_call(line, table):
    vmem = pl.BlockSpec(memory_space=pltpu.VMEM)
    return pl.pallas_call(
        lines_kernel,
        out_shape=jax.ShapeDtypeStruct((256, table.shape[1]), F32),
        in_specs=[vmem] * 2,
        out_specs=vmem,
        compiler_params=pltpu.CompilerParams(vmem_limit_bytes=24 * 2**20),
        name="through_logits",
    )(line, table)


def spread_kernel(spread, pair, one, two, three, base, mine, theirs):
    half = mine.shape[0]
    side = spread[...].reshape(2 * half, spread.shape[2])
    depth = side.shape[1] // 4
    total = base[...]
    for x, piece in enumerate((pair, one, two, three)):
        block = piece[...].reshape(depth, piece.shape[2])
        total = total + jnp.dot(side[:, x * depth : (x + 1) * depth], block, preferred_element_type=F32)
    mine[...] = total[:half]
    theirs[...] = total[half:]


def spread_call(spread, pieces, base):
    vmem = pl.BlockSpec(memory_space=pltpu.VMEM)
    half, width = base.shape[0] // 2, base.shape[1]
    return pl.pallas_call(
        spread_kernel,
        out_shape=[jax.ShapeDtypeStruct((half, width), F32)] * 2,
        in_specs=[vmem] * 6,
        out_specs=[vmem] * 2,
        compiler_params=pltpu.CompilerParams(vmem_limit_bytes=24 * 2**20),
        name="through_slots",
    )(spread, *pieces, base)


def after(value, *earlier):
    return lax.optimization_barrier((value,) + earlier)[0]


def units_of(w_in, w_out):
    z = lax.axis_index("dp") // 4
    quarter = w_in.shape[1] // 4

    def unit(zz):
        start = zz * quarter
        return jnp.stack(
            [
                lax.dynamic_slice_in_dim(w_in, start, quarter, 1),
                lax.dynamic_slice_in_dim(w_out, start, quarter, 1),
            ]
        )

    return [unit(z ^ a) for a in range(4)]


def together(*values):
    return lax.optimization_barrier(values)


def reduce_z(own, *far):
    one, two, three = together(*[swap(v, "dp", 4 * a) for a, v in enumerate(far, 1)])
    return (own + one.astype(F32)) + (two.astype(F32) + three.astype(F32))


def pair_z(own, second, others):
    got = swap(others, "dp", 4)
    return own + got[0].astype(F32), (second + got[1].astype(F32)).astype(BF16)


def all_x(v):
    return [v, *together(swap(v, "expert", 4), swap(v, "expert", 8), swap(v, "expert", 12))]


def doubled(v, axis, *steps):
    for k in steps:
        v = jnp.concatenate([v, swap(v, axis, k)], axis=0)
    return v


def summed(v, axis, *steps):
    for k in steps:
        v = v + swap(v, axis, k)
    return v


def summed_three(v, axis, *steps):
    one, two, three = together(*[swap(v, axis, k) for k in steps])
    return (v + one) + (two + three)


def per_device(tokens, out_grad, slot_params, w_in, w_out):
    images, count, width = tokens.shape
    own = slot_params.shape[1]
    half = images * own

    units = units_of(w_in, w_out.T)
    table = doubled(slot_params.T, "expert", 2)
    u1 = swap(units[1], "dp", 4)
    u2 = swap(units[2], "dp", 8)
    l0, r0 = swap(units[0], "dp", 1), swap(units[0], "dp", 3)
    p0, q0 = swap(r0[0], "dp", 1), swap(l0[1], "dp", 3)

    u1, u2, p0, q0, table = together(u1, u2, p0, q0, table)
    both = jnp.stack([u1, u2], axis=1)
    lb, rb = swap(both, "dp", 1), swap(both, "dp", 3)
    u3 = swap(after(units[3], u1), "dp", 12)
    table = doubled(table, "expert", 4, 8, 1)
    rows, dispatch, combine, spread = slots_call(table, tokens, out_grad)
    rows = rows.reshape(2 * half, width)

    lb, rb, u3, rows = together(lb, rb, u3, rows)
    z1, z2 = swap(rows, "dp", 4), swap(rows, "dp", 8)
    l3, r3 = swap(u3, "dp", 1), swap(u3, "dp", 3)
    pb, qb = swap(rb[0], "dp", 1), swap(lb[1], "dp", 3)
    l3, r3, z1, z2 = together(l3, r3, z1, z2)
    p3, q3 = swap(r3[0], "dp", 1), swap(l3[1], "dp", 3)
    z3 = swap(z2, "dp", 4)
    pb, qb, p3, q3, z3 = together(pb, qb, p3, q3, z3)
    rows_in = jnp.concatenate([v[:half] for v in (rows, z1, z2, z3)], axis=0)
    rows_go = jnp.concatenate([v[half:] for v in (rows, z1, z2, z3)], axis=0)

    blocks = [units[0], l0, r0, p0, q0, both, lb, rb, pb, qb, u3, l3, r3, p3, q3]
    halves = ffn(rows_in, rows_go, blocks, half)
    slot_out = reduce_z(*halves[:4])
    first, second = pair_z(*halves[4:])
    slot_in_grad = first + swap(second, "dp", 8).astype(F32)
    near = slot_in_grad.astype(BF16)
    far = swap(near, "expert", 2)

    part, mix = against(after(slot_out, second), out_grad, combine, False)
    mix = summed_three(mix, "expert", 1, 2, 3)
    mix = summed_three(after(mix, near), "expert", 4, 8, 12)
    (back,) = against(slot_in_grad, tokens, dispatch, True)
    logit_grad = back + (part - combine * jnp.repeat(mix, own, axis=0))
    logit_grad_b = logit_grad.astype(BF16)
    term = jnp.einsum(
        "bsm,bmd->sd", logit_grad_b.reshape(images, own, count), tokens, preferred_element_type=F32
    )

    line = doubled(logit_grad_b, "expert", 2)
    line, far = together(line, far)
    term = summed(term, "dp", 4)
    *line, term, far = together(*all_x(line), term, far)
    pieces = all_x(jnp.stack([near, far]))
    base = lines_call(jnp.concatenate(line, axis=0), table)
    term = summed(term, "dp", 8, 1)
    slot_grad = summed(after(term, *pieces), "dp", 2).T

    mine, theirs = spread_call(spread, pieces, after(base, term))
    token_grad = (mine + swap(theirs, "expert", 1)).astype(BF16)
    return (token_grad.reshape(images, -1, width), slot_grad)


def solution(mesh):
    return jax.shard_map(
        per_device,
        mesh=mesh,
        in_specs=(
            P("dp", None, None),
            P("dp", None, None),
            P(None, "expert"),
            P("dp", "expert"),
            P("expert", "dp"),
        ),
        out_specs=(P("dp", "expert", None), P(None, "expert")),
        check_vma=False,
    )
```

```python
import math
import jax
import jax.numpy as jnp
from jax import lax
from jax.experimental import pallas as pl
from jax.experimental.pallas import tpu as pltpu
from jax.sharding import PartitionSpec as P

F32 = jnp.float32
BF16 = jnp.bfloat16
ROOT = math.sqrt(2.0 / math.pi)


def swap(value, axis, k):
    count = lax.axis_size(axis)
    return lax.ppermute(value, axis, [(i, i ^ k) for i in range(count)])


def nt(a, b):
    return lax.dot_general(a, b, (((1,), (1,)), ((), ())), preferred_element_type=F32)


def ffn_kernel(rows_in, rows_go, *refs):
    own, l0, r0, p0, q0, both, lb, rb, pb, qb, last, l3, r3, p3, q3 = refs[:15]
    f0, f3 = (p0, q0), (p3, q3)
    outs, grads, (w1, w2) = refs[15:19], refs[19:23], refs[23:]
    me = lax.axis_index("dp")
    depth = w1.shape[0] // 16

    def place(which, dst):
        for a, sources in (
            (0, (own.at[which], l0.at[which], f0[which], r0.at[which])),
            (3, (last.at[which], l3.at[which], f3[which], r3.at[which])),
            (1, (both.at[which, 0], lb.at[which, 0], (pb, qb)[which].at[0], rb.at[which, 0])),
            (2, (both.at[which, 1], lb.at[which, 1], (pb, qb)[which].at[1], rb.at[which, 1])),
        ):
            for b, src in enumerate(sources):
                start = pl.multiple_of((me ^ (4 * a + b)) * depth, 16)
                dst[pl.ds(start, depth), :] = src[...]

    place(0, w1)
    place(1, w2)
    pre = jnp.dot(rows_in[...], w1[...], preferred_element_type=F32)
    sq = pre * pre
    th = jnp.tanh(ROOT * (pre + 0.044715 * (sq * pre)))
    cdf = 0.5 * (1.0 + th)
    hidden = (pre * cdf).astype(BF16)
    slope = cdf + 0.5 * pre * (1.0 - th * th) * (ROOT * (1.0 + 3 * 0.044715 * sq))
    hidden_grad = jnp.dot(rows_go[...], w2[...], preferred_element_type=F32)
    pre_grad = (hidden_grad * slope).astype(BF16)
    rows = outs[0].shape[0]
    for whole, blocks in ((nt(hidden, w2[...]), outs), (nt(pre_grad, w1[...]), grads)):
        for a, block in enumerate(blocks):
            block[...] = whole[a * rows : (a + 1) * rows].astype(block.dtype)


def ffn(rows_in, rows_go, blocks, own_rows):
    rows, width = rows_in.shape
    quarter = blocks[0].shape[2]
    vmem = pl.BlockSpec(memory_space=pltpu.VMEM)
    return pl.pallas_call(
        ffn_kernel,
        out_shape=[jax.ShapeDtypeStruct((own_rows, width), t) for t in (F32, BF16, BF16, BF16)] * 2,
        in_specs=[vmem] * (2 + len(blocks)),
        out_specs=[vmem] * 8,
        scratch_shapes=[pltpu.VMEM((width, quarter), BF16), pltpu.VMEM((width, quarter), BF16)],
        compiler_params=pltpu.CompilerParams(vmem_limit_bytes=40 * 2**20),
        name="ffn",
    )(rows_in, rows_go, *blocks)


def pick_rows(count):
    col = lax.broadcasted_iota(jnp.int32, (32, count), 1)
    row = lax.broadcasted_iota(jnp.int32, (32, count), 0)
    owner = lax.axis_index("expert") ^ (row // 16)
    return (col == owner * 16 + row % 16).astype(BF16)


def slots_kernel(table, tokens, out_grad, rows, dispatch_own, combine_own, spread):
    step = pl.program_id(0)
    own = 8
    near = table.shape[0] // 2
    count = tokens.shape[1]
    pick = pick_rows(count)
    ins, gos, disp, comb, mine, theirs = [], [], [], [], [], []
    for i in range(2):
        logits = nt(table[...], tokens[i])
        up = jnp.exp(logits[:near] - jnp.max(logits[:near], axis=1, keepdims=True))
        dispatch = up / jnp.sum(up, axis=1, keepdims=True)
        down = jnp.exp(logits - jnp.max(logits, axis=0, keepdims=True))
        combine = down[:own] / jnp.sum(down, axis=0, keepdims=True)
        dispatch_b = dispatch.astype(BF16)
        ins.append(jnp.dot(dispatch_b[:16], tokens[i], preferred_element_type=F32)[:own])
        both = jnp.concatenate([combine, combine], axis=0).astype(BF16)
        gos.append(jnp.dot(both, out_grad[i], preferred_element_type=F32)[:own])
        disp.append(dispatch[:own])
        comb.append(combine)
        lines = nt(pick, dispatch_b).astype(BF16)
        image = 2 * step + i
        q = lax.broadcasted_iota(jnp.int32, (near, 8 * near), 0)
        col = lax.broadcasted_iota(jnp.int32, (near, 8 * near), 1)
        wide = (col == (q // 8) * 64 + q % 8 + image * 8).astype(BF16)
        lines = jnp.dot(lines, wide, preferred_element_type=F32)
        mine.append(lines[:16])
        theirs.append(lines[16:])
    rows[0] = jnp.concatenate(ins, axis=0).astype(BF16)
    rows[1] = jnp.concatenate(gos, axis=0).astype(BF16)
    dispatch_own[...] = jnp.concatenate(disp, axis=0)
    combine_own[...] = jnp.concatenate(comb, axis=0)
    spread[0] = jnp.concatenate(mine, axis=0).astype(BF16)
    spread[1] = jnp.concatenate(theirs, axis=0).astype(BF16)


def slots_call(table, tokens, out_grad):
    images, count, width = tokens.shape
    slots = table.shape[0]
    return pl.pallas_call(
        slots_kernel,
        grid=(images // 2,),
        out_shape=[
            jax.ShapeDtypeStruct((2, images * 8, width), BF16),
            jax.ShapeDtypeStruct((images * 8, count), F32),
            jax.ShapeDtypeStruct((images * 8, count), F32),
            jax.ShapeDtypeStruct((2, images * 16, slots * 4), BF16),
        ],
        in_specs=[
            pl.BlockSpec((slots, width), lambda i: (0, 0)),
            pl.BlockSpec((2, count, width), lambda i: (i, 0, 0)),
            pl.BlockSpec((2, count, width), lambda i: (i, 0, 0)),
        ],
        out_specs=[
            pl.BlockSpec((2, 16, width), lambda i: (0, i, 0)),
            pl.BlockSpec((16, count), lambda i: (i, 0)),
            pl.BlockSpec((16, count), lambda i: (i, 0)),
            pl.BlockSpec((2, 32, slots * 4), lambda i: (0, i, 0)),
        ],
        compiler_params=pltpu.CompilerParams(vmem_limit_bytes=24 * 2**20),
        cost_estimate=pl.CostEstimate(
            flops=2 * tokens.size * (slots + 32), bytes_accessed=4 * tokens.size, transcendentals=2 * images * slots * count
        ),
        name="slots",
    )(table, tokens, out_grad)


def against_kernel(over_tokens, rows, big, weight, *outs):
    value = rows[...]
    high = value.astype(BF16)
    low = (value - high.astype(F32)).astype(BF16)
    both = jnp.concatenate([high, low], axis=0)
    prods = []
    for i in range(2):
        prod = nt(both, big[i])
        prods.append(prod[8 * i : 8 * i + 8] + prod[16 + 8 * i : 24 + 8 * i])
    prod = jnp.concatenate(prods, axis=0)
    w = weight[...]
    part = w * prod
    if over_tokens:
        outs[0][...] = w * (prod - jnp.sum(part, axis=1, keepdims=True))
    else:
        outs[0][...] = part
        step = pl.program_id(0)
        for i in range(2):
            outs[1][pl.ds(2 * step + i, 1), :] = jnp.sum(part[8 * i : 8 * i + 8], axis=0, keepdims=True)


def against(rows, big, weight, over_tokens):
    images, count, width = big.shape
    total = images * 8
    out_shape = [jax.ShapeDtypeStruct((total, count), F32)]
    out_specs = [pl.BlockSpec((16, count), lambda i: (i, 0))]
    if not over_tokens:
        out_shape.append(jax.ShapeDtypeStruct((images, count), F32))
        out_specs.append(pl.BlockSpec((images, count), lambda i: (0, 0)))
    return pl.pallas_call(
        lambda *refs: against_kernel(over_tokens, *refs),
        grid=(images // 2,),
        out_shape=out_shape,
        in_specs=[
            pl.BlockSpec((16, width), lambda i: (i, 0)),
            pl.BlockSpec((2, count, width), lambda i: (i, 0, 0)),
            pl.BlockSpec((16, count), lambda i: (i, 0)),
        ],
        out_specs=out_specs,
        compiler_params=pltpu.CompilerParams(vmem_limit_bytes=16 * 2**20),
        cost_estimate=pl.CostEstimate(flops=2048 * big.size, bytes_accessed=2 * big.size, transcendentals=0),
        name="dispatch_grad" if over_tokens else "combine_grad",
    )(rows, big, weight)


def tokens_kernel(spread, pair, one, two, three, table, mine, theirs):
    half, width = mine.shape
    pieces = [ref[...].reshape(2 * ref.shape[1], ref.shape[2]) for ref in (pair, one, two, three)]
    depth = pieces[0].shape[0]
    count = pieces[0].shape[1] - width
    grads = jnp.concatenate([piece[:, width:] for piece in pieces], axis=0)
    total = grads.shape[0]
    near = total // 8
    c = lax.broadcasted_iota(jnp.int32, (total, near), 0)
    q = lax.broadcasted_iota(jnp.int32, (total, near), 1)
    fold = ((c // 64 == q // 8) & (c % 8 == q % 8)).astype(BF16)
    x = nt(pick_rows(count), grads)
    parts = []
    for side in range(2):
        y = jnp.concatenate([x[16 * side : 16 * side + 16]] * 8, axis=0)
        row = lax.broadcasted_iota(jnp.int32, y.shape, 0)
        col = lax.broadcasted_iota(jnp.int32, y.shape, 1)
        y = jnp.where((col // 8) % 8 == row // 16, y, 0.0).astype(BF16)
        parts.append(jnp.dot(y, fold, preferred_element_type=F32).astype(BF16))
    sums = jnp.dot(jnp.concatenate(parts, axis=0), table[:near], preferred_element_type=F32)
    side = spread[...].reshape(2 * half, spread.shape[2])
    for x, piece in enumerate(pieces):
        sums = sums + jnp.dot(side[:, x * depth : (x + 1) * depth], piece[:, :width], preferred_element_type=F32)
    mine[...] = sums[:half]
    theirs[...] = sums[half:]


def tokens_call(spread, pieces, table):
    vmem = pl.BlockSpec(memory_space=pltpu.VMEM)
    half, width = spread.shape[1], table.shape[1]
    return pl.pallas_call(
        tokens_kernel,
        out_shape=[jax.ShapeDtypeStruct((half, width), F32)] * 2,
        in_specs=[vmem] * 6,
        out_specs=[vmem] * 2,
        compiler_params=pltpu.CompilerParams(vmem_limit_bytes=24 * 2**20),
        name="token_grad",
    )(spread, *pieces, table)


def after(value, *earlier):
    return lax.optimization_barrier((value,) + earlier)[0]


def units_of(w_in, w_out):
    z = lax.axis_index("dp") // 4
    quarter = w_in.shape[1] // 4

    def unit(zz):
        start = zz * quarter
        return jnp.stack(
            [
                lax.dynamic_slice_in_dim(w_in, start, quarter, 1),
                lax.dynamic_slice_in_dim(w_out, start, quarter, 1),
            ]
        )

    return [unit(z ^ a) for a in range(4)]


def together(*values):
    return lax.optimization_barrier(values)


def reduce_z(own, *far):
    one, two, three = together(*[swap(v, "dp", 4 * a) for a, v in enumerate(far, 1)])
    return (own + one.astype(F32)) + (two.astype(F32) + three.astype(F32))


def all_x(v):
    return [v, *together(swap(v, "expert", 4), swap(v, "expert", 8), swap(v, "expert", 12))]


def doubled(v, axis, *steps):
    for k in steps:
        v = jnp.concatenate([v, swap(v, axis, k)], axis=0)
    return v


def summed(v, axis, *steps):
    for k in steps:
        v = v + swap(v, axis, k)
    return v


def summed_three(v, axis, *steps):
    one, two, three = together(*[swap(v, axis, k) for k in steps])
    return (v + one) + (two + three)


def per_device(tokens, out_grad, slot_params, w_in, w_out):
    images, count, width = tokens.shape
    own = slot_params.shape[1]
    half = images * own

    units = units_of(w_in, w_out.T)
    l0, r0 = swap(units[0], "dp", 1), swap(units[0], "dp", 3)
    u1 = swap(units[1], "dp", 4)
    u2 = swap(units[2], "dp", 8)
    l0, r0, u1 = together(l0, r0, u1)
    p0, q0 = swap(r0[0], "dp", 1), swap(l0[1], "dp", 3)
    table = doubled(after(slot_params.T, u1), "expert", 2)

    u1, u2, p0, q0, table = together(u1, u2, p0, q0, table)
    both = jnp.stack([u1, u2], axis=1)
    lb, rb = swap(both, "dp", 1), swap(both, "dp", 3)
    u3 = swap(after(units[3], u1), "dp", 12)
    table = doubled(table, "expert", 4, 8, 1)
    rows, dispatch, combine, spread = slots_call(table, tokens, out_grad)
    rows = rows.reshape(2 * half, width)

    lb, rb, u3, rows = together(lb, rb, u3, rows)
    z1, z2 = swap(rows, "dp", 4), swap(rows, "dp", 8)
    l3, r3 = swap(u3, "dp", 1), swap(u3, "dp", 3)
    pb, qb = swap(rb[0], "dp", 1), swap(lb[1], "dp", 3)
    l3, r3, z1, z2 = together(l3, r3, z1, z2)
    p3, q3 = swap(r3[0], "dp", 1), swap(l3[1], "dp", 3)
    z3 = swap(z2, "dp", 4)
    pb, qb, p3, q3, z3 = together(pb, qb, p3, q3, z3)
    rows_in = jnp.concatenate([v[:half] for v in (rows, z1, z2, z3)], axis=0)
    rows_go = jnp.concatenate([v[half:] for v in (rows, z1, z2, z3)], axis=0)

    blocks = [units[0], l0, r0, p0, q0, both, lb, rb, pb, qb, u3, l3, r3, p3, q3]
    halves = ffn(rows_in, rows_go, blocks, half)
    slot_out = reduce_z(*halves[:4])
    slot_in_grad = reduce_z(*halves[4:])
    part, mix = against(slot_out, out_grad, combine, False)
    mix = summed_three(mix, "expert", 1, 2, 3)
    mix = summed_three(after(mix, slot_in_grad), "expert", 4, 8, 12)
    (back,) = against(slot_in_grad, tokens, dispatch, True)
    logit_grad = back + (part - combine * jnp.repeat(mix, own, axis=0))
    logit_grad_b = logit_grad.astype(BF16)

    near = jnp.concatenate([slot_in_grad.astype(BF16), logit_grad_b], axis=1)
    far = swap(near, "expert", 2)
    term = jnp.einsum(
        "bsm,bmd->sd", logit_grad_b.reshape(images, own, count), tokens, preferred_element_type=F32
    )
    term = summed(term, "dp", 4)
    term, far = together(term, far)
    pieces = all_x(jnp.stack([near, far]))
    term = summed(term, "dp", 8, 1)
    slot_grad = summed(after(term, *pieces), "dp", 2).T

    pieces[1] = after(pieces[1], term)
    mine, theirs = tokens_call(spread, pieces, table)
    token_grad = (mine + swap(theirs, "expert", 1)).astype(BF16)
    return (token_grad.reshape(images, -1, width), slot_grad)


def solution(mesh):
    return jax.shard_map(
        per_device,
        mesh=mesh,
        in_specs=(
            P("dp", None, None),
            P("dp", None, None),
            P(None, "expert"),
            P("dp", "expert"),
            P("expert", "dp"),
        ),
        out_specs=(P("dp", "expert", None), P(None, "expert")),
        check_vma=False,
    )
```

```python
import math
import jax
import jax.numpy as jnp
from jax import lax
from jax.experimental import pallas as pl
from jax.experimental.pallas import tpu as pltpu
from jax.sharding import PartitionSpec as P

F32 = jnp.float32
BF16 = jnp.bfloat16
ROOT = math.sqrt(2.0 / math.pi)


def swap(value, axis, k):
    count = lax.axis_size(axis)
    return lax.ppermute(value, axis, [(i, i ^ k) for i in range(count)])


def nt(a, b):
    return lax.dot_general(a, b, (((1,), (1,)), ((), ())), preferred_element_type=F32)


def ffn_kernel(rows_in, rows_go, *refs):
    own, l0, r0, p0, q0, both, lb, rb, pb, qb, last, l3, r3, p3, q3 = refs[:15]
    f0, f3 = (p0, q0), (p3, q3)
    outs, grads, (w1, w2) = refs[15:19], refs[19:23], refs[23:]
    me = lax.axis_index("dp")
    depth = w1.shape[0] // 16

    def place(which, dst):
        for a, sources in (
            (0, (own.at[which], l0.at[which], f0[which], r0.at[which])),
            (3, (last.at[which], l3.at[which], f3[which], r3.at[which])),
            (1, (both.at[which, 0], lb.at[which, 0], (pb, qb)[which].at[0], rb.at[which, 0])),
            (2, (both.at[which, 1], lb.at[which, 1], (pb, qb)[which].at[1], rb.at[which, 1])),
        ):
            for b, src in enumerate(sources):
                start = pl.multiple_of((me ^ (4 * a + b)) * depth, 16)
                dst[pl.ds(start, depth), :] = src[...]

    place(0, w1)
    place(1, w2)
    pre = jnp.dot(rows_in[...], w1[...], preferred_element_type=F32)
    sq = pre * pre
    th = jnp.tanh(ROOT * (pre + 0.044715 * (sq * pre)))
    cdf = 0.5 * (1.0 + th)
    hidden = (pre * cdf).astype(BF16)
    slope = cdf + 0.5 * pre * (1.0 - th * th) * (ROOT * (1.0 + 3 * 0.044715 * sq))
    hidden_grad = jnp.dot(rows_go[...], w2[...], preferred_element_type=F32)
    pre_grad = (hidden_grad * slope).astype(BF16)
    rows = outs[0].shape[0]
    for whole, blocks in ((nt(hidden, w2[...]), outs), (nt(pre_grad, w1[...]), grads)):
        for a, block in enumerate(blocks):
            block[...] = whole[a * rows : (a + 1) * rows].astype(block.dtype)


def ffn(rows_in, rows_go, blocks, own_rows):
    rows, width = rows_in.shape
    quarter = blocks[0].shape[2]
    vmem = pl.BlockSpec(memory_space=pltpu.VMEM)
    return pl.pallas_call(
        ffn_kernel,
        out_shape=[jax.ShapeDtypeStruct((own_rows, width), t) for t in (F32, BF16, BF16, BF16)] * 2,
        in_specs=[vmem] * (2 + len(blocks)),
        out_specs=[vmem] * 8,
        scratch_shapes=[pltpu.VMEM((width, quarter), BF16), pltpu.VMEM((width, quarter), BF16)],
        compiler_params=pltpu.CompilerParams(vmem_limit_bytes=40 * 2**20),
        name="ffn",
    )(rows_in, rows_go, *blocks)


def pick_rows(count):
    col = lax.broadcasted_iota(jnp.int32, (32, count), 1)
    row = lax.broadcasted_iota(jnp.int32, (32, count), 0)
    owner = lax.axis_index("expert") ^ (row // 16)
    return (col == owner * 16 + row % 16).astype(BF16)


def slots_kernel(table, tokens, out_grad, rows, dispatch_own, combine_own, spread):
    step = pl.program_id(0)
    own = 8
    near = table.shape[0] // 2
    count = tokens.shape[1]
    pick = pick_rows(count)
    ins, gos, disp, comb, mine, theirs = [], [], [], [], [], []
    for i in range(2):
        logits = nt(table[...], tokens[i])
        up = jnp.exp(logits[:near] - jnp.max(logits[:near], axis=1, keepdims=True))
        dispatch = up / jnp.sum(up, axis=1, keepdims=True)
        down = jnp.exp(logits - jnp.max(logits, axis=0, keepdims=True))
        combine = down[:own] / jnp.sum(down, axis=0, keepdims=True)
        dispatch_b = dispatch.astype(BF16)
        ins.append(jnp.dot(dispatch_b[:16], tokens[i], preferred_element_type=F32)[:own])
        both = jnp.concatenate([combine, combine], axis=0).astype(BF16)
        gos.append(jnp.dot(both, out_grad[i], preferred_element_type=F32)[:own])
        disp.append(dispatch[:own])
        comb.append(combine)
        lines = nt(pick, dispatch_b).astype(BF16)
        image = 2 * step + i
        q = lax.broadcasted_iota(jnp.int32, (near, 8 * near), 0)
        col = lax.broadcasted_iota(jnp.int32, (near, 8 * near), 1)
        wide = (col == (q // 8) * 64 + q % 8 + image * 8).astype(BF16)
        lines = jnp.dot(lines, wide, preferred_element_type=F32)
        mine.append(lines[:16])
        theirs.append(lines[16:])
    rows[0] = jnp.concatenate(ins, axis=0).astype(BF16)
    rows[1] = jnp.concatenate(gos, axis=0).astype(BF16)
    dispatch_own[...] = jnp.concatenate(disp, axis=0)
    combine_own[...] = jnp.concatenate(comb, axis=0)
    spread[0] = jnp.concatenate(mine, axis=0).astype(BF16)
    spread[1] = jnp.concatenate(theirs, axis=0).astype(BF16)


def slots_call(table, tokens, out_grad):
    images, count, width = tokens.shape
    slots = table.shape[0]
    return pl.pallas_call(
        slots_kernel,
        grid=(images // 2,),
        out_shape=[
            jax.ShapeDtypeStruct((2, images * 8, width), BF16),
            jax.ShapeDtypeStruct((images * 8, count), F32),
            jax.ShapeDtypeStruct((images * 8, count), F32),
            jax.ShapeDtypeStruct((2, images * 16, slots * 4), BF16),
        ],
        in_specs=[
            pl.BlockSpec((slots, width), lambda i: (0, 0)),
            pl.BlockSpec((2, count, width), lambda i: (i, 0, 0)),
            pl.BlockSpec((2, count, width), lambda i: (i, 0, 0)),
        ],
        out_specs=[
            pl.BlockSpec((2, 16, width), lambda i: (0, i, 0)),
            pl.BlockSpec((16, count), lambda i: (i, 0)),
            pl.BlockSpec((16, count), lambda i: (i, 0)),
            pl.BlockSpec((2, 32, slots * 4), lambda i: (0, i, 0)),
        ],
        compiler_params=pltpu.CompilerParams(vmem_limit_bytes=24 * 2**20),
        cost_estimate=pl.CostEstimate(
            flops=2 * tokens.size * (slots + 32), bytes_accessed=4 * tokens.size, transcendentals=2 * images * slots * count
        ),
        name="slots",
    )(table, tokens, out_grad)


def against_kernel(over_tokens, rows, big, weight, *outs):
    value = rows[...]
    high = value.astype(BF16)
    low = (value - high.astype(F32)).astype(BF16)
    both = jnp.concatenate([high, low], axis=0)
    prods = []
    for i in range(2):
        prod = nt(both, big[i])
        prods.append(prod[8 * i : 8 * i + 8] + prod[16 + 8 * i : 24 + 8 * i])
    prod = jnp.concatenate(prods, axis=0)
    w = weight[...]
    part = w * prod
    if over_tokens:
        outs[0][...] = w * (prod - jnp.sum(part, axis=1, keepdims=True))
    else:
        outs[0][...] = part
        step = pl.program_id(0)
        for i in range(2):
            outs[1][pl.ds(2 * step + i, 1), :] = jnp.sum(part[8 * i : 8 * i + 8], axis=0, keepdims=True)


def against(rows, big, weight, over_tokens):
    images, count, width = big.shape
    total = images * 8
    out_shape = [jax.ShapeDtypeStruct((total, count), F32)]
    out_specs = [pl.BlockSpec((16, count), lambda i: (i, 0))]
    if not over_tokens:
        out_shape.append(jax.ShapeDtypeStruct((images, count), F32))
        out_specs.append(pl.BlockSpec((images, count), lambda i: (0, 0)))
    return pl.pallas_call(
        lambda *refs: against_kernel(over_tokens, *refs),
        grid=(images // 2,),
        out_shape=out_shape,
        in_specs=[
            pl.BlockSpec((16, width), lambda i: (i, 0)),
            pl.BlockSpec((2, count, width), lambda i: (i, 0, 0)),
            pl.BlockSpec((16, count), lambda i: (i, 0)),
        ],
        out_specs=out_specs,
        compiler_params=pltpu.CompilerParams(vmem_limit_bytes=16 * 2**20),
        cost_estimate=pl.CostEstimate(flops=2048 * big.size, bytes_accessed=2 * big.size, transcendentals=0),
        name="dispatch_grad" if over_tokens else "combine_grad",
    )(rows, big, weight)


def tokens_kernel(spread, pair, one, two, three, table, mine, theirs):
    half, width = mine.shape
    pieces = [ref[...].reshape(2 * ref.shape[1], ref.shape[2]) for ref in (pair, one, two, three)]
    depth = pieces[0].shape[0]
    count = pieces[0].shape[1] - width
    grads = jnp.concatenate([piece[:, width:] for piece in pieces], axis=0)
    total = grads.shape[0]
    near = total // 8
    c = lax.broadcasted_iota(jnp.int32, (total, near), 0)
    q = lax.broadcasted_iota(jnp.int32, (total, near), 1)
    fold = ((c // 64 == q // 8) & (c % 8 == q % 8)).astype(BF16)
    x = nt(pick_rows(count), grads)
    parts = []
    for side in range(2):
        y = jnp.concatenate([x[16 * side : 16 * side + 16]] * 8, axis=0)
        row = lax.broadcasted_iota(jnp.int32, y.shape, 0)
        col = lax.broadcasted_iota(jnp.int32, y.shape, 1)
        y = jnp.where((col // 8) % 8 == row // 16, y, 0.0).astype(BF16)
        parts.append(jnp.dot(y, fold, preferred_element_type=F32).astype(BF16))
    sums = jnp.dot(jnp.concatenate(parts, axis=0), table[:near], preferred_element_type=F32)
    side = spread[...].reshape(2 * half, spread.shape[2])
    for x, piece in enumerate(pieces):
        sums = sums + jnp.dot(side[:, x * depth : (x + 1) * depth], piece[:, :width], preferred_element_type=F32)
    mine[...] = sums[:half]
    theirs[...] = sums[half:]


def tokens_call(spread, pieces, table):
    vmem = pl.BlockSpec(memory_space=pltpu.VMEM)
    half, width = spread.shape[1], table.shape[1]
    return pl.pallas_call(
        tokens_kernel,
        out_shape=[jax.ShapeDtypeStruct((half, width), F32)] * 2,
        in_specs=[vmem] * 6,
        out_specs=[vmem] * 2,
        compiler_params=pltpu.CompilerParams(vmem_limit_bytes=24 * 2**20),
        name="token_grad",
    )(spread, *pieces, table)


def after(value, *earlier):
    return lax.optimization_barrier((value,) + earlier)[0]


def units_of(w_in, w_out):
    z = lax.axis_index("dp") // 4
    quarter = w_in.shape[1] // 4

    def unit(zz):
        start = zz * quarter
        return jnp.stack(
            [
                lax.dynamic_slice_in_dim(w_in, start, quarter, 1),
                lax.dynamic_slice_in_dim(w_out, start, quarter, 1),
            ]
        )

    return [unit(z ^ a) for a in range(4)]


def together(*values):
    return lax.optimization_barrier(values)


def reduce_z(own, *far):
    one, two, three = together(*[swap(v, "dp", 4 * a) for a, v in enumerate(far, 1)])
    return (own + one.astype(F32)) + (two.astype(F32) + three.astype(F32))


def all_x(v):
    return [v, *together(swap(v, "expert", 4), swap(v, "expert", 8), swap(v, "expert", 12))]


def doubled(v, axis, *steps):
    for k in steps:
        v = jnp.concatenate([v, swap(v, axis, k)], axis=0)
    return v


def summed(v, axis, *steps):
    for k in steps:
        v = v + swap(v, axis, k)
    return v


def summed_three(v, axis, *steps):
    one, two, three = together(*[swap(v, axis, k) for k in steps])
    return (v + one) + (two + three)


def per_device(tokens, out_grad, slot_params, w_in, w_out):
    images, count, width = tokens.shape
    own = slot_params.shape[1]
    half = images * own

    units = units_of(w_in, w_out.T)
    l0, r0 = swap(units[0], "dp", 1), swap(units[0], "dp", 3)
    u1 = swap(units[1], "dp", 4)
    u2 = swap(units[2], "dp", 8)
    table = doubled(slot_params.T, "expert", 2, 4)
    l0, r0, table = together(l0, r0, table)
    p0, q0 = swap(r0[0], "dp", 1), swap(l0[1], "dp", 3)
    table = doubled(table, "expert", 8, 1)

    u1, u2, p0, q0, table = together(u1, u2, p0, q0, table)
    both = jnp.stack([u1, u2], axis=1)
    lb, rb = swap(both, "dp", 1), swap(both, "dp", 3)
    u3 = swap(after(units[3], u1), "dp", 12)
    rows, dispatch, combine, spread = slots_call(table, tokens, out_grad)
    rows = rows.reshape(2 * half, width)

    lb, rb, u3, rows = together(lb, rb, u3, rows)
    z1, z2 = swap(rows, "dp", 4), swap(rows, "dp", 8)
    l3, r3 = swap(u3, "dp", 1), swap(u3, "dp", 3)
    pb, qb = swap(rb[0], "dp", 1), swap(lb[1], "dp", 3)
    l3, r3, z2 = together(l3, r3, z2)
    p3, q3 = swap(r3[0], "dp", 1), swap(l3[1], "dp", 3)
    z3 = swap(z2, "dp", 4)
    pb, qb, p3, q3, z3 = together(pb, qb, p3, q3, z3)
    rows_in = jnp.concatenate([v[:half] for v in (rows, z1, z2, z3)], axis=0)
    rows_go = jnp.concatenate([v[half:] for v in (rows, z1, z2, z3)], axis=0)

    blocks = [units[0], l0, r0, p0, q0, both, lb, rb, pb, qb, u3, l3, r3, p3, q3]
    halves = ffn(rows_in, rows_go, blocks, half)
    slot_out = reduce_z(*halves[:4])
    slot_in_grad = reduce_z(*halves[4:])
    part, mix = against(slot_out, out_grad, combine, False)
    mix = summed_three(mix, "expert", 1, 2, 3)
    mix = summed_three(mix, "expert", 4, 8, 12)
    (back,) = against(slot_in_grad, tokens, dispatch, True)
    logit_grad = back + (part - combine * jnp.repeat(mix, own, axis=0))
    logit_grad_b = logit_grad.astype(BF16)

    near = jnp.concatenate([slot_in_grad.astype(BF16), logit_grad_b], axis=1)
    far = swap(near, "expert", 2)
    term = jnp.einsum(
        "bsm,bmd->sd", logit_grad_b.reshape(images, own, count), tokens, preferred_element_type=F32
    )
    term = summed(term, "dp", 4)
    term, far = together(term, far)
    pieces = all_x(jnp.stack([near, far]))
    term = summed(term, "dp", 8, 1, 2)
    slot_grad = term.T

    pieces[1] = after(pieces[1], term)
    mine, theirs = tokens_call(spread, pieces, table)
    token_grad = (mine + swap(theirs, "expert", 1)).astype(BF16)
    return (token_grad.reshape(images, -1, width), slot_grad)


def solution(mesh):
    return jax.shard_map(
        per_device,
        mesh=mesh,
        in_specs=(
            P("dp", None, None),
            P("dp", None, None),
            P(None, "expert"),
            P("dp", "expert"),
            P("expert", "dp"),
        ),
        out_specs=(P("dp", "expert", None), P(None, "expert")),
        check_vma=False,
    )
```

```python
import math
import jax
import jax.numpy as jnp
from jax import lax
from jax.experimental import pallas as pl
from jax.experimental.pallas import tpu as pltpu
from jax.sharding import PartitionSpec as P

F32 = jnp.float32
BF16 = jnp.bfloat16
ROOT = math.sqrt(2.0 / math.pi)


def swap(value, axis, k):
    count = lax.axis_size(axis)
    return lax.ppermute(value, axis, [(i, i ^ k) for i in range(count)])


def nt(a, b):
    return lax.dot_general(a, b, (((1,), (1,)), ((), ())), preferred_element_type=F32)


def ffn_kernel(rows_in, rows_go, *refs):
    own, l0, r0, p0, q0, both, lb, rb, pb, qb, last, l3, r3, p3, q3 = refs[:15]
    f0, f3 = (p0, q0), (p3, q3)
    outs, grads, (w1, w2) = refs[15:19], refs[19:23], refs[23:]
    me = lax.axis_index("dp")
    depth = w1.shape[0] // 16

    def place(which, dst):
        for a, sources in (
            (0, (own.at[which], l0.at[which], f0[which], r0.at[which])),
            (3, (last.at[which], l3.at[which], f3[which], r3.at[which])),
            (1, (both.at[which, 0], lb.at[which, 0], (pb, qb)[which].at[0], rb.at[which, 0])),
            (2, (both.at[which, 1], lb.at[which, 1], (pb, qb)[which].at[1], rb.at[which, 1])),
        ):
            for b, src in enumerate(sources):
                start = pl.multiple_of((me ^ (4 * a + b)) * depth, 16)
                dst[pl.ds(start, depth), :] = src[...]

    place(0, w1)
    place(1, w2)
    pre = jnp.dot(rows_in[...], w1[...], preferred_element_type=F32)
    sq = pre * pre
    th = jnp.tanh(ROOT * (pre + 0.044715 * (sq * pre)))
    cdf = 0.5 * (1.0 + th)
    hidden = (pre * cdf).astype(BF16)
    slope = cdf + 0.5 * pre * (1.0 - th * th) * (ROOT * (1.0 + 3 * 0.044715 * sq))
    hidden_grad = jnp.dot(rows_go[...], w2[...], preferred_element_type=F32)
    pre_grad = (hidden_grad * slope).astype(BF16)
    rows = outs[0].shape[0]
    for whole, blocks in ((nt(hidden, w2[...]), outs), (nt(pre_grad, w1[...]), grads)):
        for a, block in enumerate(blocks):
            block[...] = whole[a * rows : (a + 1) * rows].astype(block.dtype)


def ffn(rows_in, rows_go, blocks, own_rows):
    rows, width = rows_in.shape
    quarter = blocks[0].shape[2]
    vmem = pl.BlockSpec(memory_space=pltpu.VMEM)
    return pl.pallas_call(
        ffn_kernel,
        out_shape=[jax.ShapeDtypeStruct((own_rows, width), t) for t in (F32, BF16, BF16, BF16)] * 2,
        in_specs=[vmem] * (2 + len(blocks)),
        out_specs=[vmem] * 8,
        scratch_shapes=[pltpu.VMEM((width, quarter), BF16), pltpu.VMEM((width, quarter), BF16)],
        compiler_params=pltpu.CompilerParams(vmem_limit_bytes=40 * 2**20),
        name="ffn",
    )(rows_in, rows_go, *blocks)


def pick_rows(count):
    col = lax.broadcasted_iota(jnp.int32, (32, count), 1)
    row = lax.broadcasted_iota(jnp.int32, (32, count), 0)
    owner = lax.axis_index("expert") ^ (row // 16)
    return (col == owner * 16 + row % 16).astype(BF16)


def slots_kernel(table, tokens, out_grad, rows, dispatch_own, combine_own, spread):
    step = pl.program_id(0)
    own = 8
    near = table.shape[0] // 2
    count = tokens.shape[1]
    pick = pick_rows(count)
    ins, gos, disp, comb, mine, theirs = [], [], [], [], [], []
    for i in range(2):
        logits = nt(table[...], tokens[i])
        up = jnp.exp(logits[:near] - jnp.max(logits[:near], axis=1, keepdims=True))
        dispatch = up / jnp.sum(up, axis=1, keepdims=True)
        down = jnp.exp(logits - jnp.max(logits, axis=0, keepdims=True))
        combine = down[:own] / jnp.sum(down, axis=0, keepdims=True)
        dispatch_b = dispatch.astype(BF16)
        ins.append(jnp.dot(dispatch_b[:16], tokens[i], preferred_element_type=F32)[:own])
        both = jnp.concatenate([combine, combine], axis=0).astype(BF16)
        gos.append(jnp.dot(both, out_grad[i], preferred_element_type=F32)[:own])
        disp.append(dispatch[:own])
        comb.append(combine)
        lines = nt(pick, dispatch_b).astype(BF16)
        image = 2 * step + i
        q = lax.broadcasted_iota(jnp.int32, (near, 8 * near), 0)
        col = lax.broadcasted_iota(jnp.int32, (near, 8 * near), 1)
        wide = (col == (q // 8) * 64 + q % 8 + image * 8).astype(BF16)
        lines = jnp.dot(lines, wide, preferred_element_type=F32)
        mine.append(lines[:16])
        theirs.append(lines[16:])
    rows[0] = jnp.concatenate(ins, axis=0).astype(BF16)
    rows[1] = jnp.concatenate(gos, axis=0).astype(BF16)
    dispatch_own[...] = jnp.concatenate(disp, axis=0)
    combine_own[...] = jnp.concatenate(comb, axis=0)
    spread[0] = jnp.concatenate(mine, axis=0).astype(BF16)
    spread[1] = jnp.concatenate(theirs, axis=0).astype(BF16)


def slots_call(table, tokens, out_grad):
    images, count, width = tokens.shape
    slots = table.shape[0]
    return pl.pallas_call(
        slots_kernel,
        grid=(images // 2,),
        out_shape=[
            jax.ShapeDtypeStruct((2, images * 8, width), BF16),
            jax.ShapeDtypeStruct((images * 8, count), F32),
            jax.ShapeDtypeStruct((images * 8, count), F32),
            jax.ShapeDtypeStruct((2, images * 16, slots * 4), BF16),
        ],
        in_specs=[
            pl.BlockSpec((slots, width), lambda i: (0, 0)),
            pl.BlockSpec((2, count, width), lambda i: (i, 0, 0)),
            pl.BlockSpec((2, count, width), lambda i: (i, 0, 0)),
        ],
        out_specs=[
            pl.BlockSpec((2, 16, width), lambda i: (0, i, 0)),
            pl.BlockSpec((16, count), lambda i: (i, 0)),
            pl.BlockSpec((16, count), lambda i: (i, 0)),
            pl.BlockSpec((2, 32, slots * 4), lambda i: (0, i, 0)),
        ],
        compiler_params=pltpu.CompilerParams(vmem_limit_bytes=24 * 2**20),
        cost_estimate=pl.CostEstimate(
            flops=2 * tokens.size * (slots + 32), bytes_accessed=4 * tokens.size, transcendentals=2 * images * slots * count
        ),
        name="slots",
    )(table, tokens, out_grad)


def against_kernel(over_tokens, rows, big, weight, *outs):
    value = rows[...]
    high = value.astype(BF16)
    low = (value - high.astype(F32)).astype(BF16)
    both = jnp.concatenate([high, low], axis=0)
    prods = []
    for i in range(2):
        prod = nt(both, big[i])
        prods.append(prod[8 * i : 8 * i + 8] + prod[16 + 8 * i : 24 + 8 * i])
    prod = jnp.concatenate(prods, axis=0)
    w = weight[...]
    part = w * prod
    if over_tokens:
        outs[0][...] = w * (prod - jnp.sum(part, axis=1, keepdims=True))
    else:
        outs[0][...] = part
        step = pl.program_id(0)
        for i in range(2):
            outs[1][pl.ds(2 * step + i, 1), :] = jnp.sum(part[8 * i : 8 * i + 8], axis=0, keepdims=True)


def against(rows, big, weight, over_tokens):
    images, count, width = big.shape
    total = images * 8
    out_shape = [jax.ShapeDtypeStruct((total, count), F32)]
    out_specs = [pl.BlockSpec((16, count), lambda i: (i, 0))]
    if not over_tokens:
        out_shape.append(jax.ShapeDtypeStruct((images, count), F32))
        out_specs.append(pl.BlockSpec((images, count), lambda i: (0, 0)))
    return pl.pallas_call(
        lambda *refs: against_kernel(over_tokens, *refs),
        grid=(images // 2,),
        out_shape=out_shape,
        in_specs=[
            pl.BlockSpec((16, width), lambda i: (i, 0)),
            pl.BlockSpec((2, count, width), lambda i: (i, 0, 0)),
            pl.BlockSpec((16, count), lambda i: (i, 0)),
        ],
        out_specs=out_specs,
        compiler_params=pltpu.CompilerParams(vmem_limit_bytes=16 * 2**20),
        name="dispatch_grad" if over_tokens else "combine_grad",
    )(rows, big, weight)


def tokens_kernel(spread, pair, one, two, three, table, mine, theirs):
    half, width = mine.shape
    pieces = [ref[...].reshape(2 * ref.shape[1], ref.shape[2]) for ref in (pair, one, two, three)]
    depth = pieces[0].shape[0]
    count = pieces[0].shape[1] - width
    grads = jnp.concatenate([piece[:, width:] for piece in pieces], axis=0)
    total = grads.shape[0]
    near = total // 8
    c = lax.broadcasted_iota(jnp.int32, (total, near), 0)
    q = lax.broadcasted_iota(jnp.int32, (total, near), 1)
    fold = ((c // 64 == q // 8) & (c % 8 == q % 8)).astype(BF16)
    x = nt(pick_rows(count), grads)
    parts = []
    for side in range(2):
        y = jnp.concatenate([x[16 * side : 16 * side + 16]] * 8, axis=0)
        row = lax.broadcasted_iota(jnp.int32, y.shape, 0)
        col = lax.broadcasted_iota(jnp.int32, y.shape, 1)
        y = jnp.where((col // 8) % 8 == row // 16, y, 0.0).astype(BF16)
        parts.append(jnp.dot(y, fold, preferred_element_type=F32).astype(BF16))
    sums = jnp.dot(jnp.concatenate(parts, axis=0), table[:near], preferred_element_type=F32)
    side = spread[...].reshape(2 * half, spread.shape[2])
    for x, piece in enumerate(pieces):
        sums = sums + jnp.dot(side[:, x * depth : (x + 1) * depth], piece[:, :width], preferred_element_type=F32)
    mine[...] = sums[:half]
    theirs[...] = sums[half:]


def tokens_call(spread, pieces, table):
    vmem = pl.BlockSpec(memory_space=pltpu.VMEM)
    half, width = spread.shape[1], table.shape[1]
    return pl.pallas_call(
        tokens_kernel,
        out_shape=[jax.ShapeDtypeStruct((half, width), F32)] * 2,
        in_specs=[vmem] * 6,
        out_specs=[vmem] * 2,
        compiler_params=pltpu.CompilerParams(vmem_limit_bytes=24 * 2**20),
        name="token_grad",
    )(spread, *pieces, table)


def after(value, *earlier):
    return lax.optimization_barrier((value,) + earlier)[0]


def units_of(w_in, w_out):
    z = lax.axis_index("dp") // 4
    quarter = w_in.shape[1] // 4

    def unit(zz):
        start = zz * quarter
        return jnp.stack(
            [
                lax.dynamic_slice_in_dim(w_in, start, quarter, 1),
                lax.dynamic_slice_in_dim(w_out, start, quarter, 1),
            ]
        )

    return [unit(z ^ a) for a in range(4)]


def together(*values):
    return lax.optimization_barrier(values)


def reduce_z(own, *far):
    one, two, three = together(*[swap(v, "dp", 4 * a) for a, v in enumerate(far, 1)])
    return (own + one.astype(F32)) + (two.astype(F32) + three.astype(F32))


def all_x(v):
    return [v, *together(swap(v, "expert", 4), swap(v, "expert", 8), swap(v, "expert", 12))]


def doubled(v, axis, *steps):
    for k in steps:
        v = jnp.concatenate([v, swap(v, axis, k)], axis=0)
    return v


def summed(v, axis, *steps):
    for k in steps:
        v = v + swap(v, axis, k)
    return v


def summed_three(v, axis, *steps):
    one, two, three = together(*[swap(v, axis, k) for k in steps])
    return (v + one) + (two + three)


def per_device(tokens, out_grad, slot_params, w_in, w_out):
    images, count, width = tokens.shape
    own = slot_params.shape[1]
    half = images * own

    units = units_of(w_in, w_out.T)
    l0, r0 = swap(units[0], "dp", 1), swap(units[0], "dp", 3)
    u2 = swap(units[2], "dp", 8)
    u1 = swap(units[1], "dp", 4)
    table = doubled(slot_params.T, "expert", 2, 4)
    p0, q0 = swap(r0[0], "dp", 1), swap(l0[1], "dp", 3)
    table = doubled(table, "expert", 8)
    table = doubled(after(table, p0, q0), "expert", 1)

    table, p0, q0, u1, u2 = together(table, p0, q0, u1, u2)
    both = jnp.stack([u1, u2], axis=1)
    lb, rb = swap(both, "dp", 1), swap(both, "dp", 3)
    u3 = swap(after(units[3], u1), "dp", 12)
    rows, dispatch, combine, spread = slots_call(table, tokens, out_grad)
    rows = rows.reshape(2 * half, width)

    lb, rb, u3, rows = together(lb, rb, u3, rows)
    z1, z2 = swap(rows, "dp", 4), swap(rows, "dp", 8)
    l3, r3 = swap(u3, "dp", 1), swap(u3, "dp", 3)
    pb, qb = swap(rb[0], "dp", 1), swap(lb[1], "dp", 3)
    l3, r3, z2 = together(l3, r3, z2)
    p3, q3 = swap(r3[0], "dp", 1), swap(l3[1], "dp", 3)
    z3 = swap(z2, "dp", 4)
    pb, qb, p3, q3, z3 = together(pb, qb, p3, q3, z3)
    rows_in = jnp.concatenate([v[:half] for v in (rows, z1, z2, z3)], axis=0)
    rows_go = jnp.concatenate([v[half:] for v in (rows, z1, z2, z3)], axis=0)

    blocks = [units[0], l0, r0, p0, q0, both, lb, rb, pb, qb, u3, l3, r3, p3, q3]
    halves = ffn(rows_in, rows_go, blocks, half)
    slot_out = reduce_z(*halves[:4])
    slot_in_grad = reduce_z(*halves[4:])
    part, mix = against(slot_out, out_grad, combine, False)
    mix = summed_three(mix, "expert", 1, 2, 3)
    mix = summed_three(mix, "expert", 4, 8, 12)
    (back,) = against(slot_in_grad, tokens, dispatch, True)
    logit_grad = back + (part - combine * jnp.repeat(mix, own, axis=0))
    logit_grad_b = logit_grad.astype(BF16)

    near = jnp.concatenate([slot_in_grad.astype(BF16), logit_grad_b], axis=1)
    far = swap(near, "expert", 2)
    term = jnp.einsum(
        "bsm,bmd->sd", logit_grad_b.reshape(images, own, count), tokens, preferred_element_type=F32
    )
    term = summed(term, "dp", 4)
    term, far = together(term, far)
    pieces = all_x(jnp.stack([near, far]))
    term = summed(term, "dp", 8, 1, 2)
    slot_grad = term.T

    pieces[1] = after(pieces[1], term)
    mine, theirs = tokens_call(spread, pieces, table)
    token_grad = (mine + swap(theirs, "expert", 1)).astype(BF16)
    return (token_grad.reshape(images, -1, width), slot_grad)


def solution(mesh):
    return jax.shard_map(
        per_device,
        mesh=mesh,
        in_specs=(
            P("dp", None, None),
            P("dp", None, None),
            P(None, "expert"),
            P("dp", "expert"),
            P("expert", "dp"),
        ),
        out_specs=(P("dp", "expert", None), P(None, "expert")),
        check_vma=False,
    )
```

```python
import math
import jax
import jax.numpy as jnp
from jax import lax
from jax.experimental import pallas as pl
from jax.experimental.pallas import tpu as pltpu
from jax.sharding import PartitionSpec as P

F32 = jnp.float32
BF16 = jnp.bfloat16
ROOT = math.sqrt(2.0 / math.pi)


def swap(value, axis, k):
    count = lax.axis_size(axis)
    return lax.ppermute(value, axis, [(i, i ^ k) for i in range(count)])


def nt(a, b):
    return lax.dot_general(a, b, (((1,), (1,)), ((), ())), preferred_element_type=F32)


def ffn_kernel(rows_in, rows_go, *refs):
    own, l0, r0, p0, q0, both, lb, rb, pb, qb, last, l3, r3, p3, q3 = refs[:15]
    f0, f3 = (p0, q0), (p3, q3)
    outs, grads, (w1, w2) = refs[15:21], refs[21:25], refs[25:]
    me = lax.axis_index("dp")
    depth = w1.shape[0] // 16

    def place(which, dst):
        for a, sources in (
            (0, (own.at[which], l0.at[which], f0[which], r0.at[which])),
            (3, (last.at[which], l3.at[which], f3[which], r3.at[which])),
            (1, (both.at[which, 0], lb.at[which, 0], (pb, qb)[which].at[0], rb.at[which, 0])),
            (2, (both.at[which, 1], lb.at[which, 1], (pb, qb)[which].at[1], rb.at[which, 1])),
        ):
            for b, src in enumerate(sources):
                start = pl.multiple_of((me ^ (4 * a + b)) * depth, 16)
                dst[pl.ds(start, depth), :] = src[...]

    place(0, w1)
    place(1, w2)
    pre = jnp.dot(rows_in[...], w1[...], preferred_element_type=F32)
    sq = pre * pre
    th = jnp.tanh(ROOT * (pre + 0.044715 * (sq * pre)))
    cdf = 0.5 * (1.0 + th)
    hidden = (pre * cdf).astype(BF16)
    slope = cdf + 0.5 * pre * (1.0 - th * th) * (ROOT * (1.0 + 3 * 0.044715 * sq))
    hidden_grad = jnp.dot(rows_go[...], w2[...], preferred_element_type=F32)
    pre_grad = (hidden_grad * slope).astype(BF16)
    for whole, blocks in ((nt(hidden, w2[...]), outs), (nt(pre_grad, w1[...]), grads)):
        start = 0
        for block in blocks:
            stop = start + block.shape[0]
            block[...] = whole[start:stop].astype(block.dtype)
            start = stop


def ffn(rows_in, rows_go, blocks, own_rows):
    rows, width = rows_in.shape
    quarter = blocks[0].shape[2]
    vmem = pl.BlockSpec(memory_space=pltpu.VMEM)
    return pl.pallas_call(
        ffn_kernel,
        out_shape=[jax.ShapeDtypeStruct((own_rows, width), F32), jax.ShapeDtypeStruct((own_rows, width), BF16)]
        + [jax.ShapeDtypeStruct((own_rows // 2, width), BF16)] * 4
        + [jax.ShapeDtypeStruct((own_rows, width), t) for t in (F32, BF16, BF16, BF16)],
        in_specs=[vmem] * (2 + len(blocks)),
        out_specs=[vmem] * 10,
        scratch_shapes=[pltpu.VMEM((width, quarter), BF16), pltpu.VMEM((width, quarter), BF16)],
        compiler_params=pltpu.CompilerParams(vmem_limit_bytes=40 * 2**20),
        name="ffn",
    )(rows_in, rows_go, *blocks)


def pick_rows(count):
    col = lax.broadcasted_iota(jnp.int32, (32, count), 1)
    row = lax.broadcasted_iota(jnp.int32, (32, count), 0)
    owner = lax.axis_index("expert") ^ (row // 16)
    return (col == owner * 16 + row % 16).astype(BF16)


def slots_kernel(table, tokens, out_grad, rows, dispatch_own, combine_own, spread):
    step = pl.program_id(0)
    own = 8
    near = table.shape[0] // 2
    count = tokens.shape[1]
    pick = pick_rows(count)
    ins, gos, disp, comb, mine, theirs = [], [], [], [], [], []
    for i in range(2):
        logits = nt(table[...], tokens[i])
        up = jnp.exp(logits[:near] - jnp.max(logits[:near], axis=1, keepdims=True))
        dispatch = up / jnp.sum(up, axis=1, keepdims=True)
        down = jnp.exp(logits - jnp.max(logits, axis=0, keepdims=True))
        combine = down[:own] / jnp.sum(down, axis=0, keepdims=True)
        dispatch_b = dispatch.astype(BF16)
        ins.append(jnp.dot(dispatch_b[:16], tokens[i], preferred_element_type=F32)[:own])
        both = jnp.concatenate([combine, combine], axis=0).astype(BF16)
        gos.append(jnp.dot(both, out_grad[i], preferred_element_type=F32)[:own])
        disp.append(dispatch[:own])
        comb.append(combine)
        lines = nt(pick, dispatch_b).astype(BF16)
        image = 2 * step + i
        q = lax.broadcasted_iota(jnp.int32, (near, 8 * near), 0)
        col = lax.broadcasted_iota(jnp.int32, (near, 8 * near), 1)
        wide = (col == (q // 8) * 64 + q % 8 + image * 8).astype(BF16)
        lines = jnp.dot(lines, wide, preferred_element_type=F32)
        mine.append(lines[:16])
        theirs.append(lines[16:])
    rows[0] = jnp.concatenate(ins, axis=0).astype(BF16)
    rows[1] = jnp.concatenate(gos, axis=0).astype(BF16)
    dispatch_own[...] = jnp.concatenate(disp, axis=0)
    combine_own[...] = jnp.concatenate(comb, axis=0)
    spread[0] = jnp.concatenate(mine, axis=0).astype(BF16)
    spread[1] = jnp.concatenate(theirs, axis=0).astype(BF16)


def slots_call(table, tokens, out_grad):
    images, count, width = tokens.shape
    slots = table.shape[0]
    return pl.pallas_call(
        slots_kernel,
        grid=(images // 2,),
        out_shape=[
            jax.ShapeDtypeStruct((2, images * 8, width), BF16),
            jax.ShapeDtypeStruct((images * 8, count), F32),
            jax.ShapeDtypeStruct((images * 8, count), F32),
            jax.ShapeDtypeStruct((2, images * 16, slots * 4), BF16),
        ],
        in_specs=[
            pl.BlockSpec((slots, width), lambda i: (0, 0)),
            pl.BlockSpec((2, count, width), lambda i: (i, 0, 0)),
            pl.BlockSpec((2, count, width), lambda i: (i, 0, 0)),
        ],
        out_specs=[
            pl.BlockSpec((2, 16, width), lambda i: (0, i, 0)),
            pl.BlockSpec((16, count), lambda i: (i, 0)),
            pl.BlockSpec((16, count), lambda i: (i, 0)),
            pl.BlockSpec((2, 32, slots * 4), lambda i: (0, i, 0)),
        ],
        compiler_params=pltpu.CompilerParams(vmem_limit_bytes=24 * 2**20),
        cost_estimate=pl.CostEstimate(
            flops=2 * tokens.size * (slots + 32), bytes_accessed=4 * tokens.size, transcendentals=2 * images * slots * count
        ),
        name="slots",
    )(table, tokens, out_grad)


def against_kernel(over_tokens, rows, big, weight, *outs):
    value = rows[...]
    high = value.astype(BF16)
    low = (value - high.astype(F32)).astype(BF16)
    both = jnp.concatenate([high, low], axis=0)
    prods = []
    for i in range(2):
        prod = nt(both, big[i])
        prods.append(prod[8 * i : 8 * i + 8] + prod[16 + 8 * i : 24 + 8 * i])
    prod = jnp.concatenate(prods, axis=0)
    w = weight[...]
    part = w * prod
    if over_tokens:
        outs[0][...] = w * (prod - jnp.sum(part, axis=1, keepdims=True))
    else:
        outs[0][...] = part
        step = pl.program_id(0)
        for i in range(2):
            outs[1][pl.ds(2 * step + i, 1), :] = jnp.sum(part[8 * i : 8 * i + 8], axis=0, keepdims=True)


def against(rows, big, weight, over_tokens):
    images, count, width = big.shape
    total = images * 8
    out_shape = [jax.ShapeDtypeStruct((total, count), F32)]
    out_specs = [pl.BlockSpec((16, count), lambda i: (i, 0))]
    if not over_tokens:
        out_shape.append(jax.ShapeDtypeStruct((images, count), F32))
        out_specs.append(pl.BlockSpec((images, count), lambda i: (0, 0)))
    return pl.pallas_call(
        lambda *refs: against_kernel(over_tokens, *refs),
        grid=(images // 2,),
        out_shape=out_shape,
        in_specs=[
            pl.BlockSpec((16, width), lambda i: (i, 0)),
            pl.BlockSpec((2, count, width), lambda i: (i, 0, 0)),
            pl.BlockSpec((16, count), lambda i: (i, 0)),
        ],
        out_specs=out_specs,
        compiler_params=pltpu.CompilerParams(vmem_limit_bytes=16 * 2**20),
        name="dispatch_grad" if over_tokens else "combine_grad",
    )(rows, big, weight)


def tokens_kernel(spread, pair, one, two, three, table, mine, theirs):
    half, width = mine.shape
    pieces = [ref[...].reshape(2 * ref.shape[1], ref.shape[2]) for ref in (pair, one, two, three)]
    depth = pieces[0].shape[0]
    count = pieces[0].shape[1] - width
    grads = jnp.concatenate([piece[:, width:] for piece in pieces], axis=0)
    total = grads.shape[0]
    near = total // 8
    c = lax.broadcasted_iota(jnp.int32, (total, near), 0)
    q = lax.broadcasted_iota(jnp.int32, (total, near), 1)
    fold = ((c // 64 == q // 8) & (c % 8 == q % 8)).astype(BF16)
    x = nt(pick_rows(count), grads)
    parts = []
    for side in range(2):
        y = jnp.concatenate([x[16 * side : 16 * side + 16]] * 8, axis=0)
        row = lax.broadcasted_iota(jnp.int32, y.shape, 0)
        col = lax.broadcasted_iota(jnp.int32, y.shape, 1)
        y = jnp.where((col // 8) % 8 == row // 16, y, 0.0).astype(BF16)
        parts.append(jnp.dot(y, fold, preferred_element_type=F32).astype(BF16))
    sums = jnp.dot(jnp.concatenate(parts, axis=0), table[:near], preferred_element_type=F32)
    side = spread[...].reshape(2 * half, spread.shape[2])
    for x, piece in enumerate(pieces):
        sums = sums + jnp.dot(side[:, x * depth : (x + 1) * depth], piece[:, :width], preferred_element_type=F32)
    mine[...] = sums[:half]
    theirs[...] = sums[half:]


def tokens_call(spread, pieces, table):
    vmem = pl.BlockSpec(memory_space=pltpu.VMEM)
    half, width = spread.shape[1], table.shape[1]
    return pl.pallas_call(
        tokens_kernel,
        out_shape=[jax.ShapeDtypeStruct((half, width), F32)] * 2,
        in_specs=[vmem] * 6,
        out_specs=[vmem] * 2,
        compiler_params=pltpu.CompilerParams(vmem_limit_bytes=24 * 2**20),
        name="token_grad",
    )(spread, *pieces, table)


def after(value, *earlier):
    return lax.optimization_barrier((value,) + earlier)[0]


def units_of(w_in, w_out):
    z = lax.axis_index("dp") // 4
    quarter = w_in.shape[1] // 4

    def unit(zz):
        start = zz * quarter
        return jnp.stack(
            [
                lax.dynamic_slice_in_dim(w_in, start, quarter, 1),
                lax.dynamic_slice_in_dim(w_out, start, quarter, 1),
            ]
        )

    return [unit(z ^ a) for a in range(4)]


def together(*values):
    return lax.optimization_barrier(values)


def sent_z(blocks):
    places = (1, 2, 3) if len(blocks) == 3 else (1, 2, 2, 3, 3)
    return [swap(v, "dp", 4 * a) for a, v in zip(places, blocks)]


def added(own, *parts):
    parts = together(*parts)
    if len(parts) > 3:
        one, two, two_b, three, three_b = parts
        parts = one, jnp.concatenate([two, two_b], axis=0), jnp.concatenate([three, three_b], axis=0)
    one, two, three = parts
    return (own + one.astype(F32)) + (two.astype(F32) + three.astype(F32))


def all_x(v):
    return [v, *together(swap(v, "expert", 4), swap(v, "expert", 8), swap(v, "expert", 12))]


def doubled(v, axis, *steps):
    for k in steps:
        v = jnp.concatenate([v, swap(v, axis, k)], axis=0)
    return v


def summed(v, axis, *steps):
    for k in steps:
        v = v + swap(v, axis, k)
    return v


def summed_three(v, axis, *steps):
    one, two, three = together(*[swap(v, axis, k) for k in steps])
    return (v + one) + (two + three)


def per_device(tokens, out_grad, slot_params, w_in, w_out):
    images, count, width = tokens.shape
    own = slot_params.shape[1]
    half = images * own

    units = units_of(w_in, w_out.T)
    l0, r0 = swap(units[0], "dp", 1), swap(units[0], "dp", 3)
    u2 = swap(units[2], "dp", 8)
    u1 = swap(units[1], "dp", 4)
    table = doubled(slot_params.T, "expert", 4, 1)
    p0, q0 = swap(r0[0], "dp", 1), swap(l0[1], "dp", 3)
    table = doubled(table, "expert", 8)
    table = doubled(after(table, p0, q0), "expert", 2)

    table, p0, q0, u1, u2 = together(table, p0, q0, u1, u2)
    both = jnp.stack([u1, u2], axis=1)
    lb, rb = swap(both, "dp", 1), swap(both, "dp", 3)
    u3 = swap(after(units[3], u1), "dp", 12)
    table = table.reshape(2, 2, 2, 2, own, width).transpose(2, 1, 3, 0, 4, 5).reshape(-1, width)
    rows, dispatch, combine, spread = slots_call(table, tokens, out_grad)
    rows = rows.reshape(2 * half, width)

    lb, rb, u3, rows = together(lb, rb, u3, rows)
    z1, z2 = swap(rows, "dp", 4), swap(rows, "dp", 8)
    l3, r3 = swap(u3, "dp", 1), swap(u3, "dp", 3)
    pb, qb = swap(rb[0], "dp", 1), swap(lb[1], "dp", 3)
    l3, r3, z2 = together(l3, r3, z2)
    p3, q3 = swap(r3[0], "dp", 1), swap(l3[1], "dp", 3)
    z3 = swap(z2, "dp", 4)
    pb, qb, p3, q3, z3 = together(pb, qb, p3, q3, z3)
    rows_in = jnp.concatenate([v[:half] for v in (rows, z1, z2, z3)], axis=0)
    rows_go = jnp.concatenate([v[half:] for v in (rows, z1, z2, z3)], axis=0)

    blocks = [units[0], l0, r0, p0, q0, both, lb, rb, pb, qb, u3, l3, r3, p3, q3]
    halves = ffn(rows_in, rows_go, blocks, half)
    slot_out = added(halves[0], *sent_z(halves[1:6]))
    slot_in_grad = added(halves[6], *sent_z(halves[7:]))
    part, mix = against(slot_out, out_grad, combine, False)
    mix = summed_three(mix, "expert", 1, 2, 3)
    mix = summed_three(mix, "expert", 4, 8, 12)
    (back,) = against(slot_in_grad, tokens, dispatch, True)
    logit_grad = back + (part - combine * jnp.repeat(mix, own, axis=0))
    logit_grad_b = logit_grad.astype(BF16)

    near = jnp.concatenate([slot_in_grad.astype(BF16), logit_grad_b], axis=1)
    far = swap(near, "expert", 2)
    term = jnp.einsum(
        "bsm,bmd->sd", logit_grad_b.reshape(images, own, count), tokens, preferred_element_type=F32
    )
    term = summed(term, "dp", 4)
    term, far = together(term, far)
    pieces = all_x(jnp.stack([near, far]))
    term = summed(term, "dp", 8, 1, 2)
    slot_grad = term.T

    pieces[1] = after(pieces[1], term)
    mine, theirs = tokens_call(spread, pieces, table)
    token_grad = (mine + swap(theirs, "expert", 1)).astype(BF16)
    return (token_grad.reshape(images, -1, width), slot_grad)


def solution(mesh):
    return jax.shard_map(
        per_device,
        mesh=mesh,
        in_specs=(
            P("dp", None, None),
            P("dp", None, None),
            P(None, "expert"),
            P("dp", "expert"),
            P("expert", "dp"),
        ),
        out_specs=(P("dp", "expert", None), P(None, "expert")),
        check_vma=False,
    )
```

```python
import math
import jax
import jax.numpy as jnp
from jax import lax
from jax.experimental import pallas as pl
from jax.experimental.pallas import tpu as pltpu
from jax.sharding import PartitionSpec as P

F32 = jnp.float32
BF16 = jnp.bfloat16
ROOT = math.sqrt(2.0 / math.pi)


def swap(value, axis, k):
    count = lax.axis_size(axis)
    return lax.ppermute(value, axis, [(i, i ^ k) for i in range(count)])


def nt(a, b):
    return lax.dot_general(a, b, (((1,), (1,)), ((), ())), preferred_element_type=F32)


def ffn_kernel(rows_in, rows_go, *refs):
    own, l0, r0, p0, q0, both, lb, rb, pb, qb, last, l3, r3, p3, q3 = refs[:15]
    f0, f3 = (p0, q0), (p3, q3)
    outs, grads, (w1, w2) = refs[15:19], refs[19:23], refs[23:]
    me = lax.axis_index("dp")
    depth = w1.shape[0] // 16

    def place(which, dst):
        for a, sources in (
            (0, (own.at[which], l0.at[which], f0[which], r0.at[which])),
            (3, (last.at[which], l3.at[which], f3[which], r3.at[which])),
            (1, (both.at[which, 0], lb.at[which, 0], (pb, qb)[which].at[0], rb.at[which, 0])),
            (2, (both.at[which, 1], lb.at[which, 1], (pb, qb)[which].at[1], rb.at[which, 1])),
        ):
            for b, src in enumerate(sources):
                start = pl.multiple_of((me ^ (4 * a + b)) * depth, 16)
                dst[pl.ds(start, depth), :] = src[...]

    place(0, w1)
    place(1, w2)
    pre = jnp.dot(rows_in[...], w1[...], preferred_element_type=F32)
    sq = pre * pre
    th = jnp.tanh(ROOT * (pre + 0.044715 * (sq * pre)))
    cdf = 0.5 * (1.0 + th)
    hidden = (pre * cdf).astype(BF16)
    slope = cdf + 0.5 * pre * (1.0 - th * th) * (ROOT * (1.0 + 3 * 0.044715 * sq))
    hidden_grad = jnp.dot(rows_go[...], w2[...], preferred_element_type=F32)
    pre_grad = (hidden_grad * slope).astype(BF16)
    rows = outs[0].shape[0]
    for whole, blocks in ((nt(hidden, w2[...]), outs), (nt(pre_grad, w1[...]), grads)):
        for a, block in enumerate(blocks):
            block[...] = whole[a * rows : (a + 1) * rows].astype(block.dtype)


def ffn(rows_in, rows_go, blocks, own_rows):
    rows, width = rows_in.shape
    quarter = blocks[0].shape[2]
    vmem = pl.BlockSpec(memory_space=pltpu.VMEM)
    return pl.pallas_call(
        ffn_kernel,
        out_shape=[jax.ShapeDtypeStruct((own_rows, width), t) for t in (F32, BF16, BF16, BF16)] * 2,
        in_specs=[vmem] * (2 + len(blocks)),
        out_specs=[vmem] * 8,
        scratch_shapes=[pltpu.VMEM((width, quarter), BF16), pltpu.VMEM((width, quarter), BF16)],
        compiler_params=pltpu.CompilerParams(vmem_limit_bytes=40 * 2**20),
        name="ffn",
    )(rows_in, rows_go, *blocks)


def pick_rows(count):
    col = lax.broadcasted_iota(jnp.int32, (32, count), 1)
    row = lax.broadcasted_iota(jnp.int32, (32, count), 0)
    owner = lax.axis_index("expert") ^ (row // 16)
    return (col == owner * 16 + row % 16).astype(BF16)


def slots_kernel(table, tokens, rows, dispatch_own, combine_own, near_out):
    own = 8
    near = table.shape[0] // 2
    ins, disp, comb = [], [], []
    for i in range(2):
        logits = nt(table[...], tokens[i])
        up = jnp.exp(logits[:near] - jnp.max(logits[:near], axis=1, keepdims=True))
        dispatch = up / jnp.sum(up, axis=1, keepdims=True)
        down = jnp.exp(logits - jnp.max(logits, axis=0, keepdims=True))
        combine = down[:own] / jnp.sum(down, axis=0, keepdims=True)
        dispatch_b = dispatch.astype(BF16)
        ins.append(jnp.dot(dispatch_b[:16], tokens[i], preferred_element_type=F32)[:own])
        disp.append(dispatch[:own])
        comb.append(combine)
        near_out[i] = dispatch_b
    rows[...] = jnp.concatenate(ins, axis=0).astype(BF16)
    dispatch_own[...] = jnp.concatenate(disp, axis=0)
    combine_own[...] = jnp.concatenate(comb, axis=0)


def slots_call(table, tokens):
    images, count, width = tokens.shape
    slots = table.shape[0]
    return pl.pallas_call(
        slots_kernel,
        grid=(images // 2,),
        out_shape=[
            jax.ShapeDtypeStruct((images * 8, width), BF16),
            jax.ShapeDtypeStruct((images * 8, count), F32),
            jax.ShapeDtypeStruct((images * 8, count), F32),
            jax.ShapeDtypeStruct((images, slots // 2, count), BF16),
        ],
        in_specs=[
            pl.BlockSpec((slots, width), lambda i: (0, 0)),
            pl.BlockSpec((2, count, width), lambda i: (i, 0, 0)),
        ],
        out_specs=[
            pl.BlockSpec((16, width), lambda i: (i, 0)),
            pl.BlockSpec((16, count), lambda i: (i, 0)),
            pl.BlockSpec((16, count), lambda i: (i, 0)),
            pl.BlockSpec((2, slots // 2, count), lambda i: (i, 0, 0)),
        ],
        compiler_params=pltpu.CompilerParams(vmem_limit_bytes=24 * 2**20),
        cost_estimate=pl.CostEstimate(
            flops=2 * tokens.size * (slots + 16), bytes_accessed=2 * tokens.size, transcendentals=2 * images * slots * count
        ),
        name="slots",
    )(table, tokens)


def spread_kernel(near, out):
    images, slots, count = near.shape
    pick = pick_rows(count)
    q = lax.broadcasted_iota(jnp.int32, (slots, 8 * slots), 0)
    col = lax.broadcasted_iota(jnp.int32, (slots, 8 * slots), 1)
    first = (q // 8) * 64 + q % 8
    for image in range(images):
        lines = nt(pick, near[image]).astype(BF16)
        wide = (col == first + image * 8).astype(BF16)
        lines = jnp.dot(lines, wide, preferred_element_type=F32).astype(BF16)
        out[0, 16 * image : 16 * image + 16] = lines[:16]
        out[1, 16 * image : 16 * image + 16] = lines[16:]


def spread_call(near):
    images, slots, _ = near.shape
    vmem = pl.BlockSpec(memory_space=pltpu.VMEM)
    return pl.pallas_call(
        spread_kernel,
        out_shape=jax.ShapeDtypeStruct((2, images * 16, slots * 8), BF16),
        in_specs=[vmem],
        out_specs=vmem,
        compiler_params=pltpu.CompilerParams(vmem_limit_bytes=16 * 2**20),
        name="spread",
    )(near)


def against_kernel(over_tokens, rows, big, weight, *outs):
    value = rows[...]
    high = value.astype(BF16)
    low = (value - high.astype(F32)).astype(BF16)
    both = jnp.concatenate([high, low], axis=0)
    prods = []
    for i in range(2):
        prod = nt(both, big[i])
        prods.append(prod[8 * i : 8 * i + 8] + prod[16 + 8 * i : 24 + 8 * i])
    prod = jnp.concatenate(prods, axis=0)
    w = weight[...]
    part = w * prod
    if over_tokens:
        outs[0][...] = w * (prod - jnp.sum(part, axis=1, keepdims=True))
    else:
        outs[0][...] = part
        step = pl.program_id(0)
        for i in range(2):
            outs[1][pl.ds(2 * step + i, 1), :] = jnp.sum(part[8 * i : 8 * i + 8], axis=0, keepdims=True)


def against(rows, big, weight, over_tokens):
    images, count, width = big.shape
    total = images * 8
    out_shape = [jax.ShapeDtypeStruct((total, count), F32)]
    out_specs = [pl.BlockSpec((16, count), lambda i: (i, 0))]
    if not over_tokens:
        out_shape.append(jax.ShapeDtypeStruct((images, count), F32))
        out_specs.append(pl.BlockSpec((images, count), lambda i: (0, 0)))
    return pl.pallas_call(
        lambda *refs: against_kernel(over_tokens, *refs),
        grid=(images // 2,),
        out_shape=out_shape,
        in_specs=[
            pl.BlockSpec((16, width), lambda i: (i, 0)),
            pl.BlockSpec((2, count, width), lambda i: (i, 0, 0)),
            pl.BlockSpec((16, count), lambda i: (i, 0)),
        ],
        out_specs=out_specs,
        compiler_params=pltpu.CompilerParams(vmem_limit_bytes=16 * 2**20),
        name="dispatch_grad" if over_tokens else "combine_grad",
    )(rows, big, weight)


def tokens_kernel(spread, pair, one, two, three, table, mine, theirs):
    half, width = mine.shape
    pieces = [ref[...].reshape(2 * ref.shape[1], ref.shape[2]) for ref in (pair, one, two, three)]
    depth = pieces[0].shape[0]
    count = pieces[0].shape[1] - width
    grads = jnp.concatenate([piece[:, width:] for piece in pieces], axis=0)
    total = grads.shape[0]
    near = total // 8
    c = lax.broadcasted_iota(jnp.int32, (total, near), 0)
    q = lax.broadcasted_iota(jnp.int32, (total, near), 1)
    fold = ((c // 64 == q // 8) & (c % 8 == q % 8)).astype(BF16)
    x = nt(pick_rows(count), grads)
    parts = []
    for side in range(2):
        y = jnp.concatenate([x[16 * side : 16 * side + 16]] * 8, axis=0)
        row = lax.broadcasted_iota(jnp.int32, y.shape, 0)
        col = lax.broadcasted_iota(jnp.int32, y.shape, 1)
        y = jnp.where((col // 8) % 8 == row // 16, y, 0.0).astype(BF16)
        parts.append(jnp.dot(y, fold, preferred_element_type=F32).astype(BF16))
    sums = jnp.dot(jnp.concatenate(parts, axis=0), table[:near], preferred_element_type=F32)
    side = spread[...].reshape(2 * half, spread.shape[2])
    for x, piece in enumerate(pieces):
        sums = sums + jnp.dot(side[:, x * depth : (x + 1) * depth], piece[:, :width], preferred_element_type=F32)
    mine[...] = sums[:half]
    theirs[...] = sums[half:]


def tokens_call(spread, pieces, table):
    vmem = pl.BlockSpec(memory_space=pltpu.VMEM)
    half, width = spread.shape[1], table.shape[1]
    return pl.pallas_call(
        tokens_kernel,
        out_shape=[jax.ShapeDtypeStruct((half, width), F32)] * 2,
        in_specs=[vmem] * 6,
        out_specs=[vmem] * 2,
        compiler_params=pltpu.CompilerParams(vmem_limit_bytes=24 * 2**20),
        name="token_grad",
    )(spread, *pieces, table)


def after(value, *earlier):
    return lax.optimization_barrier((value,) + earlier)[0]


def units_of(w_in, w_out):
    z = lax.axis_index("dp") // 4
    quarter = w_in.shape[1] // 4

    def unit(zz):
        start = zz * quarter
        return jnp.stack(
            [
                lax.dynamic_slice_in_dim(w_in, start, quarter, 1),
                lax.dynamic_slice_in_dim(w_out, start, quarter, 1),
            ]
        )

    return [unit(z ^ a) for a in range(4)]


def together(*values):
    return lax.optimization_barrier(values)


def reduce_z(own, *far):
    one, two, three = together(*[swap(v, "dp", 4 * a) for a, v in enumerate(far, 1)])
    return (own + one.astype(F32)) + (two.astype(F32) + three.astype(F32))


def all_x(v):
    return [v, *together(swap(v, "expert", 4), swap(v, "expert", 8), swap(v, "expert", 12))]


def doubled(v, axis, *steps):
    for k in steps:
        v = jnp.concatenate([v, swap(v, axis, k)], axis=0)
    return v


def summed(v, axis, *steps):
    for k in steps:
        v = v + swap(v, axis, k)
    return v


def summed_three(v, axis, *steps):
    one, two, three = together(*[swap(v, axis, k) for k in steps])
    return (v + one) + (two + three)


def per_device(tokens, out_grad, slot_params, w_in, w_out):
    images, count, width = tokens.shape
    own = slot_params.shape[1]
    half = images * own

    units = units_of(w_in, w_out.T)
    l0, r0 = swap(units[0], "dp", 1), swap(units[0], "dp", 3)
    u2 = swap(units[2], "dp", 8)
    u1 = swap(units[1], "dp", 4)
    p0, q0 = swap(r0[0], "dp", 1), swap(l0[1], "dp", 3)
    table = doubled(slot_params.T, "expert", 2, 4)

    table, p0, q0, u1, u2 = together(table, p0, q0, u1, u2)
    both = jnp.stack([u1, u2], axis=1)
    lb, rb = swap(both, "dp", 1), swap(both, "dp", 3)
    u3 = swap(after(units[3], u1), "dp", 12)
    table = doubled(table, "expert", 8, 1)
    slot_in, dispatch, combine, near = slots_call(table, tokens)
    slot_go = jnp.einsum(
        "bsm,bmd->bsd", combine.astype(BF16).reshape(images, own, count), out_grad, preferred_element_type=F32
    )
    rows = jnp.concatenate([slot_in, slot_go.astype(BF16).reshape(half, width)], axis=0)

    lb, rb, u3, rows = together(lb, rb, u3, rows)
    z2, z1 = swap(rows, "dp", 8), swap(rows, "dp", 4)
    l3, r3 = swap(u3, "dp", 1), swap(u3, "dp", 3)
    pb, qb = swap(rb[0], "dp", 1), swap(lb[1], "dp", 3)
    spread = spread_call(near)
    l3, r3, z2, spread = together(l3, r3, z2, spread)
    p3, q3 = swap(r3[0], "dp", 1), swap(l3[1], "dp", 3)
    z3 = swap(z2, "dp", 4)
    pb, qb, p3, q3, z3 = together(pb, qb, p3, q3, z3)
    rows_in = jnp.concatenate([v[:half] for v in (rows, z1, z2, z3)], axis=0)
    rows_go = jnp.concatenate([v[half:] for v in (rows, z1, z2, z3)], axis=0)

    blocks = [units[0], l0, r0, p0, q0, both, lb, rb, pb, qb, u3, l3, r3, p3, q3]
    halves = ffn(rows_in, rows_go, blocks, half)
    slot_out = reduce_z(*halves[:4])
    slot_in_grad = reduce_z(*halves[4:])
    part, mix = against(slot_out, out_grad, combine, False)
    mix = summed_three(mix, "expert", 1, 2, 3)
    mix = summed_three(mix, "expert", 4, 8, 12)
    (back,) = against(slot_in_grad, tokens, dispatch, True)
    logit_grad = back + (part - combine * jnp.repeat(mix, own, axis=0))
    logit_grad_b = logit_grad.astype(BF16)

    near = jnp.concatenate([slot_in_grad.astype(BF16), logit_grad_b], axis=1)
    far = swap(near, "expert", 2)
    term = jnp.einsum(
        "bsm,bmd->sd", logit_grad_b.reshape(images, own, count), tokens, preferred_element_type=F32
    )
    term = summed(term, "dp", 4)
    term, far = together(term, far)
    pieces = all_x(jnp.stack([near, far]))
    term = summed(term, "dp", 8, 1, 2)
    slot_grad = term.T

    pieces[1] = after(pieces[1], term)
    mine, theirs = tokens_call(spread, pieces, table)
    token_grad = (mine + swap(theirs, "expert", 1)).astype(BF16)
    return (token_grad.reshape(images, -1, width), slot_grad)


def solution(mesh):
    return jax.shard_map(
        per_device,
        mesh=mesh,
        in_specs=(
            P("dp", None, None),
            P("dp", None, None),
            P(None, "expert"),
            P("dp", "expert"),
            P("expert", "dp"),
        ),
        out_specs=(P("dp", "expert", None), P(None, "expert")),
        check_vma=False,
    )
```

```python
import math
import jax
import jax.numpy as jnp
from jax import lax
from jax.experimental import pallas as pl
from jax.experimental.pallas import tpu as pltpu
from jax.sharding import PartitionSpec as P

F32 = jnp.float32
BF16 = jnp.bfloat16
ROOT = math.sqrt(2.0 / math.pi)


def swap(value, axis, k):
    count = lax.axis_size(axis)
    return lax.ppermute(value, axis, [(i, i ^ k) for i in range(count)])


def nt(a, b):
    return lax.dot_general(a, b, (((1,), (1,)), ((), ())), preferred_element_type=F32)


def ffn_kernel(rows_in, rows_go, *refs):
    own, l0, r0, p0, q0, both, lb, rb, pb, qb, last, l3, r3, p3, q3 = refs[:15]
    f0, f3 = (p0, q0), (p3, q3)
    outs, grads, (w1, w2) = refs[15:19], refs[19:23], refs[23:]
    me = lax.axis_index("dp")
    depth = w1.shape[0] // 16

    def place(which, dst):
        for a, sources in (
            (0, (own.at[which], l0.at[which], f0[which], r0.at[which])),
            (3, (last.at[which], l3.at[which], f3[which], r3.at[which])),
            (1, (both.at[which, 0], lb.at[which, 0], (pb, qb)[which].at[0], rb.at[which, 0])),
            (2, (both.at[which, 1], lb.at[which, 1], (pb, qb)[which].at[1], rb.at[which, 1])),
        ):
            for b, src in enumerate(sources):
                start = pl.multiple_of((me ^ (4 * a + b)) * depth, 16)
                dst[pl.ds(start, depth), :] = src[...]

    place(0, w1)
    place(1, w2)
    pre = jnp.dot(rows_in[...], w1[...], preferred_element_type=F32)
    sq = pre * pre
    th = jnp.tanh(ROOT * (pre + 0.044715 * (sq * pre)))
    cdf = 0.5 * (1.0 + th)
    hidden = (pre * cdf).astype(BF16)
    slope = cdf + 0.5 * pre * (1.0 - th * th) * (ROOT * (1.0 + 3 * 0.044715 * sq))
    hidden_grad = jnp.dot(rows_go[...], w2[...], preferred_element_type=F32)
    pre_grad = (hidden_grad * slope).astype(BF16)
    rows = outs[0].shape[0]
    for whole, blocks in ((nt(hidden, w2[...]), outs), (nt(pre_grad, w1[...]), grads)):
        for a, block in enumerate(blocks):
            block[...] = whole[a * rows : (a + 1) * rows].astype(block.dtype)


def ffn(rows_in, rows_go, blocks, own_rows):
    rows, width = rows_in.shape
    quarter = blocks[0].shape[2]
    vmem = pl.BlockSpec(memory_space=pltpu.VMEM)
    return pl.pallas_call(
        ffn_kernel,
        out_shape=[jax.ShapeDtypeStruct((own_rows, width), t) for t in (F32, BF16, BF16, BF16)] * 2,
        in_specs=[vmem] * (2 + len(blocks)),
        out_specs=[vmem] * 8,
        scratch_shapes=[pltpu.VMEM((width, quarter), BF16), pltpu.VMEM((width, quarter), BF16)],
        compiler_params=pltpu.CompilerParams(vmem_limit_bytes=40 * 2**20),
        name="ffn",
    )(rows_in, rows_go, *blocks)


def pick_rows(count):
    col = lax.broadcasted_iota(jnp.int32, (32, count), 1)
    row = lax.broadcasted_iota(jnp.int32, (32, count), 0)
    owner = lax.axis_index("expert") ^ (row // 16)
    return (col == owner * 16 + row % 16).astype(BF16)


def slots_kernel(table, tokens, rows, dispatch_own, combine_own, near_out):
    own = 8
    near = table.shape[0] // 2
    ins, disp, comb = [], [], []
    for i in range(2):
        logits = nt(table[...], tokens[i])
        up = jnp.exp(logits[:near] - jnp.max(logits[:near], axis=1, keepdims=True))
        dispatch = up / jnp.sum(up, axis=1, keepdims=True)
        down = jnp.exp(logits - jnp.max(logits, axis=0, keepdims=True))
        combine = down[:own] / jnp.sum(down, axis=0, keepdims=True)
        dispatch_b = dispatch.astype(BF16)
        ins.append(jnp.dot(dispatch_b[:16], tokens[i], preferred_element_type=F32)[:own])
        disp.append(dispatch[:own])
        comb.append(combine)
        near_out[i] = dispatch_b
    rows[...] = jnp.concatenate(ins, axis=0).astype(BF16)
    dispatch_own[...] = jnp.concatenate(disp, axis=0)
    combine_own[...] = jnp.concatenate(comb, axis=0)


def slots_call(table, tokens):
    images, count, width = tokens.shape
    slots = table.shape[0]
    return pl.pallas_call(
        slots_kernel,
        grid=(images // 2,),
        out_shape=[
            jax.ShapeDtypeStruct((images * 8, width), BF16),
            jax.ShapeDtypeStruct((images * 8, count), F32),
            jax.ShapeDtypeStruct((images * 8, count), F32),
            jax.ShapeDtypeStruct((images, slots // 2, count), BF16),
        ],
        in_specs=[
            pl.BlockSpec((slots, width), lambda i: (0, 0)),
            pl.BlockSpec((2, count, width), lambda i: (i, 0, 0)),
        ],
        out_specs=[
            pl.BlockSpec((16, width), lambda i: (i, 0)),
            pl.BlockSpec((16, count), lambda i: (i, 0)),
            pl.BlockSpec((16, count), lambda i: (i, 0)),
            pl.BlockSpec((2, slots // 2, count), lambda i: (i, 0, 0)),
        ],
        compiler_params=pltpu.CompilerParams(vmem_limit_bytes=24 * 2**20),
        cost_estimate=pl.CostEstimate(
            flops=2 * tokens.size * (slots + 16), bytes_accessed=2 * tokens.size, transcendentals=2 * images * slots * count
        ),
        name="slots",
    )(table, tokens)


def spread_kernel(near, out):
    images, slots, count = near.shape
    pick = pick_rows(count)
    q = lax.broadcasted_iota(jnp.int32, (slots, 8 * slots), 0)
    col = lax.broadcasted_iota(jnp.int32, (slots, 8 * slots), 1)
    first = (q // 8) * 64 + q % 8
    for image in range(images):
        lines = nt(pick, near[image]).astype(BF16)
        wide = (col == first + image * 8).astype(BF16)
        lines = jnp.dot(lines, wide, preferred_element_type=F32).astype(BF16)
        out[0, 16 * image : 16 * image + 16] = lines[:16]
        out[1, 16 * image : 16 * image + 16] = lines[16:]


def spread_call(near):
    images, slots, _ = near.shape
    vmem = pl.BlockSpec(memory_space=pltpu.VMEM)
    return pl.pallas_call(
        spread_kernel,
        out_shape=jax.ShapeDtypeStruct((2, images * 16, slots * 8), BF16),
        in_specs=[vmem],
        out_specs=vmem,
        compiler_params=pltpu.CompilerParams(vmem_limit_bytes=16 * 2**20),
        name="spread",
    )(near)


def against_kernel(over_tokens, rows, big, weight, *outs):
    value = rows[...]
    high = value.astype(BF16)
    low = (value - high.astype(F32)).astype(BF16)
    both = jnp.concatenate([high, low], axis=0)
    prods = []
    for i in range(2):
        prod = nt(both, big[i])
        prods.append(prod[8 * i : 8 * i + 8] + prod[16 + 8 * i : 24 + 8 * i])
    prod = jnp.concatenate(prods, axis=0)
    w = weight[...]
    part = w * prod
    if over_tokens:
        outs[0][...] = w * (prod - jnp.sum(part, axis=1, keepdims=True))
    else:
        outs[0][...] = part
        step = pl.program_id(0)
        for i in range(2):
            outs[1][pl.ds(2 * step + i, 1), :] = jnp.sum(part[8 * i : 8 * i + 8], axis=0, keepdims=True)


def against(rows, big, weight, over_tokens):
    images, count, width = big.shape
    total = images * 8
    out_shape = [jax.ShapeDtypeStruct((total, count), F32)]
    out_specs = [pl.BlockSpec((16, count), lambda i: (i, 0))]
    if not over_tokens:
        out_shape.append(jax.ShapeDtypeStruct((images, count), F32))
        out_specs.append(pl.BlockSpec((images, count), lambda i: (0, 0)))
    return pl.pallas_call(
        lambda *refs: against_kernel(over_tokens, *refs),
        grid=(images // 2,),
        out_shape=out_shape,
        in_specs=[
            pl.BlockSpec((16, width), lambda i: (i, 0)),
            pl.BlockSpec((2, count, width), lambda i: (i, 0, 0)),
            pl.BlockSpec((16, count), lambda i: (i, 0)),
        ],
        out_specs=out_specs,
        compiler_params=pltpu.CompilerParams(vmem_limit_bytes=16 * 2**20),
        name="dispatch_grad" if over_tokens else "combine_grad",
    )(rows, big, weight)


def tokens_kernel(spread, pair, one, two, three, table, mine, theirs):
    half, width = mine.shape
    pieces = [ref[...].reshape(2 * ref.shape[1], ref.shape[2]) for ref in (pair, one, two, three)]
    depth = pieces[0].shape[0]
    count = pieces[0].shape[1] - width
    grads = jnp.concatenate([piece[:, width:] for piece in pieces], axis=0)
    total = grads.shape[0]
    near = total // 8
    c = lax.broadcasted_iota(jnp.int32, (total, near), 0)
    q = lax.broadcasted_iota(jnp.int32, (total, near), 1)
    fold = ((c // 64 == q // 8) & (c % 8 == q % 8)).astype(BF16)
    x = nt(pick_rows(count), grads)
    parts = []
    for side in range(2):
        y = jnp.concatenate([x[16 * side : 16 * side + 16]] * 8, axis=0)
        row = lax.broadcasted_iota(jnp.int32, y.shape, 0)
        col = lax.broadcasted_iota(jnp.int32, y.shape, 1)
        y = jnp.where((col // 8) % 8 == row // 16, y, 0.0).astype(BF16)
        parts.append(jnp.dot(y, fold, preferred_element_type=F32).astype(BF16))
    sums = jnp.dot(jnp.concatenate(parts, axis=0), table[:near], preferred_element_type=F32)
    side = spread[...].reshape(2 * half, spread.shape[2])
    for x, piece in enumerate(pieces):
        sums = sums + jnp.dot(side[:, x * depth : (x + 1) * depth], piece[:, :width], preferred_element_type=F32)
    mine[...] = sums[:half]
    theirs[...] = sums[half:]


def tokens_call(spread, pieces, table):
    vmem = pl.BlockSpec(memory_space=pltpu.VMEM)
    half, width = spread.shape[1], table.shape[1]
    return pl.pallas_call(
        tokens_kernel,
        out_shape=[jax.ShapeDtypeStruct((half, width), F32)] * 2,
        in_specs=[vmem] * 6,
        out_specs=[vmem] * 2,
        compiler_params=pltpu.CompilerParams(vmem_limit_bytes=24 * 2**20),
        name="token_grad",
    )(spread, *pieces, table)


def after(value, *earlier):
    return lax.optimization_barrier((value,) + earlier)[0]


def units_of(w_in, w_out):
    z = lax.axis_index("dp") // 4
    quarter = w_in.shape[1] // 4

    def unit(zz):
        start = zz * quarter
        return jnp.stack(
            [
                lax.dynamic_slice_in_dim(w_in, start, quarter, 1),
                lax.dynamic_slice_in_dim(w_out, start, quarter, 1),
            ]
        )

    return [unit(z ^ a) for a in range(4)]


def together(*values):
    return lax.optimization_barrier(values)


def reduce_z(own, *far):
    one, two, three = together(*[swap(v, "dp", 4 * a) for a, v in enumerate(far, 1)])
    return (own + one.astype(F32)) + (two.astype(F32) + three.astype(F32))


def all_x(v):
    return [v, *together(swap(v, "expert", 4), swap(v, "expert", 8), swap(v, "expert", 12))]


def doubled(v, axis, *steps):
    for k in steps:
        v = jnp.concatenate([v, swap(v, axis, k)], axis=0)
    return v


def summed(v, axis, *steps):
    for k in steps:
        v = v + swap(v, axis, k)
    return v


def summed_three(v, axis, *steps):
    one, two, three = together(*[swap(v, axis, k) for k in steps])
    return (v + one) + (two + three)


def per_device(tokens, out_grad, slot_params, w_in, w_out):
    images, count, width = tokens.shape
    own = slot_params.shape[1]
    half = images * own

    units = units_of(w_in, w_out.T)
    l0, r0 = swap(units[0], "dp", 1), swap(units[0], "dp", 3)
    u2 = swap(units[2], "dp", 8)
    u1 = swap(units[1], "dp", 4)
    p0, q0 = swap(r0[0], "dp", 1), swap(l0[1], "dp", 3)
    table = doubled(slot_params.T, "expert", 2, 4)

    u3 = swap(after(units[3], u1), "dp", 12)
    table, p0, q0, u1, u2 = together(table, p0, q0, u1, u2)
    both = jnp.stack([u1, u2], axis=1)
    lb, rb = swap(both, "dp", 1), swap(both, "dp", 3)
    table = doubled(table, "expert", 8, 1)
    slot_in, dispatch, combine, near = slots_call(table, tokens)
    slot_go = jnp.einsum(
        "bsm,bmd->bsd", combine.astype(BF16).reshape(images, own, count), out_grad, preferred_element_type=F32
    )
    rows = jnp.concatenate([slot_in, slot_go.astype(BF16).reshape(half, width)], axis=0)

    z2, z1 = swap(rows, "dp", 8), swap(rows, "dp", 4)
    lb, rb, u3, z1 = together(lb, rb, u3, z1)
    l3, r3 = swap(u3, "dp", 1), swap(u3, "dp", 3)
    pb, qb = swap(rb[0], "dp", 1), swap(lb[1], "dp", 3)
    spread = spread_call(near)
    l3, r3, z2, spread = together(l3, r3, z2, spread)
    p3, q3 = swap(r3[0], "dp", 1), swap(l3[1], "dp", 3)
    z3 = swap(z2, "dp", 4)
    pb, qb, p3, q3, z3 = together(pb, qb, p3, q3, z3)
    rows_in = jnp.concatenate([v[:half] for v in (rows, z1, z2, z3)], axis=0)
    rows_go = jnp.concatenate([v[half:] for v in (rows, z1, z2, z3)], axis=0)

    blocks = [units[0], l0, r0, p0, q0, both, lb, rb, pb, qb, u3, l3, r3, p3, q3]
    halves = ffn(rows_in, rows_go, blocks, half)
    slot_out = reduce_z(*halves[:4])
    slot_in_grad = reduce_z(*halves[4:])
    part, mix = against(slot_out, out_grad, combine, False)
    mix = summed_three(mix, "expert", 1, 2, 3)
    mix = summed_three(mix, "expert", 4, 8, 12)
    (back,) = against(slot_in_grad, tokens, dispatch, True)
    logit_grad = back + (part - combine * jnp.repeat(mix, own, axis=0))
    logit_grad_b = logit_grad.astype(BF16)

    near = jnp.concatenate([slot_in_grad.astype(BF16), logit_grad_b], axis=1)
    far = swap(near, "expert", 2)
    term = jnp.einsum(
        "bsm,bmd->sd", logit_grad_b.reshape(images, own, count), tokens, preferred_element_type=F32
    )
    term = summed(term, "dp", 4)
    term, far = together(term, far)
    pieces = all_x(jnp.stack([near, far]))
    term = summed(term, "dp", 8, 1, 2)
    slot_grad = term.T

    pieces[1] = after(pieces[1], term)
    mine, theirs = tokens_call(spread, pieces, table)
    token_grad = (mine + swap(theirs, "expert", 1)).astype(BF16)
    return (token_grad.reshape(images, -1, width), slot_grad)


def solution(mesh):
    return jax.shard_map(
        per_device,
        mesh=mesh,
        in_specs=(
            P("dp", None, None),
            P("dp", None, None),
            P(None, "expert"),
            P("dp", "expert"),
            P("expert", "dp"),
        ),
        out_specs=(P("dp", "expert", None), P(None, "expert")),
        check_vma=False,
    )
```

```python
import math
import jax
import jax.numpy as jnp
from jax import lax
from jax.experimental import pallas as pl
from jax.experimental.pallas import tpu as pltpu
from jax.sharding import PartitionSpec as P

F32 = jnp.float32
BF16 = jnp.bfloat16
ROOT = math.sqrt(2.0 / math.pi)


def swap(value, axis, k):
    count = lax.axis_size(axis)
    return lax.ppermute(value, axis, [(i, i ^ k) for i in range(count)])


def nt(a, b):
    return lax.dot_general(a, b, (((1,), (1,)), ((), ())), preferred_element_type=F32)


def ffn_kernel(rows_in, rows_go, *refs):
    own, l0, r0, p0, q0, both, lb, rb, pb, qb, last, l3, r3, p3, q3 = refs[:15]
    f0, f3 = (p0, q0), (p3, q3)
    outs, grads, (w1, w2) = refs[15:19], refs[19:23], refs[23:]
    me = lax.axis_index("dp")
    depth = w1.shape[0] // 16

    def place(which, dst):
        for a, sources in (
            (0, (own.at[which], l0.at[which], f0[which], r0.at[which])),
            (3, (last.at[which], l3.at[which], f3[which], r3.at[which])),
            (1, (both.at[which, 0], lb.at[which, 0], (pb, qb)[which].at[0], rb.at[which, 0])),
            (2, (both.at[which, 1], lb.at[which, 1], (pb, qb)[which].at[1], rb.at[which, 1])),
        ):
            for b, src in enumerate(sources):
                start = pl.multiple_of((me ^ (4 * a + b)) * depth, 16)
                dst[pl.ds(start, depth), :] = src[...]

    place(0, w1)
    place(1, w2)
    pre = jnp.dot(rows_in[...], w1[...], preferred_element_type=F32)
    sq = pre * pre
    th = jnp.tanh(ROOT * (pre + 0.044715 * (sq * pre)))
    cdf = 0.5 * (1.0 + th)
    hidden = (pre * cdf).astype(BF16)
    slope = cdf + 0.5 * pre * (1.0 - th * th) * (ROOT * (1.0 + 3 * 0.044715 * sq))
    hidden_grad = jnp.dot(rows_go[...], w2[...], preferred_element_type=F32)
    pre_grad = (hidden_grad * slope).astype(BF16)
    rows = outs[0].shape[0]
    for whole, blocks in ((nt(hidden, w2[...]), outs), (nt(pre_grad, w1[...]), grads)):
        for a, block in enumerate(blocks):
            block[...] = whole[a * rows : (a + 1) * rows].astype(block.dtype)


def ffn(rows_in, rows_go, blocks, own_rows):
    rows, width = rows_in.shape
    quarter = blocks[0].shape[2]
    vmem = pl.BlockSpec(memory_space=pltpu.VMEM)
    return pl.pallas_call(
        ffn_kernel,
        out_shape=[jax.ShapeDtypeStruct((own_rows, width), t) for t in (F32, BF16, BF16, BF16)] * 2,
        in_specs=[vmem] * (2 + len(blocks)),
        out_specs=[vmem] * 8,
        scratch_shapes=[pltpu.VMEM((width, quarter), BF16), pltpu.VMEM((width, quarter), BF16)],
        compiler_params=pltpu.CompilerParams(vmem_limit_bytes=40 * 2**20),
        name="ffn",
    )(rows_in, rows_go, *blocks)


def pick_rows(count):
    col = lax.broadcasted_iota(jnp.int32, (32, count), 1)
    row = lax.broadcasted_iota(jnp.int32, (32, count), 0)
    owner = lax.axis_index("expert") ^ (row // 16)
    return (col == owner * 16 + row % 16).astype(BF16)


def slots_kernel(table, tokens, rows, dispatch_own, combine_own, near_out):
    own = 8
    near = table.shape[0] // 2
    ins, disp, comb = [], [], []
    for i in range(2):
        logits = nt(table[...], tokens[i])
        up = jnp.exp(logits[:near] - jnp.max(logits[:near], axis=1, keepdims=True))
        dispatch = up / jnp.sum(up, axis=1, keepdims=True)
        down = jnp.exp(logits - jnp.max(logits, axis=0, keepdims=True))
        combine = down[:own] / jnp.sum(down, axis=0, keepdims=True)
        dispatch_b = dispatch.astype(BF16)
        ins.append(jnp.dot(dispatch_b[:16], tokens[i], preferred_element_type=F32)[:own])
        disp.append(dispatch[:own])
        comb.append(combine)
        near_out[i] = dispatch_b
    rows[...] = jnp.concatenate(ins, axis=0).astype(BF16)
    dispatch_own[...] = jnp.concatenate(disp, axis=0)
    combine_own[...] = jnp.concatenate(comb, axis=0)


def slots_call(table, tokens):
    images, count, width = tokens.shape
    slots = table.shape[0]
    return pl.pallas_call(
        slots_kernel,
        grid=(images // 2,),
        out_shape=[
            jax.ShapeDtypeStruct((images * 8, width), BF16),
            jax.ShapeDtypeStruct((images * 8, count), F32),
            jax.ShapeDtypeStruct((images * 8, count), F32),
            jax.ShapeDtypeStruct((images, slots // 2, count), BF16),
        ],
        in_specs=[
            pl.BlockSpec((slots, width), lambda i: (0, 0)),
            pl.BlockSpec((2, count, width), lambda i: (i, 0, 0)),
        ],
        out_specs=[
            pl.BlockSpec((16, width), lambda i: (i, 0)),
            pl.BlockSpec((16, count), lambda i: (i, 0)),
            pl.BlockSpec((16, count), lambda i: (i, 0)),
            pl.BlockSpec((2, slots // 2, count), lambda i: (i, 0, 0)),
        ],
        compiler_params=pltpu.CompilerParams(vmem_limit_bytes=24 * 2**20),
        cost_estimate=pl.CostEstimate(
            flops=2 * tokens.size * (slots + 16), bytes_accessed=2 * tokens.size, transcendentals=2 * images * slots * count
        ),
        name="slots",
    )(table, tokens)


def spread_kernel(near, out):
    images, slots, count = near.shape
    pick = pick_rows(count)
    q = lax.broadcasted_iota(jnp.int32, (slots, 8 * slots), 0)
    col = lax.broadcasted_iota(jnp.int32, (slots, 8 * slots), 1)
    first = (q // 8) * 64 + q % 8
    for image in range(images):
        lines = nt(pick, near[image]).astype(BF16)
        wide = (col == first + image * 8).astype(BF16)
        lines = jnp.dot(lines, wide, preferred_element_type=F32).astype(BF16)
        out[0, 16 * image : 16 * image + 16] = lines[:16]
        out[1, 16 * image : 16 * image + 16] = lines[16:]


def spread_call(near):
    images, slots, _ = near.shape
    vmem = pl.BlockSpec(memory_space=pltpu.VMEM)
    return pl.pallas_call(
        spread_kernel,
        out_shape=jax.ShapeDtypeStruct((2, images * 16, slots * 8), BF16),
        in_specs=[vmem],
        out_specs=vmem,
        compiler_params=pltpu.CompilerParams(vmem_limit_bytes=16 * 2**20),
        name="spread",
    )(near)


def against_kernel(over_tokens, parts, *refs):
    value = refs[0][...]
    for ref in refs[1:parts]:
        value = value + ref[...].astype(F32)
    big, weight, *outs = refs[parts:]
    high = value.astype(BF16)
    low = (value - high.astype(F32)).astype(BF16)
    both = jnp.concatenate([high, low], axis=0)
    prods = []
    for i in range(2):
        prod = nt(both, big[i])
        prods.append(prod[8 * i : 8 * i + 8] + prod[16 + 8 * i : 24 + 8 * i])
    prod = jnp.concatenate(prods, axis=0)
    w = weight[...]
    part = w * prod
    if over_tokens:
        outs[0][...] = w * (prod - jnp.sum(part, axis=1, keepdims=True))
    else:
        outs[0][...] = part
        step = pl.program_id(0)
        for i in range(2):
            outs[1][pl.ds(2 * step + i, 1), :] = jnp.sum(part[8 * i : 8 * i + 8], axis=0, keepdims=True)


def against(parts, big, weight, over_tokens):
    images, count, width = big.shape
    total = images * 8
    out_shape = [jax.ShapeDtypeStruct((total, count), F32)]
    out_specs = [pl.BlockSpec((16, count), lambda i: (i, 0))]
    if not over_tokens:
        out_shape.append(jax.ShapeDtypeStruct((images, count), F32))
        out_specs.append(pl.BlockSpec((images, count), lambda i: (0, 0)))
    return pl.pallas_call(
        lambda *refs: against_kernel(over_tokens, len(parts), *refs),
        grid=(images // 2,),
        out_shape=out_shape,
        in_specs=[pl.BlockSpec((16, width), lambda i: (i, 0))] * len(parts)
        + [
            pl.BlockSpec((2, count, width), lambda i: (i, 0, 0)),
            pl.BlockSpec((16, count), lambda i: (i, 0)),
        ],
        out_specs=out_specs,
        compiler_params=pltpu.CompilerParams(vmem_limit_bytes=16 * 2**20),
        name="dispatch_grad" if over_tokens else "combine_grad",
    )(*parts, big, weight)


def tokens_kernel(spread, pair, one, two, three, table, mine, theirs):
    half, width = mine.shape
    pieces = [ref[...].reshape(2 * ref.shape[1], ref.shape[2]) for ref in (pair, one, two, three)]
    depth = pieces[0].shape[0]
    count = pieces[0].shape[1] - width
    grads = jnp.concatenate([piece[:, width:] for piece in pieces], axis=0)
    total = grads.shape[0]
    near = total // 8
    c = lax.broadcasted_iota(jnp.int32, (total, near), 0)
    q = lax.broadcasted_iota(jnp.int32, (total, near), 1)
    fold = ((c // 64 == q // 8) & (c % 8 == q % 8)).astype(BF16)
    x = nt(pick_rows(count), grads)
    parts = []
    for side in range(2):
        y = jnp.concatenate([x[16 * side : 16 * side + 16]] * 8, axis=0)
        row = lax.broadcasted_iota(jnp.int32, y.shape, 0)
        col = lax.broadcasted_iota(jnp.int32, y.shape, 1)
        y = jnp.where((col // 8) % 8 == row // 16, y, 0.0).astype(BF16)
        parts.append(jnp.dot(y, fold, preferred_element_type=F32).astype(BF16))
    sums = jnp.dot(jnp.concatenate(parts, axis=0), table[:near], preferred_element_type=F32)
    side = spread[...].reshape(2 * half, spread.shape[2])
    for x, piece in enumerate(pieces):
        sums = sums + jnp.dot(side[:, x * depth : (x + 1) * depth], piece[:, :width], preferred_element_type=F32)
    mine[...] = sums[:half]
    theirs[...] = sums[half:]


def tokens_call(spread, pieces, table):
    vmem = pl.BlockSpec(memory_space=pltpu.VMEM)
    half, width = spread.shape[1], table.shape[1]
    return pl.pallas_call(
        tokens_kernel,
        out_shape=[jax.ShapeDtypeStruct((half, width), F32)] * 2,
        in_specs=[vmem] * 6,
        out_specs=[vmem] * 2,
        compiler_params=pltpu.CompilerParams(vmem_limit_bytes=24 * 2**20),
        name="token_grad",
    )(spread, *pieces, table)


def after(value, *earlier):
    return lax.optimization_barrier((value,) + earlier)[0]


def units_of(w_in, w_out):
    z = lax.axis_index("dp") // 4
    quarter = w_in.shape[1] // 4

    def unit(zz):
        start = zz * quarter
        return jnp.stack(
            [
                lax.dynamic_slice_in_dim(w_in, start, quarter, 1),
                lax.dynamic_slice_in_dim(w_out, start, quarter, 1),
            ]
        )

    return [unit(z ^ a) for a in range(4)]


def together(*values):
    return lax.optimization_barrier(values)


def parts_z(own, *far):
    return [own, *together(*[swap(v, "dp", 4 * a) for a, v in enumerate(far, 1)])]


def all_x(v):
    return [v, *together(swap(v, "expert", 4), swap(v, "expert", 8), swap(v, "expert", 12))]


def doubled(v, axis, *steps):
    for k in steps:
        v = jnp.concatenate([v, swap(v, axis, k)], axis=0)
    return v


def summed(v, axis, *steps):
    for k in steps:
        v = v + swap(v, axis, k)
    return v


def summed_three(v, axis, *steps):
    one, two, three = together(*[swap(v, axis, k) for k in steps])
    return (v + one) + (two + three)


def per_device(tokens, out_grad, slot_params, w_in, w_out):
    images, count, width = tokens.shape
    own = slot_params.shape[1]
    half = images * own

    units = units_of(w_in, w_out.T)
    l0, r0 = swap(units[0], "dp", 1), swap(units[0], "dp", 3)
    u2 = swap(units[2], "dp", 8)
    u1 = swap(units[1], "dp", 4)
    p0, q0 = swap(r0[0], "dp", 1), swap(l0[1], "dp", 3)
    table = doubled(slot_params.T, "expert", 2, 4)

    table, p0, q0, u1, u2 = together(table, p0, q0, u1, u2)
    both = jnp.stack([u1, u2], axis=1)
    lb, rb = swap(both, "dp", 1), swap(both, "dp", 3)
    u3 = swap(after(units[3], u1), "dp", 12)
    table = doubled(table, "expert", 8, 1)
    slot_in, dispatch, combine, near = slots_call(table, tokens)
    slot_go = jnp.einsum(
        "bsm,bmd->bsd", combine.astype(BF16).reshape(images, own, count), out_grad, preferred_element_type=F32
    )
    rows = jnp.concatenate([slot_in, slot_go.astype(BF16).reshape(half, width)], axis=0)

    u3, rows = together(u3, rows)
    z2 = swap(rows, "dp", 8)
    lb, rb, u3 = together(lb, rb, u3)
    z1 = swap(after(rows, lb), "dp", 4)
    l3, r3 = swap(u3, "dp", 1), swap(u3, "dp", 3)
    pb, qb = swap(rb[0], "dp", 1), swap(lb[1], "dp", 3)
    spread = spread_call(near)
    l3, r3, z1, z2, spread = together(l3, r3, z1, z2, spread)
    p3, q3 = swap(r3[0], "dp", 1), swap(l3[1], "dp", 3)
    z3 = swap(z2, "dp", 4)
    pb, qb, p3, q3, z3 = together(pb, qb, p3, q3, z3)
    rows_in = jnp.concatenate([v[:half] for v in (rows, z1, z2, z3)], axis=0)
    rows_go = jnp.concatenate([v[half:] for v in (rows, z1, z2, z3)], axis=0)

    blocks = [units[0], l0, r0, p0, q0, both, lb, rb, pb, qb, u3, l3, r3, p3, q3]
    halves = ffn(rows_in, rows_go, blocks, half)
    outs = parts_z(*halves[:4])
    own_grad, one, two, three = parts_z(*halves[4:])
    slot_in_grad = (own_grad + one.astype(F32)) + (two.astype(F32) + three.astype(F32))
    part, mix = against(outs, out_grad, combine, False)
    mix = summed_three(mix, "expert", 1, 2, 3)
    mix = summed_three(mix, "expert", 4, 8, 12)
    (back,) = against([slot_in_grad], tokens, dispatch, True)
    logit_grad = back + (part - combine * jnp.repeat(mix, own, axis=0))
    logit_grad_b = logit_grad.astype(BF16)

    near = jnp.concatenate([slot_in_grad.astype(BF16), logit_grad_b], axis=1)
    far = swap(near, "expert", 2)
    term = jnp.einsum(
        "bsm,bmd->sd", logit_grad_b.reshape(images, own, count), tokens, preferred_element_type=F32
    )
    term = summed(term, "dp", 4)
    term, far = together(term, far)
    pieces = all_x(jnp.stack([near, far]))
    term = summed(term, "dp", 8, 1)
    last = swap(term, "dp", 2)
    slot_grad = (term + last).T

    pieces[1] = after(pieces[1], last)
    mine, theirs = tokens_call(spread, pieces, table)
    token_grad = (mine + swap(theirs, "expert", 1)).astype(BF16)
    return (token_grad.reshape(images, -1, width), slot_grad)


def solution(mesh):
    return jax.shard_map(
        per_device,
        mesh=mesh,
        in_specs=(
            P("dp", None, None),
            P("dp", None, None),
            P(None, "expert"),
            P("dp", "expert"),
            P("expert", "dp"),
        ),
        out_specs=(P("dp", "expert", None), P(None, "expert")),
        check_vma=False,
    )
```

```python
import math
import jax
import jax.numpy as jnp
from jax import lax
from jax.experimental import pallas as pl
from jax.experimental.pallas import tpu as pltpu
from jax.sharding import PartitionSpec as P

F32 = jnp.float32
BF16 = jnp.bfloat16
ROOT = math.sqrt(2.0 / math.pi)


def swap(value, axis, k):
    count = lax.axis_size(axis)
    return lax.ppermute(value, axis, [(i, i ^ k) for i in range(count)])


def nt(a, b):
    return lax.dot_general(a, b, (((1,), (1,)), ((), ())), preferred_element_type=F32)


def ffn_kernel(rows_in, rows_go, *refs):
    own, l0, r0, p0, q0, both, lb, rb, pb, qb, last, l3, r3, p3, q3 = refs[:15]
    f0, f3 = (p0, q0), (p3, q3)
    outs, grads, (w1, w2) = refs[15:19], refs[19:23], refs[23:]
    me = lax.axis_index("dp")
    depth = w1.shape[0] // 16

    def place(which, dst):
        for a, sources in (
            (0, (own.at[which], l0.at[which], f0[which], r0.at[which])),
            (3, (last.at[which], l3.at[which], f3[which], r3.at[which])),
            (1, (both.at[which, 0], lb.at[which, 0], (pb, qb)[which].at[0], rb.at[which, 0])),
            (2, (both.at[which, 1], lb.at[which, 1], (pb, qb)[which].at[1], rb.at[which, 1])),
        ):
            for b, src in enumerate(sources):
                start = pl.multiple_of((me ^ (4 * a + b)) * depth, 16)
                dst[pl.ds(start, depth), :] = src[...]

    place(0, w1)
    place(1, w2)
    pre = jnp.dot(rows_in[...], w1[...], preferred_element_type=F32)
    sq = pre * pre
    th = jnp.tanh(ROOT * (pre + 0.044715 * (sq * pre)))
    cdf = 0.5 * (1.0 + th)
    hidden = (pre * cdf).astype(BF16)
    slope = cdf + 0.5 * pre * (1.0 - th * th) * (ROOT * (1.0 + 3 * 0.044715 * sq))
    hidden_grad = jnp.dot(rows_go[...], w2[...], preferred_element_type=F32)
    pre_grad = (hidden_grad * slope).astype(BF16)
    rows = outs[0].shape[0]
    for whole, blocks in ((nt(hidden, w2[...]), outs), (nt(pre_grad, w1[...]), grads)):
        for a, block in enumerate(blocks):
            block[...] = whole[a * rows : (a + 1) * rows].astype(block.dtype)


def ffn(rows_in, rows_go, blocks, own_rows):
    rows, width = rows_in.shape
    quarter = blocks[0].shape[2]
    vmem = pl.BlockSpec(memory_space=pltpu.VMEM)
    return pl.pallas_call(
        ffn_kernel,
        out_shape=[jax.ShapeDtypeStruct((own_rows, width), t) for t in (F32, BF16, BF16, BF16)] * 2,
        in_specs=[vmem] * (2 + len(blocks)),
        out_specs=[vmem] * 8,
        scratch_shapes=[pltpu.VMEM((width, quarter), BF16), pltpu.VMEM((width, quarter), BF16)],
        compiler_params=pltpu.CompilerParams(vmem_limit_bytes=40 * 2**20),
        name="ffn",
    )(rows_in, rows_go, *blocks)


def pick_rows(count):
    col = lax.broadcasted_iota(jnp.int32, (32, count), 1)
    row = lax.broadcasted_iota(jnp.int32, (32, count), 0)
    owner = lax.axis_index("expert") ^ (row // 16)
    return (col == owner * 16 + row % 16).astype(BF16)


def slots_kernel(table, tokens, rows, dispatch_own, combine_own, near_out):
    own = 8
    near = table.shape[0] // 2
    ins, disp, comb = [], [], []
    for i in range(2):
        logits = nt(table[...], tokens[i])
        up = jnp.exp(logits[:near] - jnp.max(logits[:near], axis=1, keepdims=True))
        dispatch = up / jnp.sum(up, axis=1, keepdims=True)
        down = jnp.exp(logits - jnp.max(logits, axis=0, keepdims=True))
        combine = down[:own] / jnp.sum(down, axis=0, keepdims=True)
        dispatch_b = dispatch.astype(BF16)
        ins.append(jnp.dot(dispatch_b[:16], tokens[i], preferred_element_type=F32)[:own])
        disp.append(dispatch[:own])
        comb.append(combine)
        near_out[i] = dispatch_b
    rows[...] = jnp.concatenate(ins, axis=0).astype(BF16)
    dispatch_own[...] = jnp.concatenate(disp, axis=0)
    combine_own[...] = jnp.concatenate(comb, axis=0)


def slots_call(table, tokens):
    images, count, width = tokens.shape
    slots = table.shape[0]
    return pl.pallas_call(
        slots_kernel,
        grid=(images // 2,),
        out_shape=[
            jax.ShapeDtypeStruct((images * 8, width), BF16),
            jax.ShapeDtypeStruct((images * 8, count), F32),
            jax.ShapeDtypeStruct((images * 8, count), F32),
            jax.ShapeDtypeStruct((images, slots // 2, count), BF16),
        ],
        in_specs=[
            pl.BlockSpec((slots, width), lambda i: (0, 0)),
            pl.BlockSpec((2, count, width), lambda i: (i, 0, 0)),
        ],
        out_specs=[
            pl.BlockSpec((16, width), lambda i: (i, 0)),
            pl.BlockSpec((16, count), lambda i: (i, 0)),
            pl.BlockSpec((16, count), lambda i: (i, 0)),
            pl.BlockSpec((2, slots // 2, count), lambda i: (i, 0, 0)),
        ],
        compiler_params=pltpu.CompilerParams(vmem_limit_bytes=24 * 2**20),
        cost_estimate=pl.CostEstimate(
            flops=2 * tokens.size * (slots + 16), bytes_accessed=2 * tokens.size, transcendentals=2 * images * slots * count
        ),
        name="slots",
    )(table, tokens)


def spread_kernel(near, out):
    images, slots, count = near.shape
    pick = pick_rows(count)
    q = lax.broadcasted_iota(jnp.int32, (slots, 8 * slots), 0)
    col = lax.broadcasted_iota(jnp.int32, (slots, 8 * slots), 1)
    first = (q // 8) * 64 + q % 8
    for image in range(images):
        lines = nt(pick, near[image]).astype(BF16)
        wide = (col == first + image * 8).astype(BF16)
        lines = jnp.dot(lines, wide, preferred_element_type=F32).astype(BF16)
        out[0, 16 * image : 16 * image + 16] = lines[:16]
        out[1, 16 * image : 16 * image + 16] = lines[16:]


def spread_call(near):
    images, slots, _ = near.shape
    vmem = pl.BlockSpec(memory_space=pltpu.VMEM)
    return pl.pallas_call(
        spread_kernel,
        out_shape=jax.ShapeDtypeStruct((2, images * 16, slots * 8), BF16),
        in_specs=[vmem],
        out_specs=vmem,
        compiler_params=pltpu.CompilerParams(vmem_limit_bytes=16 * 2**20),
        name="spread",
    )(near)


def against_kernel(over_tokens, parts, *refs):
    value = refs[0][...]
    for ref in refs[1:parts]:
        value = value + ref[...].astype(F32)
    big, weight, *outs = refs[parts:]
    high = value.astype(BF16)
    low = (value - high.astype(F32)).astype(BF16)
    both = jnp.concatenate([high, low], axis=0)
    prods = []
    for i in range(2):
        prod = nt(both, big[i])
        prods.append(prod[8 * i : 8 * i + 8] + prod[16 + 8 * i : 24 + 8 * i])
    prod = jnp.concatenate(prods, axis=0)
    w = weight[...]
    part = w * prod
    if over_tokens:
        outs[0][...] = w * (prod - jnp.sum(part, axis=1, keepdims=True))
    else:
        outs[0][...] = part
        step = pl.program_id(0)
        for i in range(2):
            outs[1][pl.ds(2 * step + i, 1), :] = jnp.sum(part[8 * i : 8 * i + 8], axis=0, keepdims=True)


def against(parts, big, weight, over_tokens):
    images, count, width = big.shape
    total = images * 8
    out_shape = [jax.ShapeDtypeStruct((total, count), F32)]
    out_specs = [pl.BlockSpec((16, count), lambda i: (i, 0))]
    if not over_tokens:
        out_shape.append(jax.ShapeDtypeStruct((images, count), F32))
        out_specs.append(pl.BlockSpec((images, count), lambda i: (0, 0)))
    return pl.pallas_call(
        lambda *refs: against_kernel(over_tokens, len(parts), *refs),
        grid=(images // 2,),
        out_shape=out_shape,
        in_specs=[pl.BlockSpec((16, width), lambda i: (i, 0))] * len(parts)
        + [
            pl.BlockSpec((2, count, width), lambda i: (i, 0, 0)),
            pl.BlockSpec((16, count), lambda i: (i, 0)),
        ],
        out_specs=out_specs,
        compiler_params=pltpu.CompilerParams(vmem_limit_bytes=16 * 2**20),
        name="dispatch_grad" if over_tokens else "combine_grad",
    )(*parts, big, weight)


def pack_kernel(back, part, combine, mix, grad, near, send, lines):
    images, count = mix.shape
    width = grad.shape[1]
    own = back.shape[0] // images
    spread = jnp.concatenate([jnp.broadcast_to(mix[i : i + 1], (own, count)) for i in range(images)], axis=0)
    value = (back[...] + (part[...] - combine[...] * spread)).astype(BF16)
    lines[...] = value
    place = (lax.axis_index("expert") // 2) % 2
    col = lax.broadcasted_iota(jnp.int32, (count, count // 2), 1)
    row = lax.broadcasted_iota(jnp.int32, (count, count // 2), 0)
    for out, wanted in ((near, place), (send, 1 - place)):
        pick = (row == (col // 32) * 64 + wanted * 32 + col % 32).astype(BF16)
        out[:, :width] = grad[...].astype(BF16)
        out[:, width:] = jnp.dot(value, pick, preferred_element_type=F32).astype(BF16)


def pack_call(back, part, combine, mix, grad):
    vmem = pl.BlockSpec(memory_space=pltpu.VMEM)
    rows, count = back.shape
    message = jax.ShapeDtypeStruct((rows, grad.shape[1] + count // 2), BF16)
    return pl.pallas_call(
        pack_kernel,
        out_shape=[message, message, jax.ShapeDtypeStruct((rows, count), BF16)],
        in_specs=[vmem] * 5,
        out_specs=[vmem] * 3,
        compiler_params=pltpu.CompilerParams(vmem_limit_bytes=16 * 2**20),
        name="logit_grad",
    )(back, part, combine, mix, grad)


def tokens_kernel(spread, pair, one, two, three, table, mine, theirs):
    half, width = mine.shape
    pieces = [ref[...].reshape(2 * ref.shape[1], ref.shape[2]) for ref in (pair, one, two, three)]
    depth = pieces[0].shape[0]
    count = pieces[0].shape[1] - width
    grads = jnp.concatenate([piece[:, width:] for piece in pieces], axis=0)
    total = grads.shape[0]
    near = total // 8
    c = lax.broadcasted_iota(jnp.int32, (total, near), 0)
    q = lax.broadcasted_iota(jnp.int32, (total, near), 1)
    fold = ((c // 64 == q // 8) & (c % 8 == q % 8)).astype(BF16)
    col = lax.broadcasted_iota(jnp.int32, (32, count), 1)
    row = lax.broadcasted_iota(jnp.int32, (32, count), 0)
    owner = lax.axis_index("expert") ^ (row // 16)
    x = nt((col == (owner // 4) * 32 + (owner % 2) * 16 + row % 16).astype(BF16), grads)
    parts = []
    for side in range(2):
        y = jnp.concatenate([x[16 * side : 16 * side + 16]] * 8, axis=0)
        row = lax.broadcasted_iota(jnp.int32, y.shape, 0)
        col = lax.broadcasted_iota(jnp.int32, y.shape, 1)
        y = jnp.where((col // 8) % 8 == row // 16, y, 0.0).astype(BF16)
        parts.append(jnp.dot(y, fold, preferred_element_type=F32).astype(BF16))
    sums = jnp.dot(jnp.concatenate(parts, axis=0), table[:near], preferred_element_type=F32)
    side = spread[...].reshape(2 * half, spread.shape[2])
    for x, piece in enumerate(pieces):
        sums = sums + jnp.dot(side[:, x * depth : (x + 1) * depth], piece[:, :width], preferred_element_type=F32)
    mine[...] = sums[:half]
    theirs[...] = sums[half:]


def tokens_call(spread, pieces, table):
    vmem = pl.BlockSpec(memory_space=pltpu.VMEM)
    half, width = spread.shape[1], table.shape[1]
    return pl.pallas_call(
        tokens_kernel,
        out_shape=[jax.ShapeDtypeStruct((half, width), F32)] * 2,
        in_specs=[vmem] * 6,
        out_specs=[vmem] * 2,
        compiler_params=pltpu.CompilerParams(vmem_limit_bytes=24 * 2**20),
        name="token_grad",
    )(spread, *pieces, table)


def after(value, *earlier):
    return lax.optimization_barrier((value,) + earlier)[0]


def units_of(w_in, w_out):
    z = lax.axis_index("dp") // 4
    quarter = w_in.shape[1] // 4

    def unit(zz):
        start = zz * quarter
        return jnp.stack(
            [
                lax.dynamic_slice_in_dim(w_in, start, quarter, 1),
                lax.dynamic_slice_in_dim(w_out, start, quarter, 1),
            ]
        )

    return [unit(z ^ a) for a in range(4)]


def together(*values):
    return lax.optimization_barrier(values)


def parts_z(own, *far):
    return [own, *together(*[swap(v, "dp", 4 * a) for a, v in enumerate(far, 1)])]


def all_x(v):
    return [v, *together(swap(v, "expert", 4), swap(v, "expert", 8), swap(v, "expert", 12))]


def doubled(v, axis, *steps):
    for k in steps:
        v = jnp.concatenate([v, swap(v, axis, k)], axis=0)
    return v


def summed(v, axis, *steps):
    for k in steps:
        v = v + swap(v, axis, k)
    return v


def summed_three(v, axis, *steps):
    one, two, three = together(*[swap(v, axis, k) for k in steps])
    return (v + one) + (two + three)


def per_device(tokens, out_grad, slot_params, w_in, w_out):
    images, count, width = tokens.shape
    own = slot_params.shape[1]
    half = images * own

    units = units_of(w_in, w_out.T)
    l0, r0 = swap(units[0], "dp", 1), swap(units[0], "dp", 3)
    u2 = swap(units[2], "dp", 8)
    u1 = swap(units[1], "dp", 4)
    p0, q0 = swap(r0[0], "dp", 1), swap(l0[1], "dp", 3)
    table = doubled(slot_params.T, "expert", 2, 4)

    table, p0, q0, u1, u2 = together(table, p0, q0, u1, u2)
    both = jnp.stack([u1, u2], axis=1)
    lb, rb = swap(both, "dp", 1), swap(both, "dp", 3)
    u3 = swap(after(units[3], u1), "dp", 12)
    table = doubled(table, "expert", 8, 1)
    slot_in, dispatch, combine, near = slots_call(table, tokens)
    slot_go = jnp.einsum(
        "bsm,bmd->bsd", combine.astype(BF16).reshape(images, own, count), out_grad, preferred_element_type=F32
    )
    rows = jnp.concatenate([slot_in, slot_go.astype(BF16).reshape(half, width)], axis=0)

    lb, rb, u3, rows = together(lb, rb, u3, rows)
    z1, z2 = swap(rows, "dp", 4), swap(rows, "dp", 8)
    l3, r3 = swap(u3, "dp", 1), swap(u3, "dp", 3)
    pb, qb = swap(rb[0], "dp", 1), swap(lb[1], "dp", 3)
    l3, r3, z2 = together(l3, r3, z2)
    p3, q3 = swap(r3[0], "dp", 1), swap(l3[1], "dp", 3)
    z3 = swap(z2, "dp", 4)
    spread = spread_call(near)
    pb, qb, p3, q3, z3, spread = together(pb, qb, p3, q3, z3, spread)
    rows_in = jnp.concatenate([v[:half] for v in (rows, z1, z2, z3)], axis=0)
    rows_go = jnp.concatenate([v[half:] for v in (rows, z1, z2, z3)], axis=0)

    blocks = [units[0], l0, r0, p0, q0, both, lb, rb, pb, qb, u3, l3, r3, p3, q3]
    halves = ffn(rows_in, rows_go, blocks, half)
    outs = parts_z(*halves[:4])
    own_grad, one, two, three = parts_z(*halves[4:])
    slot_in_grad = (own_grad + one.astype(F32)) + (two.astype(F32) + three.astype(F32))
    part, mix = against(outs, out_grad, combine, False)
    mix = summed_three(mix, "expert", 1, 2, 3)
    mix = summed_three(mix, "expert", 4, 8, 12)
    (back,) = against([slot_in_grad], tokens, dispatch, True)
    near, send, logit_grad_b = pack_call(back, part, combine, mix, slot_in_grad)
    far = swap(send, "expert", 2)
    term = jnp.einsum(
        "bsm,bmd->sd", logit_grad_b.reshape(images, own, count), tokens, preferred_element_type=F32
    )
    term = summed(term, "dp", 4)
    term, far = together(term, far)
    pieces = all_x(jnp.stack([near, far]))
    term = summed(term, "dp", 8, 1)
    last = swap(term, "dp", 2)
    slot_grad = (term + last).T

    pieces[1] = after(pieces[1], last)
    mine, theirs = tokens_call(spread, pieces, table)
    token_grad = (mine + swap(theirs, "expert", 1)).astype(BF16)
    return (token_grad.reshape(images, -1, width), slot_grad)


def solution(mesh):
    return jax.shard_map(
        per_device,
        mesh=mesh,
        in_specs=(
            P("dp", None, None),
            P("dp", None, None),
            P(None, "expert"),
            P("dp", "expert"),
            P("expert", "dp"),
        ),
        out_specs=(P("dp", "expert", None), P(None, "expert")),
        check_vma=False,
    )
```

```python
import math
import jax
import jax.numpy as jnp
from jax import lax
from jax.experimental import pallas as pl
from jax.experimental.pallas import tpu as pltpu
from jax.sharding import PartitionSpec as P

F32 = jnp.float32
BF16 = jnp.bfloat16
ROOT = math.sqrt(2.0 / math.pi)


def swap(value, axis, k):
    count = lax.axis_size(axis)
    return lax.ppermute(value, axis, [(i, i ^ k) for i in range(count)])


def nt(a, b):
    return lax.dot_general(a, b, (((1,), (1,)), ((), ())), preferred_element_type=F32)


def ffn_kernel(rows_in, rows_go, *refs):
    own, l0, r0, p0, q0, both, lb, rb, pb, qb, last, l3, r3, p3, q3 = refs[:15]
    f0, f3 = (p0, q0), (p3, q3)
    outs, grads, (w1, w2) = refs[15:19], refs[19:23], refs[23:]
    me = lax.axis_index("dp")
    depth = w1.shape[0] // 16

    def place(which, dst):
        for a, sources in (
            (0, (own.at[which], l0.at[which], f0[which], r0.at[which])),
            (3, (last.at[which], l3.at[which], f3[which], r3.at[which])),
            (1, (both.at[which, 0], lb.at[which, 0], (pb, qb)[which].at[0], rb.at[which, 0])),
            (2, (both.at[which, 1], lb.at[which, 1], (pb, qb)[which].at[1], rb.at[which, 1])),
        ):
            for b, src in enumerate(sources):
                start = pl.multiple_of((me ^ (4 * a + b)) * depth, 16)
                dst[pl.ds(start, depth), :] = src[...]

    place(0, w1)
    place(1, w2)
    pre = jnp.dot(rows_in[...], w1[...], preferred_element_type=F32)
    sq = pre * pre
    th = jnp.tanh(ROOT * (pre + 0.044715 * (sq * pre)))
    cdf = 0.5 * (1.0 + th)
    hidden = (pre * cdf).astype(BF16)
    slope = cdf + 0.5 * pre * (1.0 - th * th) * (ROOT * (1.0 + 3 * 0.044715 * sq))
    hidden_grad = jnp.dot(rows_go[...], w2[...], preferred_element_type=F32)
    pre_grad = (hidden_grad * slope).astype(BF16)
    rows = outs[0].shape[0]
    for whole, blocks in ((nt(hidden, w2[...]), outs), (nt(pre_grad, w1[...]), grads)):
        for a, block in enumerate(blocks):
            block[...] = whole[a * rows : (a + 1) * rows].astype(block.dtype)


def ffn(rows_in, rows_go, blocks, own_rows):
    rows, width = rows_in.shape
    quarter = blocks[0].shape[2]
    vmem = pl.BlockSpec(memory_space=pltpu.VMEM)
    return pl.pallas_call(
        ffn_kernel,
        out_shape=[jax.ShapeDtypeStruct((own_rows, width), t) for t in (F32, BF16, BF16, BF16)] * 2,
        in_specs=[vmem] * (2 + len(blocks)),
        out_specs=[vmem] * 8,
        scratch_shapes=[pltpu.VMEM((width, quarter), BF16), pltpu.VMEM((width, quarter), BF16)],
        compiler_params=pltpu.CompilerParams(vmem_limit_bytes=40 * 2**20),
        name="ffn",
    )(rows_in, rows_go, *blocks)


def pick_rows(count):
    col = lax.broadcasted_iota(jnp.int32, (32, count), 1)
    row = lax.broadcasted_iota(jnp.int32, (32, count), 0)
    owner = lax.axis_index("expert") ^ (row // 16)
    return (col == owner * 16 + row % 16).astype(BF16)


def slots_kernel(table, tokens, rows, dispatch_own, combine_own, near_out):
    own = 8
    near = table.shape[0] // 2
    ins, disp, comb = [], [], []
    for i in range(2):
        logits = nt(table[...], tokens[i])
        up = jnp.exp(logits[:near] - jnp.max(logits[:near], axis=1, keepdims=True))
        dispatch = up / jnp.sum(up, axis=1, keepdims=True)
        down = jnp.exp(logits - jnp.max(logits, axis=0, keepdims=True))
        combine = down[:own] / jnp.sum(down, axis=0, keepdims=True)
        dispatch_b = dispatch.astype(BF16)
        ins.append(jnp.dot(dispatch_b[:16], tokens[i], preferred_element_type=F32)[:own])
        disp.append(dispatch[:own])
        comb.append(combine)
        near_out[i] = dispatch_b
    rows[...] = jnp.concatenate(ins, axis=0).astype(BF16)
    dispatch_own[...] = jnp.concatenate(disp, axis=0)
    combine_own[...] = jnp.concatenate(comb, axis=0)


def slots_call(table, tokens):
    images, count, width = tokens.shape
    slots = table.shape[0]
    return pl.pallas_call(
        slots_kernel,
        grid=(images // 2,),
        out_shape=[
            jax.ShapeDtypeStruct((images * 8, width), BF16),
            jax.ShapeDtypeStruct((images * 8, count), F32),
            jax.ShapeDtypeStruct((images * 8, count), F32),
            jax.ShapeDtypeStruct((images, slots // 2, count), BF16),
        ],
        in_specs=[
            pl.BlockSpec((slots, width), lambda i: (0, 0)),
            pl.BlockSpec((2, count, width), lambda i: (i, 0, 0)),
        ],
        out_specs=[
            pl.BlockSpec((16, width), lambda i: (i, 0)),
            pl.BlockSpec((16, count), lambda i: (i, 0)),
            pl.BlockSpec((16, count), lambda i: (i, 0)),
            pl.BlockSpec((2, slots // 2, count), lambda i: (i, 0, 0)),
        ],
        compiler_params=pltpu.CompilerParams(vmem_limit_bytes=24 * 2**20),
        cost_estimate=pl.CostEstimate(
            flops=2 * tokens.size * (slots + 16), bytes_accessed=2 * tokens.size, transcendentals=2 * images * slots * count
        ),
        name="slots",
    )(table, tokens)


def spread_kernel(near, out):
    images, slots, count = near.shape
    pick = pick_rows(count)
    q = lax.broadcasted_iota(jnp.int32, (slots, 8 * slots), 0)
    col = lax.broadcasted_iota(jnp.int32, (slots, 8 * slots), 1)
    first = (q // 8) * 64 + q % 8
    for image in range(images):
        lines = nt(pick, near[image]).astype(BF16)
        wide = (col == first + image * 8).astype(BF16)
        lines = jnp.dot(lines, wide, preferred_element_type=F32).astype(BF16)
        out[0, 16 * image : 16 * image + 16] = lines[:16]
        out[1, 16 * image : 16 * image + 16] = lines[16:]


def spread_call(near):
    images, slots, _ = near.shape
    vmem = pl.BlockSpec(memory_space=pltpu.VMEM)
    return pl.pallas_call(
        spread_kernel,
        out_shape=jax.ShapeDtypeStruct((2, images * 16, slots * 8), BF16),
        in_specs=[vmem],
        out_specs=vmem,
        compiler_params=pltpu.CompilerParams(vmem_limit_bytes=16 * 2**20),
        name="spread",
    )(near)


def against_kernel(over_tokens, parts, *refs):
    value = refs[0][...]
    for ref in refs[1:parts]:
        value = value + ref[...].astype(F32)
    big, weight, *outs = refs[parts:]
    high = value.astype(BF16)
    low = (value - high.astype(F32)).astype(BF16)
    both = jnp.concatenate([high, low], axis=0)
    prods = []
    for i in range(2):
        prod = nt(both, big[i])
        prods.append(prod[8 * i : 8 * i + 8] + prod[16 + 8 * i : 24 + 8 * i])
    prod = jnp.concatenate(prods, axis=0)
    w = weight[...]
    part = w * prod
    if over_tokens:
        outs[0][...] = w * (prod - jnp.sum(part, axis=1, keepdims=True))
    else:
        outs[0][...] = part
        step = pl.program_id(0)
        for i in range(2):
            outs[1][pl.ds(2 * step + i, 1), :] = jnp.sum(part[8 * i : 8 * i + 8], axis=0, keepdims=True)


def against(parts, big, weight, over_tokens):
    images, count, width = big.shape
    total = images * 8
    out_shape = [jax.ShapeDtypeStruct((total, count), F32)]
    out_specs = [pl.BlockSpec((16, count), lambda i: (i, 0))]
    if not over_tokens:
        out_shape.append(jax.ShapeDtypeStruct((images, count), F32))
        out_specs.append(pl.BlockSpec((images, count), lambda i: (0, 0)))
    return pl.pallas_call(
        lambda *refs: against_kernel(over_tokens, len(parts), *refs),
        grid=(images // 2,),
        out_shape=out_shape,
        in_specs=[pl.BlockSpec((16, width), lambda i: (i, 0))] * len(parts)
        + [
            pl.BlockSpec((2, count, width), lambda i: (i, 0, 0)),
            pl.BlockSpec((16, count), lambda i: (i, 0)),
        ],
        out_specs=out_specs,
        compiler_params=pltpu.CompilerParams(vmem_limit_bytes=16 * 2**20),
        name="dispatch_grad" if over_tokens else "combine_grad",
    )(*parts, big, weight)


def pack_kernel(back, part, combine, mix, grad, near, send, lines):
    images, count = mix.shape
    width = grad.shape[1]
    own = back.shape[0] // images
    spread = jnp.concatenate([jnp.broadcast_to(mix[i : i + 1], (own, count)) for i in range(images)], axis=0)
    value = (back[...] + (part[...] - combine[...] * spread)).astype(BF16)
    lines[...] = value
    place = (lax.axis_index("expert") // 2) % 2
    col = lax.broadcasted_iota(jnp.int32, (count, count // 2), 1)
    row = lax.broadcasted_iota(jnp.int32, (count, count // 2), 0)
    for out, wanted in ((near, place), (send, 1 - place)):
        pick = (row == (col // 32) * 64 + wanted * 32 + col % 32).astype(BF16)
        out[:, :width] = grad[...].astype(BF16)
        out[:, width:] = jnp.dot(value, pick, preferred_element_type=F32).astype(BF16)


def pack_call(back, part, combine, mix, grad):
    vmem = pl.BlockSpec(memory_space=pltpu.VMEM)
    rows, count = back.shape
    message = jax.ShapeDtypeStruct((rows, grad.shape[1] + count // 2), BF16)
    return pl.pallas_call(
        pack_kernel,
        out_shape=[message, message, jax.ShapeDtypeStruct((rows, count), BF16)],
        in_specs=[vmem] * 5,
        out_specs=[vmem] * 3,
        compiler_params=pltpu.CompilerParams(vmem_limit_bytes=16 * 2**20),
        name="logit_grad",
    )(back, part, combine, mix, grad)


def tokens_kernel(spread, pair, one, two, three, table, mine, theirs):
    half, width = mine.shape
    pieces = [ref[...].reshape(2 * ref.shape[1], ref.shape[2]) for ref in (pair, one, two, three)]
    depth = pieces[0].shape[0]
    count = pieces[0].shape[1] - width
    grads = jnp.concatenate([piece[:, width:] for piece in pieces], axis=0)
    total = grads.shape[0]
    near = total // 8
    c = lax.broadcasted_iota(jnp.int32, (total, near), 0)
    q = lax.broadcasted_iota(jnp.int32, (total, near), 1)
    fold = ((c // 64 == q // 8) & (c % 8 == q % 8)).astype(BF16)
    col = lax.broadcasted_iota(jnp.int32, (32, count), 1)
    row = lax.broadcasted_iota(jnp.int32, (32, count), 0)
    owner = lax.axis_index("expert") ^ (row // 16)
    x = nt((col == (owner // 4) * 32 + (owner % 2) * 16 + row % 16).astype(BF16), grads)
    parts = []
    for side in range(2):
        y = jnp.concatenate([x[16 * side : 16 * side + 16]] * 8, axis=0)
        row = lax.broadcasted_iota(jnp.int32, y.shape, 0)
        col = lax.broadcasted_iota(jnp.int32, y.shape, 1)
        y = jnp.where((col // 8) % 8 == row // 16, y, 0.0).astype(BF16)
        parts.append(jnp.dot(y, fold, preferred_element_type=F32).astype(BF16))
    sums = jnp.dot(jnp.concatenate(parts, axis=0), table[:near], preferred_element_type=F32)
    side = spread[...].reshape(2 * half, spread.shape[2])
    for x, piece in enumerate(pieces):
        sums = sums + jnp.dot(side[:, x * depth : (x + 1) * depth], piece[:, :width], preferred_element_type=F32)
    mine[...] = sums[:half]
    theirs[...] = sums[half:]


def tokens_call(spread, pieces, table):
    vmem = pl.BlockSpec(memory_space=pltpu.VMEM)
    half, width = spread.shape[1], table.shape[1]
    return pl.pallas_call(
        tokens_kernel,
        out_shape=[jax.ShapeDtypeStruct((half, width), F32)] * 2,
        in_specs=[vmem] * 6,
        out_specs=[vmem] * 2,
        compiler_params=pltpu.CompilerParams(vmem_limit_bytes=24 * 2**20),
        name="token_grad",
    )(spread, *pieces, table)


def after(value, *earlier):
    return lax.optimization_barrier((value,) + earlier)[0]


def units_of(w_in, w_out):
    z = lax.axis_index("dp") // 4
    quarter = w_in.shape[1] // 4

    def unit(zz):
        start = zz * quarter
        return jnp.stack(
            [
                lax.dynamic_slice_in_dim(w_in, start, quarter, 1),
                lax.dynamic_slice_in_dim(w_out, start, quarter, 1),
            ]
        )

    return [unit(z ^ a) for a in range(4)]


def together(*values):
    return lax.optimization_barrier(values)


def parts_z(own, *far):
    return [own, *together(*[swap(v, "dp", 4 * a) for a, v in enumerate(far, 1)])]


def all_x(v):
    return [v, *together(swap(v, "expert", 4), swap(v, "expert", 8), swap(v, "expert", 12))]


def doubled(v, axis, *steps):
    for k in steps:
        v = jnp.concatenate([v, swap(v, axis, k)], axis=0)
    return v


def summed(v, axis, *steps):
    for k in steps:
        v = v + swap(v, axis, k)
    return v


def summed_three(v, axis, *steps):
    one, two, three = together(*[swap(v, axis, k) for k in steps])
    return (v + one) + (two + three)


def per_device(tokens, out_grad, slot_params, w_in, w_out):
    images, count, width = tokens.shape
    own = slot_params.shape[1]
    half = images * own

    units = units_of(w_in, w_out.T)
    l0, r0 = swap(units[0], "dp", 1), swap(units[0], "dp", 3)
    u2 = swap(units[2], "dp", 8)
    u1 = swap(units[1], "dp", 4)
    p0, q0 = swap(r0[0], "dp", 1), swap(l0[1], "dp", 3)
    table = doubled(slot_params.T, "expert", 2, 4)

    table, p0, q0, u1, u2 = together(table, p0, q0, u1, u2)
    both = jnp.stack([u1, u2], axis=1)
    lb, rb = swap(both, "dp", 1), swap(both, "dp", 3)
    u3 = swap(after(units[3], u1), "dp", 12)
    table = doubled(table, "expert", 8, 1)
    slot_in, dispatch, combine, near = slots_call(table, tokens)
    slot_go = jnp.einsum(
        "bsm,bmd->bsd", combine.astype(BF16).reshape(images, own, count), out_grad, preferred_element_type=F32
    )
    rows = jnp.concatenate([slot_in, slot_go.astype(BF16).reshape(half, width)], axis=0)

    lb, rb, u3, rows = together(lb, rb, u3, rows)
    z1, z2 = swap(rows, "dp", 4), swap(rows, "dp", 8)
    l3, r3 = swap(u3, "dp", 1), swap(u3, "dp", 3)
    pb, qb = swap(rb[0], "dp", 1), swap(lb[1], "dp", 3)
    l3, r3, z2 = together(l3, r3, z2)
    p3, q3 = swap(r3[0], "dp", 1), swap(l3[1], "dp", 3)
    z3 = swap(z2, "dp", 4)
    spread = spread_call(near)
    pb, qb, p3, q3, z3, spread = together(pb, qb, p3, q3, z3, spread)
    rows_in = jnp.concatenate([v[:half] for v in (rows, z1, z2, z3)], axis=0)
    rows_go = jnp.concatenate([v[half:] for v in (rows, z1, z2, z3)], axis=0)

    blocks = [units[0], l0, r0, p0, q0, both, lb, rb, pb, qb, u3, l3, r3, p3, q3]
    halves = ffn(rows_in, rows_go, blocks, half)
    outs = parts_z(*halves[:4])
    own_grad, one, two, three = parts_z(*halves[4:])
    slot_in_grad = (own_grad + one.astype(F32)) + (two.astype(F32) + three.astype(F32))
    part, mix = against(outs, out_grad, combine, False)
    mix = summed_three(mix, "expert", 1, 2, 3)
    mix = summed_three(mix, "expert", 4, 8, 12)
    (back,) = against([slot_in_grad], tokens, dispatch, True)
    near, send, logit_grad_b = pack_call(back, part, combine, mix, slot_in_grad)
    far = swap(send, "expert", 2)
    term = jnp.einsum(
        "bsm,bmd->sd", logit_grad_b.reshape(images, own, count), tokens, preferred_element_type=F32
    )
    term, far = together(term, far)
    pieces = all_x(jnp.stack([near, far]))
    term = summed(term, "dp", 4, 8, 1)
    pieces[1] = after(pieces[1], term)
    slot_grad = summed(after(term, *pieces), "dp", 2).T

    mine, theirs = tokens_call(spread, pieces, table)
    token_grad = (mine + swap(theirs, "expert", 1)).astype(BF16)
    return (token_grad.reshape(images, -1, width), slot_grad)


def solution(mesh):
    return jax.shard_map(
        per_device,
        mesh=mesh,
        in_specs=(
            P("dp", None, None),
            P("dp", None, None),
            P(None, "expert"),
            P("dp", "expert"),
            P("expert", "dp"),
        ),
        out_specs=(P("dp", "expert", None), P(None, "expert")),
        check_vma=False,
    )
```

```python
import math
import jax
import jax.numpy as jnp
from jax import lax
from jax.experimental import pallas as pl
from jax.experimental.pallas import tpu as pltpu
from jax.sharding import PartitionSpec as P

F32 = jnp.float32
BF16 = jnp.bfloat16
ROOT = math.sqrt(2.0 / math.pi)


def swap(value, axis, k):
    count = lax.axis_size(axis)
    return lax.ppermute(value, axis, [(i, i ^ k) for i in range(count)])


def nt(a, b):
    return lax.dot_general(a, b, (((1,), (1,)), ((), ())), preferred_element_type=F32)


def ffn_kernel(rows_in, rows_go, *refs):
    own, l0, r0, p0, q0, both, lb, rb, pb, qb, last, l3, r3, p3, q3 = refs[:15]
    f0, f3 = (p0, q0), (p3, q3)
    outs, grads, (w1, w2) = refs[15:19], refs[19:23], refs[23:]
    me = lax.axis_index("dp")
    depth = w1.shape[0] // 16

    def place(which, dst):
        for a, sources in (
            (0, (own.at[which], l0.at[which], f0[which], r0.at[which])),
            (3, (last.at[which], l3.at[which], f3[which], r3.at[which])),
            (1, (both.at[which, 0], lb.at[which, 0], (pb, qb)[which].at[0], rb.at[which, 0])),
            (2, (both.at[which, 1], lb.at[which, 1], (pb, qb)[which].at[1], rb.at[which, 1])),
        ):
            for b, src in enumerate(sources):
                start = pl.multiple_of((me ^ (4 * a + b)) * depth, 16)
                dst[pl.ds(start, depth), :] = src[...]

    place(0, w1)
    place(1, w2)
    pre = jnp.dot(rows_in[...], w1[...], preferred_element_type=F32)
    sq = pre * pre
    th = jnp.tanh(ROOT * (pre + 0.044715 * (sq * pre)))
    cdf = 0.5 * (1.0 + th)
    hidden = (pre * cdf).astype(BF16)
    slope = cdf + 0.5 * pre * (1.0 - th * th) * (ROOT * (1.0 + 3 * 0.044715 * sq))
    hidden_grad = jnp.dot(rows_go[...], w2[...], preferred_element_type=F32)
    pre_grad = (hidden_grad * slope).astype(BF16)
    rows = outs[0].shape[0]
    for whole, blocks in ((nt(hidden, w2[...]), outs), (nt(pre_grad, w1[...]), grads)):
        for a, block in enumerate(blocks):
            block[...] = whole[a * rows : (a + 1) * rows].astype(block.dtype)


def ffn(rows_in, rows_go, blocks, own_rows):
    rows, width = rows_in.shape
    quarter = blocks[0].shape[2]
    vmem = pl.BlockSpec(memory_space=pltpu.VMEM)
    return pl.pallas_call(
        ffn_kernel,
        out_shape=[jax.ShapeDtypeStruct((own_rows, width), t) for t in (F32, BF16, BF16, BF16)] * 2,
        in_specs=[vmem] * (2 + len(blocks)),
        out_specs=[vmem] * 8,
        scratch_shapes=[pltpu.VMEM((width, quarter), BF16), pltpu.VMEM((width, quarter), BF16)],
        compiler_params=pltpu.CompilerParams(vmem_limit_bytes=40 * 2**20),
        name="ffn",
    )(rows_in, rows_go, *blocks)


def pick_rows(count):
    col = lax.broadcasted_iota(jnp.int32, (32, count), 1)
    row = lax.broadcasted_iota(jnp.int32, (32, count), 0)
    owner = lax.axis_index("expert") ^ (row // 16)
    return (col == owner * 16 + row % 16).astype(BF16)


def slots_kernel(table, tokens, rows, dispatch_own, combine_own, near_out):
    own = 8
    near = table.shape[0] // 2
    ins, disp, comb = [], [], []
    for i in range(2):
        logits = nt(table[...], tokens[i])
        up = jnp.exp(logits[:near] - jnp.max(logits[:near], axis=1, keepdims=True))
        dispatch = up / jnp.sum(up, axis=1, keepdims=True)
        down = jnp.exp(logits - jnp.max(logits, axis=0, keepdims=True))
        combine = down[:own] / jnp.sum(down, axis=0, keepdims=True)
        dispatch_b = dispatch.astype(BF16)
        ins.append(jnp.dot(dispatch_b[:16], tokens[i], preferred_element_type=F32)[:own])
        disp.append(dispatch[:own])
        comb.append(combine)
        near_out[i] = dispatch_b
    rows[...] = jnp.concatenate(ins, axis=0).astype(BF16)
    dispatch_own[...] = jnp.concatenate(disp, axis=0)
    combine_own[...] = jnp.concatenate(comb, axis=0)


def slots_call(table, tokens):
    images, count, width = tokens.shape
    slots = table.shape[0]
    return pl.pallas_call(
        slots_kernel,
        grid=(images // 2,),
        out_shape=[
            jax.ShapeDtypeStruct((images * 8, width), BF16),
            jax.ShapeDtypeStruct((images * 8, count), F32),
            jax.ShapeDtypeStruct((images * 8, count), F32),
            jax.ShapeDtypeStruct((images, slots // 2, count), BF16),
        ],
        in_specs=[
            pl.BlockSpec((slots, width), lambda i: (0, 0)),
            pl.BlockSpec((2, count, width), lambda i: (i, 0, 0)),
        ],
        out_specs=[
            pl.BlockSpec((16, width), lambda i: (i, 0)),
            pl.BlockSpec((16, count), lambda i: (i, 0)),
            pl.BlockSpec((16, count), lambda i: (i, 0)),
            pl.BlockSpec((2, slots // 2, count), lambda i: (i, 0, 0)),
        ],
        compiler_params=pltpu.CompilerParams(vmem_limit_bytes=24 * 2**20),
        cost_estimate=pl.CostEstimate(
            flops=2 * tokens.size * (slots + 16), bytes_accessed=2 * tokens.size, transcendentals=2 * images * slots * count
        ),
        name="slots",
    )(table, tokens)


def spread_kernel(near, out):
    images, slots, count = near.shape
    pick = pick_rows(count)
    q = lax.broadcasted_iota(jnp.int32, (slots, 8 * slots), 0)
    col = lax.broadcasted_iota(jnp.int32, (slots, 8 * slots), 1)
    first = (q // 8) * 64 + q % 8
    for image in range(images):
        lines = nt(pick, near[image]).astype(BF16)
        wide = (col == first + image * 8).astype(BF16)
        lines = jnp.dot(lines, wide, preferred_element_type=F32).astype(BF16)
        out[0, 16 * image : 16 * image + 16] = lines[:16]
        out[1, 16 * image : 16 * image + 16] = lines[16:]


def spread_call(near):
    images, slots, _ = near.shape
    vmem = pl.BlockSpec(memory_space=pltpu.VMEM)
    return pl.pallas_call(
        spread_kernel,
        out_shape=jax.ShapeDtypeStruct((2, images * 16, slots * 8), BF16),
        in_specs=[vmem],
        out_specs=vmem,
        compiler_params=pltpu.CompilerParams(vmem_limit_bytes=16 * 2**20),
        name="spread",
    )(near)


def against_kernel(over_tokens, parts, *refs):
    value = refs[0][...]
    for ref in refs[1:parts]:
        value = value + ref[...].astype(F32)
    big, weight, *outs = refs[parts:]
    high = value.astype(BF16)
    low = (value - high.astype(F32)).astype(BF16)
    both = jnp.concatenate([high, low], axis=0)
    prods = []
    for i in range(2):
        prod = nt(both, big[i])
        prods.append(prod[8 * i : 8 * i + 8] + prod[16 + 8 * i : 24 + 8 * i])
    prod = jnp.concatenate(prods, axis=0)
    w = weight[...]
    part = w * prod
    if over_tokens:
        outs[0][...] = w * (prod - jnp.sum(part, axis=1, keepdims=True))
    else:
        outs[0][...] = part
        step = pl.program_id(0)
        for i in range(2):
            outs[1][pl.ds(2 * step + i, 1), :] = jnp.sum(part[8 * i : 8 * i + 8], axis=0, keepdims=True)


def against(parts, big, weight, over_tokens):
    images, count, width = big.shape
    total = images * 8
    out_shape = [jax.ShapeDtypeStruct((total, count), F32)]
    out_specs = [pl.BlockSpec((16, count), lambda i: (i, 0))]
    if not over_tokens:
        out_shape.append(jax.ShapeDtypeStruct((images, count), F32))
        out_specs.append(pl.BlockSpec((images, count), lambda i: (0, 0)))
    return pl.pallas_call(
        lambda *refs: against_kernel(over_tokens, len(parts), *refs),
        grid=(images // 2,),
        out_shape=out_shape,
        in_specs=[pl.BlockSpec((16, width), lambda i: (i, 0))] * len(parts)
        + [
            pl.BlockSpec((2, count, width), lambda i: (i, 0, 0)),
            pl.BlockSpec((16, count), lambda i: (i, 0)),
        ],
        out_specs=out_specs,
        compiler_params=pltpu.CompilerParams(vmem_limit_bytes=16 * 2**20),
        name="dispatch_grad" if over_tokens else "combine_grad",
    )(*parts, big, weight)


def pack_kernel(back, part, combine, mix, grad, near, send, lines):
    images, count = mix.shape
    width = grad.shape[1]
    own = back.shape[0] // images
    spread = jnp.concatenate([jnp.broadcast_to(mix[i : i + 1], (own, count)) for i in range(images)], axis=0)
    value = (back[...] + (part[...] - combine[...] * spread)).astype(BF16)
    lines[...] = value
    place = (lax.axis_index("expert") // 2) % 2
    col = lax.broadcasted_iota(jnp.int32, (count, count // 2), 1)
    row = lax.broadcasted_iota(jnp.int32, (count, count // 2), 0)
    for out, wanted in ((near, place), (send, 1 - place)):
        pick = (row == (col // 32) * 64 + wanted * 32 + col % 32).astype(BF16)
        out[:, :width] = grad[...].astype(BF16)
        out[:, width:] = jnp.dot(value, pick, preferred_element_type=F32).astype(BF16)


def pack_call(back, part, combine, mix, grad):
    vmem = pl.BlockSpec(memory_space=pltpu.VMEM)
    rows, count = back.shape
    message = jax.ShapeDtypeStruct((rows, grad.shape[1] + count // 2), BF16)
    return pl.pallas_call(
        pack_kernel,
        out_shape=[message, message, jax.ShapeDtypeStruct((rows, count), BF16)],
        in_specs=[vmem] * 5,
        out_specs=[vmem] * 3,
        compiler_params=pltpu.CompilerParams(vmem_limit_bytes=16 * 2**20),
        name="logit_grad",
    )(back, part, combine, mix, grad)


def tokens_kernel(spread, table, *refs):
    mine, theirs = refs[8:]
    half, width = mine.shape
    pieces = [jnp.concatenate([near[...], far[...]], axis=0) for near, far in zip(refs[:4], refs[4:8])]
    depth = pieces[0].shape[0]
    count = pieces[0].shape[1] - width
    grads = jnp.concatenate([piece[:, width:] for piece in pieces], axis=0)
    total = grads.shape[0]
    near = total // 8
    c = lax.broadcasted_iota(jnp.int32, (total, near), 0)
    q = lax.broadcasted_iota(jnp.int32, (total, near), 1)
    fold = ((c // 64 == q // 8) & (c % 8 == q % 8)).astype(BF16)
    col = lax.broadcasted_iota(jnp.int32, (32, count), 1)
    row = lax.broadcasted_iota(jnp.int32, (32, count), 0)
    owner = lax.axis_index("expert") ^ (row // 16)
    x = nt((col == (owner // 4) * 32 + (owner % 2) * 16 + row % 16).astype(BF16), grads)
    parts = []
    for side in range(2):
        y = jnp.concatenate([x[16 * side : 16 * side + 16]] * 8, axis=0)
        row = lax.broadcasted_iota(jnp.int32, y.shape, 0)
        col = lax.broadcasted_iota(jnp.int32, y.shape, 1)
        y = jnp.where((col // 8) % 8 == row // 16, y, 0.0).astype(BF16)
        parts.append(jnp.dot(y, fold, preferred_element_type=F32).astype(BF16))
    sums = jnp.dot(jnp.concatenate(parts, axis=0), table[:near], preferred_element_type=F32)
    side = spread[...].reshape(2 * half, spread.shape[2])
    for x, piece in enumerate(pieces):
        sums = sums + jnp.dot(side[:, x * depth : (x + 1) * depth], piece[:, :width], preferred_element_type=F32)
    mine[...] = sums[:half]
    theirs[...] = sums[half:]


def tokens_call(spread, table, pieces):
    vmem = pl.BlockSpec(memory_space=pltpu.VMEM)
    half, width = spread.shape[1], table.shape[1]
    return pl.pallas_call(
        tokens_kernel,
        out_shape=[jax.ShapeDtypeStruct((half, width), F32)] * 2,
        in_specs=[vmem] * 10,
        out_specs=[vmem] * 2,
        compiler_params=pltpu.CompilerParams(vmem_limit_bytes=24 * 2**20),
        name="token_grad",
    )(spread, table, *pieces)


def after(value, *earlier):
    return lax.optimization_barrier((value,) + earlier)[0]


def units_of(w_in, w_out):
    z = lax.axis_index("dp") // 4
    quarter = w_in.shape[1] // 4

    def unit(zz):
        start = zz * quarter
        return jnp.stack(
            [
                lax.dynamic_slice_in_dim(w_in, start, quarter, 1),
                lax.dynamic_slice_in_dim(w_out, start, quarter, 1),
            ]
        )

    return [unit(z ^ a) for a in range(4)]


def together(*values):
    return lax.optimization_barrier(values)


def parts_z(own, *far):
    return [own, *together(*[swap(v, "dp", 4 * a) for a, v in enumerate(far, 1)])]


def all_x(v):
    return [v, *together(swap(v, "expert", 4), swap(v, "expert", 8), swap(v, "expert", 12))]


def doubled(v, axis, *steps):
    for k in steps:
        v = jnp.concatenate([v, swap(v, axis, k)], axis=0)
    return v


def summed(v, axis, *steps):
    for k in steps:
        v = v + swap(v, axis, k)
    return v


def summed_three(v, axis, *steps):
    one, two, three = together(*[swap(v, axis, k) for k in steps])
    return (v + one) + (two + three)


def per_device(tokens, out_grad, slot_params, w_in, w_out):
    images, count, width = tokens.shape
    own = slot_params.shape[1]
    half = images * own

    units = units_of(w_in, w_out.T)
    l0, r0 = swap(units[0], "dp", 1), swap(units[0], "dp", 3)
    u2 = swap(units[2], "dp", 8)
    u1 = swap(units[1], "dp", 4)
    p0, q0 = swap(r0[0], "dp", 1), swap(l0[1], "dp", 3)
    table = doubled(slot_params.T, "expert", 2, 4)

    table, p0, q0, u1, u2 = together(table, p0, q0, u1, u2)
    both = jnp.stack([u1, u2], axis=1)
    lb, rb = swap(both, "dp", 1), swap(both, "dp", 3)
    u3 = swap(after(units[3], u1), "dp", 12)
    table = doubled(table, "expert", 8, 1)
    slot_in, dispatch, combine, near = slots_call(table, tokens)
    slot_go = jnp.einsum(
        "bsm,bmd->bsd", combine.astype(BF16).reshape(images, own, count), out_grad, preferred_element_type=F32
    )
    rows = jnp.concatenate([slot_in, slot_go.astype(BF16).reshape(half, width)], axis=0)

    lb, rb, u3, rows = together(lb, rb, u3, rows)
    z1, z2 = swap(rows, "dp", 4), swap(rows, "dp", 8)
    l3, r3 = swap(u3, "dp", 1), swap(u3, "dp", 3)
    pb, qb = swap(rb[0], "dp", 1), swap(lb[1], "dp", 3)
    l3, r3, z2 = together(l3, r3, z2)
    p3, q3 = swap(r3[0], "dp", 1), swap(l3[1], "dp", 3)
    z3 = swap(z2, "dp", 4)
    spread = spread_call(near)
    pb, qb, p3, q3, z3, spread = together(pb, qb, p3, q3, z3, spread)
    rows_in = jnp.concatenate([v[:half] for v in (rows, z1, z2, z3)], axis=0)
    rows_go = jnp.concatenate([v[half:] for v in (rows, z1, z2, z3)], axis=0)

    blocks = [units[0], l0, r0, p0, q0, both, lb, rb, pb, qb, u3, l3, r3, p3, q3]
    halves = ffn(rows_in, rows_go, blocks, half)
    outs = parts_z(*halves[:4])
    own_grad, one, two, three = parts_z(*halves[4:])
    slot_in_grad = (own_grad + one.astype(F32)) + (two.astype(F32) + three.astype(F32))
    part, mix = against(outs, out_grad, combine, False)
    mix = summed_three(mix, "expert", 1, 2, 3)
    mix = summed_three(mix, "expert", 4, 8, 12)
    (back,) = against([slot_in_grad], tokens, dispatch, True)
    near, send, logit_grad_b = pack_call(back, part, combine, mix, slot_in_grad)
    far = swap(send, "expert", 2)
    nears = all_x(near)
    term = jnp.einsum(
        "bsm,bmd->sd", logit_grad_b.reshape(images, own, count), tokens, preferred_element_type=F32
    )
    term = summed(term, "dp", 4)
    term, far = together(term, far)
    fars = all_x(far)
    *nears, term = together(*nears, term)
    term = summed(term, "dp", 8, 1)
    fars[0] = after(fars[0], term)
    slot_grad = summed(after(term, *fars[1:]), "dp", 2).T

    mine, theirs = tokens_call(spread, table, nears + fars)
    token_grad = (mine + swap(theirs, "expert", 1)).astype(BF16)
    return (token_grad.reshape(images, -1, width), slot_grad)


def solution(mesh):
    return jax.shard_map(
        per_device,
        mesh=mesh,
        in_specs=(
            P("dp", None, None),
            P("dp", None, None),
            P(None, "expert"),
            P("dp", "expert"),
            P("expert", "dp"),
        ),
        out_specs=(P("dp", "expert", None), P(None, "expert")),
        check_vma=False,
    )
```

```python
import math
import jax
import jax.numpy as jnp
from jax import lax
from jax.experimental import pallas as pl
from jax.experimental.pallas import tpu as pltpu
from jax.sharding import PartitionSpec as P

F32 = jnp.float32
BF16 = jnp.bfloat16
ROOT = math.sqrt(2.0 / math.pi)


def swap(value, axis, k):
    count = lax.axis_size(axis)
    return lax.ppermute(value, axis, [(i, i ^ k) for i in range(count)])


def nt(a, b):
    return lax.dot_general(a, b, (((1,), (1,)), ((), ())), preferred_element_type=F32)


def ffn_kernel(rows_in, rows_go, *refs):
    own, l0, r0, p0, q0, both, lb, rb, pb, qb, last, l3, r3, p3, q3 = refs[:15]
    f0, f3 = (p0, q0), (p3, q3)
    outs, grads, (w1, w2) = refs[15:19], refs[19:23], refs[23:]
    me = lax.axis_index("dp")
    depth = w1.shape[0] // 16

    def place(which, dst):
        for a, sources in (
            (0, (own.at[which], l0.at[which], f0[which], r0.at[which])),
            (3, (last.at[which], l3.at[which], f3[which], r3.at[which])),
            (1, (both.at[which, 0], lb.at[which, 0], (pb, qb)[which].at[0], rb.at[which, 0])),
            (2, (both.at[which, 1], lb.at[which, 1], (pb, qb)[which].at[1], rb.at[which, 1])),
        ):
            for b, src in enumerate(sources):
                start = pl.multiple_of((me ^ (4 * a + b)) * depth, 16)
                dst[pl.ds(start, depth), :] = src[...]

    place(0, w1)
    place(1, w2)
    pre = jnp.dot(rows_in[...], w1[...], preferred_element_type=F32)
    sq = pre * pre
    th = jnp.tanh(ROOT * (pre + 0.044715 * (sq * pre)))
    cdf = 0.5 * (1.0 + th)
    hidden = (pre * cdf).astype(BF16)
    slope = cdf + 0.5 * pre * (1.0 - th * th) * (ROOT * (1.0 + 3 * 0.044715 * sq))
    hidden_grad = jnp.dot(rows_go[...], w2[...], preferred_element_type=F32)
    pre_grad = (hidden_grad * slope).astype(BF16)
    rows = outs[0].shape[0]
    for whole, blocks in ((nt(hidden, w2[...]), outs), (nt(pre_grad, w1[...]), grads)):
        for a, block in enumerate(blocks):
            block[...] = whole[a * rows : (a + 1) * rows].astype(block.dtype)


def ffn(rows_in, rows_go, blocks, own_rows):
    rows, width = rows_in.shape
    quarter = blocks[0].shape[2]
    vmem = pl.BlockSpec(memory_space=pltpu.VMEM)
    return pl.pallas_call(
        ffn_kernel,
        out_shape=[jax.ShapeDtypeStruct((own_rows, width), t) for t in (F32, BF16, BF16, BF16)] * 2,
        in_specs=[vmem] * (2 + len(blocks)),
        out_specs=[vmem] * 8,
        scratch_shapes=[pltpu.VMEM((width, quarter), BF16), pltpu.VMEM((width, quarter), BF16)],
        compiler_params=pltpu.CompilerParams(vmem_limit_bytes=40 * 2**20),
        name="ffn",
    )(rows_in, rows_go, *blocks)


def pick_rows(count):
    col = lax.broadcasted_iota(jnp.int32, (32, count), 1)
    row = lax.broadcasted_iota(jnp.int32, (32, count), 0)
    owner = lax.axis_index("expert") ^ (row // 16)
    return (col == owner * 16 + row % 16).astype(BF16)


def slots_kernel(table, tokens, rows, dispatch_own, combine_own, near_out):
    own = 8
    near = table.shape[0] // 2
    ins, disp, comb = [], [], []
    for i in range(2):
        logits = nt(table[...], tokens[i])
        up = jnp.exp(logits[:near] - jnp.max(logits[:near], axis=1, keepdims=True))
        dispatch = up / jnp.sum(up, axis=1, keepdims=True)
        down = jnp.exp(logits - jnp.max(logits, axis=0, keepdims=True))
        combine = down[:own] / jnp.sum(down, axis=0, keepdims=True)
        dispatch_b = dispatch.astype(BF16)
        ins.append(jnp.dot(dispatch_b[:16], tokens[i], preferred_element_type=F32)[:own])
        disp.append(dispatch[:own])
        comb.append(combine)
        near_out[i] = dispatch_b
    rows[...] = jnp.concatenate(ins, axis=0).astype(BF16)
    dispatch_own[...] = jnp.concatenate(disp, axis=0)
    combine_own[...] = jnp.concatenate(comb, axis=0)


def slots_call(table, tokens):
    images, count, width = tokens.shape
    slots = table.shape[0]
    return pl.pallas_call(
        slots_kernel,
        grid=(images // 2,),
        out_shape=[
            jax.ShapeDtypeStruct((images * 8, width), BF16),
            jax.ShapeDtypeStruct((images * 8, count), F32),
            jax.ShapeDtypeStruct((images * 8, count), F32),
            jax.ShapeDtypeStruct((images, slots // 2, count), BF16),
        ],
        in_specs=[
            pl.BlockSpec((slots, width), lambda i: (0, 0)),
            pl.BlockSpec((2, count, width), lambda i: (i, 0, 0)),
        ],
        out_specs=[
            pl.BlockSpec((16, width), lambda i: (i, 0)),
            pl.BlockSpec((16, count), lambda i: (i, 0)),
            pl.BlockSpec((16, count), lambda i: (i, 0)),
            pl.BlockSpec((2, slots // 2, count), lambda i: (i, 0, 0)),
        ],
        compiler_params=pltpu.CompilerParams(vmem_limit_bytes=24 * 2**20),
        cost_estimate=pl.CostEstimate(
            flops=2 * tokens.size * (slots + 16), bytes_accessed=2 * tokens.size, transcendentals=2 * images * slots * count
        ),
        name="slots",
    )(table, tokens)


def spread_kernel(near, out):
    images, slots, count = near.shape
    pick = pick_rows(count)
    q = lax.broadcasted_iota(jnp.int32, (slots, 8 * slots), 0)
    col = lax.broadcasted_iota(jnp.int32, (slots, 8 * slots), 1)
    first = (q // 8) * 64 + q % 8
    for image in range(images):
        lines = nt(pick, near[image]).astype(BF16)
        wide = (col == first + image * 8).astype(BF16)
        lines = jnp.dot(lines, wide, preferred_element_type=F32).astype(BF16)
        out[0, 16 * image : 16 * image + 16] = lines[:16]
        out[1, 16 * image : 16 * image + 16] = lines[16:]


def spread_call(near):
    images, slots, _ = near.shape
    vmem = pl.BlockSpec(memory_space=pltpu.VMEM)
    return pl.pallas_call(
        spread_kernel,
        out_shape=jax.ShapeDtypeStruct((2, images * 16, slots * 8), BF16),
        in_specs=[vmem],
        out_specs=vmem,
        compiler_params=pltpu.CompilerParams(vmem_limit_bytes=16 * 2**20),
        name="spread",
    )(near)


def against_kernel(over_tokens, parts, *refs):
    value = refs[0][...]
    for ref in refs[1:parts]:
        value = value + ref[...].astype(F32)
    big, weight, *outs = refs[parts:]
    high = value.astype(BF16)
    low = (value - high.astype(F32)).astype(BF16)
    both = jnp.concatenate([high, low], axis=0)
    prods = []
    for i in range(2):
        prod = nt(both, big[i])
        prods.append(prod[8 * i : 8 * i + 8] + prod[16 + 8 * i : 24 + 8 * i])
    prod = jnp.concatenate(prods, axis=0)
    w = weight[...]
    part = w * prod
    if over_tokens:
        outs[0][...] = w * (prod - jnp.sum(part, axis=1, keepdims=True))
    else:
        outs[0][...] = part
        step = pl.program_id(0)
        for i in range(2):
            outs[1][pl.ds(2 * step + i, 1), :] = jnp.sum(part[8 * i : 8 * i + 8], axis=0, keepdims=True)


def against(parts, big, weight, over_tokens):
    images, count, width = big.shape
    total = images * 8
    out_shape = [jax.ShapeDtypeStruct((total, count), F32)]
    out_specs = [pl.BlockSpec((16, count), lambda i: (i, 0))]
    if not over_tokens:
        out_shape.append(jax.ShapeDtypeStruct((images, count), F32))
        out_specs.append(pl.BlockSpec((images, count), lambda i: (0, 0)))
    return pl.pallas_call(
        lambda *refs: against_kernel(over_tokens, len(parts), *refs),
        grid=(images // 2,),
        out_shape=out_shape,
        in_specs=[pl.BlockSpec((16, width), lambda i: (i, 0))] * len(parts)
        + [
            pl.BlockSpec((2, count, width), lambda i: (i, 0, 0)),
            pl.BlockSpec((16, count), lambda i: (i, 0)),
        ],
        out_specs=out_specs,
        compiler_params=pltpu.CompilerParams(vmem_limit_bytes=16 * 2**20),
        name="dispatch_grad" if over_tokens else "combine_grad",
    )(*parts, big, weight)


def pack_kernel(back, part, combine, mix, grad, near, send, lines):
    images, count = mix.shape
    width = grad.shape[1]
    own = back.shape[0] // images
    spread = jnp.concatenate([jnp.broadcast_to(mix[i : i + 1], (own, count)) for i in range(images)], axis=0)
    value = (back[...] + (part[...] - combine[...] * spread)).astype(BF16)
    lines[...] = value
    place = (lax.axis_index("expert") // 2) % 2
    col = lax.broadcasted_iota(jnp.int32, (count, count // 2), 1)
    row = lax.broadcasted_iota(jnp.int32, (count, count // 2), 0)
    for out, wanted in ((near, place), (send, 1 - place)):
        pick = (row == (col // 32) * 64 + wanted * 32 + col % 32).astype(BF16)
        out[:, :width] = grad[...].astype(BF16)
        out[:, width:] = jnp.dot(value, pick, preferred_element_type=F32).astype(BF16)


def pack_call(back, part, combine, mix, grad):
    vmem = pl.BlockSpec(memory_space=pltpu.VMEM)
    rows, count = back.shape
    message = jax.ShapeDtypeStruct((rows, grad.shape[1] + count // 2), BF16)
    return pl.pallas_call(
        pack_kernel,
        out_shape=[message, message, jax.ShapeDtypeStruct((rows, count), BF16)],
        in_specs=[vmem] * 5,
        out_specs=[vmem] * 3,
        compiler_params=pltpu.CompilerParams(vmem_limit_bytes=16 * 2**20),
        name="logit_grad",
    )(back, part, combine, mix, grad)


def tokens_kernel(spread, pair, one, two, three, table, mine, theirs):
    half, width = mine.shape
    pieces = [ref[...].reshape(2 * ref.shape[1], ref.shape[2]) for ref in (pair, one, two, three)]
    depth = pieces[0].shape[0]
    count = pieces[0].shape[1] - width
    grads = jnp.concatenate([piece[:, width:] for piece in pieces], axis=0)
    total = grads.shape[0]
    near = total // 8
    c = lax.broadcasted_iota(jnp.int32, (total, near), 0)
    q = lax.broadcasted_iota(jnp.int32, (total, near), 1)
    fold = ((c // 64 == q // 8) & (c % 8 == q % 8)).astype(BF16)
    col = lax.broadcasted_iota(jnp.int32, (32, count), 1)
    row = lax.broadcasted_iota(jnp.int32, (32, count), 0)
    owner = lax.axis_index("expert") ^ (row // 16)
    x = nt((col == (owner // 4) * 32 + (owner % 2) * 16 + row % 16).astype(BF16), grads)
    parts = []
    for side in range(2):
        y = jnp.concatenate([x[16 * side : 16 * side + 16]] * 8, axis=0)
        row = lax.broadcasted_iota(jnp.int32, y.shape, 0)
        col = lax.broadcasted_iota(jnp.int32, y.shape, 1)
        y = jnp.where((col // 8) % 8 == row // 16, y, 0.0).astype(BF16)
        parts.append(jnp.dot(y, fold, preferred_element_type=F32).astype(BF16))
    sums = jnp.dot(jnp.concatenate(parts, axis=0), table[:near], preferred_element_type=F32)
    side = spread[...].reshape(2 * half, spread.shape[2])
    for x, piece in enumerate(pieces):
        sums = sums + jnp.dot(side[:, x * depth : (x + 1) * depth], piece[:, :width], preferred_element_type=F32)
    mine[...] = sums[:half]
    theirs[...] = sums[half:]


def tokens_call(spread, pieces, table):
    vmem = pl.BlockSpec(memory_space=pltpu.VMEM)
    half, width = spread.shape[1], table.shape[1]
    return pl.pallas_call(
        tokens_kernel,
        out_shape=[jax.ShapeDtypeStruct((half, width), F32)] * 2,
        in_specs=[vmem] * 6,
        out_specs=[vmem] * 2,
        compiler_params=pltpu.CompilerParams(vmem_limit_bytes=24 * 2**20),
        name="token_grad",
    )(spread, *pieces, table)


def after(value, *earlier):
    return lax.optimization_barrier((value,) + earlier)[0]


def units_of(w_in, w_out):
    z = lax.axis_index("dp") // 4
    quarter = w_in.shape[1] // 4

    def unit(zz):
        start = zz * quarter
        return jnp.stack(
            [
                lax.dynamic_slice_in_dim(w_in, start, quarter, 1),
                lax.dynamic_slice_in_dim(w_out, start, quarter, 1),
            ]
        )

    return [unit(z ^ a) for a in range(4)]


def together(*values):
    return lax.optimization_barrier(values)


def parts_z(own, *far):
    return [own, *together(*[swap(v, "dp", 4 * a) for a, v in enumerate(far, 1)])]


def all_x(v):
    return [v, *together(swap(v, "expert", 4), swap(v, "expert", 8), swap(v, "expert", 12))]


def doubled(v, axis, *steps):
    for k in steps:
        v = jnp.concatenate([v, swap(v, axis, k)], axis=0)
    return v


def summed(v, axis, *steps):
    for k in steps:
        v = v + swap(v, axis, k)
    return v


def summed_three(v, axis, *steps):
    one, two, three = together(*[swap(v, axis, k) for k in steps])
    return (v + one) + (two + three)


def per_device(tokens, out_grad, slot_params, w_in, w_out):
    images, count, width = tokens.shape
    own = slot_params.shape[1]
    half = images * own

    units = units_of(w_in, w_out.T)
    l0, r0 = swap(units[0], "dp", 1), swap(units[0], "dp", 3)
    u2 = swap(units[2], "dp", 8)
    u1 = swap(units[1], "dp", 4)
    p0, q0 = swap(r0[0], "dp", 1), swap(l0[1], "dp", 3)
    table = doubled(slot_params.T, "expert", 2, 4)

    table, p0, q0, u1, u2 = together(table, p0, q0, u1, u2)
    both = jnp.stack([u1, u2], axis=1)
    lb, rb = swap(both, "dp", 1), swap(both, "dp", 3)
    u3 = swap(after(units[3], u1), "dp", 12)
    table = doubled(table, "expert", 8, 1)
    slot_in, dispatch, combine, near = slots_call(table, tokens)
    slot_go = jnp.einsum(
        "bsm,bmd->bsd", combine.astype(BF16).reshape(images, own, count), out_grad, preferred_element_type=F32
    )
    rows = jnp.concatenate([slot_in, slot_go.astype(BF16).reshape(half, width)], axis=0)

    u3, rows = together(u3, rows)
    z2 = swap(rows, "dp", 8)
    lb, rb, u3 = together(lb, rb, u3)
    z1 = swap(after(rows, lb), "dp", 4)
    l3, r3 = swap(u3, "dp", 1), swap(u3, "dp", 3)
    pb, qb = swap(rb[0], "dp", 1), swap(lb[1], "dp", 3)
    spread = spread_call(near)
    l3, r3, z1, z2, spread = together(l3, r3, z1, z2, spread)
    p3, q3 = swap(r3[0], "dp", 1), swap(l3[1], "dp", 3)
    z3 = swap(z2, "dp", 4)
    pb, qb, p3, q3, z3 = together(pb, qb, p3, q3, z3)
    rows_in = jnp.concatenate([v[:half] for v in (rows, z1, z2, z3)], axis=0)
    rows_go = jnp.concatenate([v[half:] for v in (rows, z1, z2, z3)], axis=0)

    blocks = [units[0], l0, r0, p0, q0, both, lb, rb, pb, qb, u3, l3, r3, p3, q3]
    halves = ffn(rows_in, rows_go, blocks, half)
    outs = parts_z(*halves[:4])
    own_grad, one, two, three = parts_z(*halves[4:])
    slot_in_grad = (own_grad + one.astype(F32)) + (two.astype(F32) + three.astype(F32))
    part, mix = against(outs, out_grad, combine, False)
    mix = summed_three(mix, "expert", 1, 2, 3)
    mix = summed_three(mix, "expert", 4, 8, 12)
    (back,) = against([slot_in_grad], tokens, dispatch, True)
    near, send, logit_grad_b = pack_call(back, part, combine, mix, slot_in_grad)
    far = swap(send, "expert", 2)
    term = jnp.einsum(
        "bsm,bmd->sd", logit_grad_b.reshape(images, own, count), tokens, preferred_element_type=F32
    )
    term = summed(term, "dp", 4)
    term, far = together(term, far)
    pieces = all_x(jnp.stack([near, far]))
    term = summed(term, "dp", 8, 1)
    last = swap(term, "dp", 2)
    slot_grad = (term + last).T

    pieces[1] = after(pieces[1], last)
    mine, theirs = tokens_call(spread, pieces, table)
    token_grad = (mine + swap(theirs, "expert", 1)).astype(BF16)
    return (token_grad.reshape(images, -1, width), slot_grad)


def solution(mesh):
    return jax.shard_map(
        per_device,
        mesh=mesh,
        in_specs=(
            P("dp", None, None),
            P("dp", None, None),
            P(None, "expert"),
            P("dp", "expert"),
            P("expert", "dp"),
        ),
        out_specs=(P("dp", "expert", None), P(None, "expert")),
        check_vma=False,
    )
```
